32 devices in a mesh: wide: 16 (over z, y, core), narrow: 2 (over x).
Axes of the slice: x: 2, y: 2, z: 4, core: 2. Of those that a mesh axis runs over, the one named last changes fastest.
Arguments:
- child_pattern: bfloat16 [32, 2, 32, 16384], P('wide', None, None, 'narrow'), may hold values from -4 to 4
- child_parent: int32 [32], replicated, may hold values from -1 to 3, as said below
- child_octant: int32 [32], replicated, may hold values from 0 to 7, as said below
- parent_center: float32 [4, 3], replicated, may hold values from -16 to 16
- stencil_start: int32 [65536], replicated, may hold values from -3 to 16381, as said below
Outputs:
- parent_pattern: float32 [4, 2, 32, 2, 32768], P(None, None, None, 'narrow', 'wide')
- far_field: float32 [2, 32, 2, 32768], P(None, None, 'narrow', 'wide')
The draws below stay inside these ranges and needn't reach their ends.
Inputs may be any that keep to these rules, and one draw needn't show every extreme that they name: `child_parent`: -1 marks an empty slot; every parent is named by one to eight slots, which lie in one aligned run of 8 slots, and slot 8 p of each run is live. `child_octant`: the live slots of one parent have distinct octants. stencil_start[j] is floor(j/4) - 2 or floor(j/4) - 3.
All inputs are finite; a program needn't handle non-finite values.
Results may differ from the reference program's by a relative error of at most 0.0029.
Values may be sent and summed in bfloat16 or wider, within the bound.
No kernel may reach another device: no remote copies, remote signals or barrier semaphores. Data moves between devices by JAX's collectives and lax.ppermute only.
A program may use at most 64 MiB of HBM per device.

```python
import math
import jax
import jax.numpy as jnp
from jax import lax

RHS = 32
K1 = 16384
K2 = 65536
CHILDREN = 32
PARENTS = 4
N_NARROW = 2


def child_tables(key):
    base = jax.random.fold_in(key, 7)
    key_perm, key_keep, key_octant = jax.random.split(base, 3)
    slot = jnp.arange(CHILDREN, dtype=jnp.int32)
    order = jax.random.permutation(key_perm, PARENTS).astype(jnp.int32)
    keep = jax.random.randint(key_keep, (CHILDREN,), 0, 10) < 7
    keep = jnp.logical_or(keep, slot % 8 == 0)
    keep = jnp.logical_and(keep, slot != 7)
    parent = jnp.where(keep, order[slot // 8], -1).astype(jnp.int32)
    group_keys = jax.random.split(key_octant, CHILDREN // 8)
    octant = jax.vmap(lambda single: jax.random.permutation(single, 8))(group_keys).reshape(-1).astype(jnp.int32)
    return (parent, octant)


def draw_child_parent(key, part):
    return child_tables(key)[0]


def draw_child_octant(key, part):
    return child_tables(key)[1]


def draw_stencil_start(key, part):
    sample = jnp.arange(K2, dtype=jnp.int32)
    excess = jax.random.randint(jax.random.fold_in(key, 11), (K2,), 0, 2).astype(jnp.int32)
    excess = excess.at[0].set(1).at[K2 - 1].set(0)
    return (sample // 4 - 2 - excess).astype(jnp.int32)


def steps_of(stream_key, extent, cuts, smallest, largest):
    def one(dim, shards_of):
        draws = jax.random.uniform(jax.random.fold_in(jax.random.fold_in(stream_key, 6), dim), (shards_of,), jnp.float32, smallest / len(cuts), largest / len(cuts))
        return jnp.repeat(jnp.exp(draws), extent[dim] // shards_of).reshape((-1,) + (1,) * (len(extent) - dim - 1))

    loudness = one(*cuts[0])
    for cut in cuts[1:]:
        loudness = loudness * one(*cut)
    return loudness


def scatter_about(key, shape, width, limit, cuts=(), held_as=jnp.bfloat16):
    gain = steps_of(key, shape, cuts, -0.22, 0.18) if cuts else 1.0
    drawn = jax.random.normal(key, shape, jnp.float32) * width * gain
    return jnp.minimum(jnp.maximum(drawn, -limit), limit).astype(held_as)


def setup_inputs(seed: int = 0) -> dict:
    arg_keys = jax.random.split(jax.random.key(seed), 6)
    child_pattern = scatter_about(arg_keys[0], (CHILDREN, 2, RHS, K1), 0.5, 4.0, ((0, 16), (3, 2)))
    child_parent = draw_child_parent(jax.random.fold_in(arg_keys[5], 71), 0)
    child_octant = draw_child_octant(jax.random.fold_in(arg_keys[5], 71), 0)
    parent_center = jnp.clip(jax.random.uniform(arg_keys[3], (PARENTS, 3), jnp.float32, -16.0, 16.0), -16.0, 16.0)
    stencil_start = draw_stencil_start(jax.random.fold_in(arg_keys[5], 71), 0)
    return dict(child_pattern=child_pattern, child_parent=child_parent, child_octant=child_octant, parent_center=parent_center, stencil_start=stencil_start)


def lagrange_taps(starts, first_out):
    sample_count = starts.shape[0]
    sample = first_out + jnp.arange(sample_count, dtype=jnp.int32)
    excess = sample // 4 - 2 - starts
    offset_u = (sample % 4).astype(jnp.float32) * 0.25 + 2.125 + excess.astype(jnp.float32)
    basis = []
    for node in range(6):
        value = jnp.ones_like(offset_u)
        for other in range(6):
            if other != node:
                value = value * (offset_u - other) / (node - other)
        basis.append(value)
    zeros = jnp.zeros_like(offset_u)
    stacked = []
    for offset in range(7):
        lower = basis[offset - 1] if offset >= 1 else zeros
        upper = basis[offset] if offset <= 5 else zeros
        stacked.append(jnp.where(excess == 0, lower, upper))
    return jnp.stack(stacked).reshape(7, sample_count // 4, 4)

def interpolate(window, tap_weights):
    block_len = tap_weights.shape[1]
    total = jnp.zeros(window.shape[:-1] + (block_len, 4), jnp.float32)
    for offset in range(7):
        total = total + window[..., offset:offset + block_len].astype(jnp.float32)[..., None] * tap_weights[offset]
    return total.reshape(window.shape[:-1] + (4 * block_len,)).astype(jnp.bfloat16)

def directions(first_out, sample_count):
    sample = first_out + jnp.arange(sample_count, dtype=jnp.int32)
    cycles = K2 // 256
    azimuth = 2.0 * math.pi * ((sample % 256).astype(jnp.float32) + 0.5) / 256.0
    polar = math.pi * ((sample // 256).astype(jnp.float32) + 0.5) / cycles
    return (jnp.sin(polar) * jnp.cos(azimuth), jnp.sin(polar) * jnp.sin(azimuth), jnp.cos(polar))

def child_phase(octant, dir_x, dir_y, dir_z):
    sign_x = (octant % 2 * 2 - 1).astype(jnp.float32)
    sign_y = (octant // 2 % 2 * 2 - 1).astype(jnp.float32)
    sign_z = (octant // 4 * 2 - 1).astype(jnp.float32)
    return 2.0 * math.pi * 2.0 * (sign_x[:, None] * dir_x + sign_y[:, None] * dir_y + sign_z[:, None] * dir_z)

def rotate(pattern, angle):
    cosine = jnp.cos(angle)
    sine_part = jnp.sin(angle)
    real_part = pattern[:, 0].astype(jnp.float32)
    imag_part = pattern[:, 1].astype(jnp.float32)
    return jnp.stack([cosine[:, None] * real_part - sine_part[:, None] * imag_part, sine_part[:, None] * real_part + cosine[:, None] * imag_part], axis=1)

def reference(child_pattern, child_parent, child_octant, parent_center, stencil_start):
    tap_weights = lagrange_taps(stencil_start, jnp.int32(0))
    dir_x, dir_y, dir_z = directions(jnp.int32(0), K2)
    parents_total = jnp.zeros((PARENTS, 2, RHS, K2), jnp.float32)

    def add_child(carry, item):
        pattern, parent, octant = item
        window = jnp.concatenate([pattern[..., -3:], pattern, pattern[..., :3]], axis=-1)
        spread = interpolate(window, tap_weights)
        angle = child_phase(octant[None], dir_x, dir_y, dir_z)
        shifted = rotate(spread[None], angle)[0]
        live = (parent >= 0).astype(jnp.float32)
        slot = jnp.maximum(parent, 0).astype(jnp.int32)
        current = lax.dynamic_index_in_dim(carry, slot, 0, keepdims=False)
        carry = lax.dynamic_update_index_in_dim(carry, current + live * shifted, slot, 0)
        return (carry, None)
    parents_total, _ = lax.scan(add_child, parents_total, (child_pattern, child_parent, child_octant))
    angle = 2.0 * math.pi * (parent_center[:, 0:1] * dir_x + parent_center[:, 1:2] * dir_y + parent_center[:, 2:3] * dir_z)
    cosine = jnp.cos(angle)
    sine_part = jnp.sin(angle)
    real_sum = jnp.einsum('pj,prj->rj', cosine, parents_total[:, 0], precision=lax.Precision.HIGHEST) - jnp.einsum('pj,prj->rj', sine_part, parents_total[:, 1], precision=lax.Precision.HIGHEST)
    imag_sum = jnp.einsum('pj,prj->rj', sine_part, parents_total[:, 0], precision=lax.Precision.HIGHEST) + jnp.einsum('pj,prj->rj', cosine, parents_total[:, 1], precision=lax.Precision.HIGHEST)
    far_field = jnp.stack([real_sum, imag_sum]) / math.sqrt(PARENTS)
    parent_pattern = parents_total.reshape(PARENTS, 2, RHS, N_NARROW, K2 // N_NARROW)
    return (parent_pattern, far_field.reshape(2, RHS, N_NARROW, K2 // N_NARROW))
```

```python
import functools
import math

import jax
import jax.numpy as jnp
import ml_dtypes
import numpy as np
from jax import lax
from jax.experimental import pallas as pl
from jax.experimental.pallas import tpu as pltpu
from jax.sharding import PartitionSpec as P

K2 = 65536


def with_halo(cells, sides, width):
    for axis, dim in sides:
        count = lax.axis_size(axis)
        head = lax.slice_in_dim(cells, 0, width, axis=dim)
        tail = lax.slice_in_dim(cells, cells.shape[dim] - width, cells.shape[dim], axis=dim)
        cells = jnp.concatenate(
            [
                lax.ppermute(tail, axis, [(i, (i + 1) % count) for i in range(count)]),
                cells,
                lax.ppermute(head, axis, [((i + 1) % count, i) for i in range(count)]),
            ],
            axis=dim,
        )
    return cells


def lagrange_taps(starts, first_out):
    sample_count = starts.shape[0]
    sample = first_out + jnp.arange(sample_count, dtype=jnp.int32)
    excess = sample // 4 - 2 - starts
    offset_u = (sample % 4).astype(jnp.float32) * 0.25 + 2.125 + excess.astype(jnp.float32)
    basis = []
    for node in range(6):
        value = jnp.ones_like(offset_u)
        for other in range(6):
            if other != node:
                value = value * (offset_u - other) / (node - other)
        basis.append(value)
    zeros = jnp.zeros_like(offset_u)
    stacked = []
    for offset in range(7):
        lower = basis[offset - 1] if offset >= 1 else zeros
        upper = basis[offset] if offset <= 5 else zeros
        stacked.append(jnp.where(excess == 0, lower, upper))
    return jnp.stack(stacked).reshape(7, sample_count // 4, 4)


def interpolate(window, tap_weights):
    block_len = tap_weights.shape[1]
    leading = window.shape[:-1]
    flat_rows = window.reshape((-1, window.shape[-1]))
    row_count = flat_rows.shape[0]
    if block_len % 64 == 0 and block_len > 64:
        group = 64
    else:
        group = block_len
    blocks = block_len // group
    taps = tap_weights.reshape(7, blocks, 4 * group)
    if blocks == 1:
        band_rows = flat_rows.shape[1]
        paired = flat_rows[:, None, :]
    else:
        band_rows = 2 * group
        extended = jnp.pad(flat_rows, ((0, 0), (0, (blocks + 1) * group - flat_rows.shape[1])))
        split_rows = extended.reshape(row_count, blocks + 1, group)
        paired = jnp.concatenate([split_rows[:, :-1], split_rows[:, 1:]], axis=2)
    column = jnp.arange(band_rows, dtype=jnp.int32)[None, :, None]
    target = (jnp.arange(4 * group, dtype=jnp.int32) // 4)[None, None, :]
    offsets = jnp.arange(7, dtype=jnp.int32)[:, None, None]
    onehot = (column == target + offsets).astype(jnp.float32)
    band = jnp.einsum("kcj,kbj->bcj", onehot, taps, precision=lax.Precision.HIGHEST)
    total = jnp.einsum(
        "rbc,bcj->rbj", paired.astype(jnp.float32), band, precision=lax.Precision.HIGHEST
    )
    return total.reshape(leading + (4 * block_len,)).astype(jnp.bfloat16)


def directions(first_out, sample_count):
    sample = first_out + jnp.arange(sample_count, dtype=jnp.int32)
    cycles = K2 // 256
    azimuth = 2.0 * math.pi * ((sample % 256).astype(jnp.float32) + 0.5) / 256.0
    polar = math.pi * ((sample // 256).astype(jnp.float32) + 0.5) / cycles
    return (jnp.sin(polar) * jnp.cos(azimuth), jnp.sin(polar) * jnp.sin(azimuth), jnp.cos(polar))


def child_phase(octant, dir_x, dir_y, dir_z):
    sign_x = (octant % 2 * 2 - 1).astype(jnp.float32)
    sign_y = (octant // 2 % 2 * 2 - 1).astype(jnp.float32)
    sign_z = (octant // 4 * 2 - 1).astype(jnp.float32)
    return (
        2.0
        * math.pi
        * 2.0
        * (sign_x[:, None] * dir_x + sign_y[:, None] * dir_y + sign_z[:, None] * dir_z)
    )


def shift_children(pattern, octant, dir_x, dir_y, dir_z):
    angle = child_phase(octant, dir_x, dir_y, dir_z)
    cosine = jnp.cos(angle)[:, None, :]
    sine_part = jnp.sin(angle)[:, None, :]
    real_part = pattern[:, 0].astype(jnp.float32)
    imag_part = pattern[:, 1].astype(jnp.float32)
    return jnp.stack(
        [cosine * real_part - sine_part * imag_part, sine_part * real_part + cosine * imag_part],
        axis=1,
    )


def exchanged(child_pattern, child_parent, child_octant, parent_center, stencil_start):
    n_wide = lax.axis_size("wide")
    box_count, _, sources, block_one = child_pattern.shape
    block_two = 4 * block_one
    piece_len = block_one // n_wide
    narrow_at = lax.axis_index("narrow")
    wide_at = lax.axis_index("wide")
    out_first = narrow_at * block_two + wide_at * (4 * piece_len)
    parent_count = parent_center.shape[0]
    parent_ids = jnp.arange(parent_count, dtype=jnp.int32)
    dir_x, dir_y, dir_z = directions(out_first, 4 * piece_len)
    padded = with_halo(child_pattern, (("narrow", 3),), 3)
    shape_pieces = (box_count, 2, sources, n_wide, piece_len)
    left_rim = padded[..., 0:block_one].reshape(shape_pieces)[..., :3]
    middle = padded[..., 3 : 3 + block_one].reshape(shape_pieces)
    right_rim = padded[..., 6 : 6 + block_one].reshape(shape_pieces)[..., piece_len - 3 :]
    windows = jnp.concatenate([left_rim, middle, right_rim], axis=-1)
    starts = lax.dynamic_slice_in_dim(stencil_start, out_first, 4 * piece_len)
    tap_weights = lagrange_taps(starts, out_first)
    gathered = interpolate(
        lax.all_to_all(windows, "wide", split_axis=3, concat_axis=0, tiled=True)[:, :, :, 0, :],
        tap_weights,
    )
    shifted = shift_children(gathered, child_octant, dir_x, dir_y, dir_z)
    selector = (child_parent[:, None] == parent_ids[None, :]).astype(jnp.float32)
    parents_total = jnp.einsum("bp,bcrj->pcrj", selector, shifted, precision=lax.Precision.HIGHEST)
    center_angle = (
        2.0
        * math.pi
        * (
            parent_center[:, 0:1] * dir_x
            + parent_center[:, 1:2] * dir_y
            + parent_center[:, 2:3] * dir_z
        )
    )
    center_cos = jnp.cos(center_angle)
    center_sin = jnp.sin(center_angle)
    real_sum = jnp.einsum(
        "pj,prj->rj", center_cos, parents_total[:, 0], precision=lax.Precision.HIGHEST
    ) - jnp.einsum("pj,prj->rj", center_sin, parents_total[:, 1], precision=lax.Precision.HIGHEST)
    imag_sum = jnp.einsum(
        "pj,prj->rj", center_sin, parents_total[:, 0], precision=lax.Precision.HIGHEST
    ) + jnp.einsum("pj,prj->rj", center_cos, parents_total[:, 1], precision=lax.Precision.HIGHEST)
    far_field = jnp.stack([real_sum, imag_sum]) / math.sqrt(parent_count)
    parent_pattern = parents_total[:, :, :, None, :]
    return (parent_pattern, far_field[:, :, None, :])


LANES = 128
HALO = 3


def pick_partner(index, step):
    return index ^ step


def stencil_tables(window, columns):
    tables = np.zeros((2, window, columns), np.float32)
    for excess in range(2):
        for column in range(columns):
            offset_u = np.float32((column % 4) * 0.25 + 2.125 + excess)
            first = window // 4 + column // 4 - 2 - excess
            for node in range(6):
                value = np.float32(1.0)
                for other in range(6):
                    if other != node:
                        value = np.float32(
                            value * np.float32(np.float32(offset_u - np.float32(other)) / np.float32(node - other))
                        )
                tables[excess, first + node, column] = value
    high = tables.astype(ml_dtypes.bfloat16)
    low = (tables - high.astype(np.float32)).astype(ml_dtypes.bfloat16)
    return np.concatenate([high, low], axis=1)


def pack_kernel(groups, members, piece, cells, *outs):
    boxes, parts, sources, block = cells.shape
    rows = boxes * parts * sources
    tiles = piece // LANES
    wide_at = lax.axis_index("wide")
    group_at, member_at = wide_at // members, wide_at % members
    slot = lax.broadcasted_iota(jnp.int32, (16, LANES), 0)
    lane = lax.broadcasted_iota(jnp.int32, (16, LANES), 1)
    pick_left = jnp.where((slot < HALO) & (lane == LANES - HALO + slot), 1.0, 0.0).astype(jnp.bfloat16)
    pick_right = jnp.where((slot >= HALO) & (slot < 2 * HALO) & (lane == slot - HALO), 1.0, 0.0).astype(jnp.bfloat16)
    across = (((1,), (1,)), ((), ()))

    def tile(at):
        return cells[:, :, :, pl.ds(pl.multiple_of(at, LANES), LANES)].reshape(rows, LANES)

    for step in range(groups):
        for swap in range(members):
            out = outs[step * members + swap]
            first = (pick_partner(group_at, step) * members + pick_partner(member_at, swap)) * piece
            for index in range(tiles):
                out[index * rows : (index + 1) * rows, :] = tile(first + index * LANES)
            before = tile(jnp.maximum(first - LANES, 0))
            after = tile(jnp.minimum(first + piece, block - LANES))
            rim = lax.dot_general(pick_left, before, across, preferred_element_type=jnp.float32)
            rim = rim + lax.dot_general(pick_right, after, across, preferred_element_type=jnp.float32)
            out[tiles * rows : tiles * rows + 16, :] = rim.astype(jnp.bfloat16)
    edge = outs[groups * members]
    rim = lax.dot_general(pick_left, tile(block - LANES), across, preferred_element_type=jnp.float32)
    rim = rim + lax.dot_general(pick_right, tile(0), across, preferred_element_type=jnp.float32)
    edge[...] = rim.astype(jnp.bfloat16)


def prep_kernel(groups, members, boxes, piece, parent_of, octant_of, center, starts, cosines, sines, center_cos, center_sin, excess):
    wide_at = lax.axis_index("wide")
    narrow_at = lax.axis_index("narrow")
    group_at, member_at = wide_at // members, wide_at % members
    rows = 4 * piece // LANES
    all_rows = starts.shape[0]
    half_rows = all_rows // lax.axis_size("narrow")
    sample_count = all_rows * LANES
    cycles = sample_count // 256
    row = lax.broadcasted_iota(jnp.int32, (rows, LANES), 0)
    lane = lax.broadcasted_iota(jnp.int32, (rows, LANES), 1)

    def place(group):
        first_row = narrow_at * half_rows + (group * members + member_at) * rows
        sample = (first_row + row) * LANES + lane
        azimuth = 2.0 * math.pi * ((sample & 255).astype(jnp.float32) + 0.5) / 256.0
        polar = math.pi * ((sample >> 8).astype(jnp.float32) + 0.5) / cycles
        sin_polar = jnp.sin(polar)
        return first_row, sample, sin_polar * jnp.cos(azimuth), sin_polar * jnp.sin(azimuth), jnp.cos(polar)

    for step in range(groups):
        first_row, sample, dir_x, dir_y, dir_z = place(pick_partner(group_at, step))
        here = starts[pl.ds(pl.multiple_of(first_row, 8), rows), :]
        excess[step] = ((sample >> 2) - 2 - here).astype(jnp.float32)
        for swap in range(members):
            for box in range(boxes):
                slot = (group_at * members + pick_partner(member_at, swap)) * boxes + box
                octant = octant_of[slot]
                live = jnp.where(parent_of[slot] >= 0, 1.0, 0.0)
                sign_x = ((octant & 1) * 2 - 1).astype(jnp.float32)
                sign_y = (((octant >> 1) & 1) * 2 - 1).astype(jnp.float32)
                sign_z = ((octant >> 2) * 2 - 1).astype(jnp.float32)
                angle = 4.0 * math.pi * (sign_x * dir_x + sign_y * dir_y + sign_z * dir_z)
                cosines[step, swap * boxes + box] = jnp.cos(angle) * live
                sines[step, swap * boxes + box] = jnp.sin(angle) * live
    _, _, dir_x, dir_y, dir_z = place(group_at)
    for parent in range(center.shape[0]):
        turns = center[parent, 0] * dir_x + center[parent, 1] * dir_y + center[parent, 2] * dir_z
        angle = 2.0 * math.pi * turns
        center_cos[parent] = jnp.cos(angle)
        center_sin[parent] = jnp.sin(angle)


def combine_kernel(step, groups, members, boxes, sources, piece, *refs):
    pays, edges = refs[:members], refs[members : 2 * members]
    cosines, sines, excess, band_zero, band_one, out, spread, total = refs[2 * members :]
    rows = boxes * 2 * sources
    tiles = piece // LANES
    wide_at = lax.axis_index("wide")
    last = lax.axis_size("wide") - 1
    group_at, member_at = wide_at // members, wide_at % members
    at = pick_partner(group_at, step) * members + member_at
    slot = lax.broadcasted_iota(jnp.int32, (16, LANES), 0)
    lane = lax.broadcasted_iota(jnp.int32, (16, LANES), 1)
    place = jnp.where(
        ((slot < HALO) & (lane == LANES - HALO + slot)) | ((slot >= HALO) & (slot < 2 * HALO) & (lane == slot - HALO)), 1.0, 0.0
    ).astype(jnp.bfloat16)
    outer = ((slot < HALO) & (at == 0)) | ((slot >= HALO) & (at == last))
    rims = []
    for swap in range(members):
        rim = pays[swap][tiles * rows : tiles * rows + 16, :].astype(jnp.float32)
        rims.append(jnp.where(outer, edges[swap][...].astype(jnp.float32), rim).astype(jnp.bfloat16))
    rim = jnp.concatenate(rims, axis=1)
    rim_tile = lax.dot_general(rim, place, (((0,), (0,)), ((), ())), preferred_element_type=jnp.float32).astype(jnp.bfloat16)

    def tile(index):
        if index < 0 or index >= tiles:
            return rim_tile
        return jnp.concatenate([pays[swap][index * rows : (index + 1) * rows, :] for swap in range(members)], axis=0)

    for group in range(-1, tiles):
        first = max(0, 4 * group + 2)
        end = min(4 * tiles, 4 * group + 6)
        left, right = tile(group), tile(group + 1)
        window = jnp.concatenate([left, right, left, right], axis=1)
        bands = []
        for column in range(first, end):
            at_column = (column + 2) % 4 * LANES
            which = jnp.broadcast_to(excess[column : column + 1, :], (16, LANES)).astype(jnp.bfloat16)
            which = jnp.concatenate([which] * (band_zero.shape[0] // 16), axis=0)
            zero = band_zero[:, at_column : at_column + LANES]
            one = band_one[:, at_column : at_column + LANES]
            bands.append(zero * (1 - which) + one * which)
        band = jnp.concatenate(bands, axis=1)
        spread[:, : (end - first) * LANES] = jnp.dot(window, band, preferred_element_type=jnp.float32)
        for column in range(first, end):
            lanes = slice((column - first) * LANES, (column - first + 1) * LANES)
            real_sum = jnp.zeros((sources, LANES), jnp.float32)
            imag_sum = jnp.zeros((sources, LANES), jnp.float32)
            for child in range(members * boxes):
                start = child * 2 * sources
                real = spread[start : start + sources, lanes].astype(jnp.bfloat16).astype(jnp.float32)
                imag = spread[start + sources : start + 2 * sources, lanes].astype(jnp.bfloat16).astype(jnp.float32)
                cosine = cosines[child, column : column + 1, :]
                sine = sines[child, column : column + 1, :]
                real_sum = real_sum + (cosine * real - sine * imag)
                imag_sum = imag_sum + (sine * real + cosine * imag)
            total[pl.ds(column, sources, stride=4 * tiles), :] = real_sum
            total[pl.ds(sources * 4 * tiles + column, sources, stride=4 * tiles), :] = imag_sum
    out[...] = total[...].astype(out.dtype)


def finish_kernel(groups, members, boxes, sources, rows, parent_of, *refs):
    arrived = refs[:groups]
    center_cos, center_sin, parent_out, far_out = refs[groups:]
    group_at = lax.axis_index("wide") // members
    parents = center_cos.shape[0]
    scale = 1.0 / math.sqrt(parents)
    names = [parent_of[pick_partner(group_at, step) * members * boxes] for step in range(groups)]
    turn_cos = [center_cos[name] * scale for name in names]
    turn_sin = [center_sin[name] * scale for name in names]
    for source in range(sources):
        real_at = slice(source * rows, (source + 1) * rows)
        imag_at = slice((sources + source) * rows, (sources + source + 1) * rows)
        real_sum = jnp.zeros((rows, LANES), jnp.float32)
        imag_sum = jnp.zeros((rows, LANES), jnp.float32)
        for step in range(groups):
            real = arrived[step][real_at, :].astype(jnp.float32)
            imag = arrived[step][imag_at, :].astype(jnp.float32)
            parent_out[names[step], real_at, :] = real
            parent_out[names[step], imag_at, :] = imag
            real_sum = real_sum + (turn_cos[step] * real - turn_sin[step] * imag)
            imag_sum = imag_sum + (turn_sin[step] * real + turn_cos[step] * imag)
        far_out[real_at, :] = real_sum
        far_out[imag_at, :] = imag_sum


def grouped(child_pattern, child_parent, child_octant, parent_center, stencil_start, members):
    n_wide, n_narrow = lax.axis_size("wide"), lax.axis_size("narrow")
    boxes, _, sources, block = child_pattern.shape
    groups = n_wide // members
    piece = block // n_wide
    tiles = piece // LANES
    rows = boxes * 2 * sources
    out_rows = 4 * tiles
    parents = parent_center.shape[0]
    vmem = pl.BlockSpec(memory_space=pltpu.VMEM)
    smem = pl.BlockSpec(memory_space=pltpu.SMEM)
    limit = pltpu.CompilerParams(vmem_limit_bytes=32 * 1024 * 1024)
    packed = pl.pallas_call(
        functools.partial(pack_kernel, groups, members, piece),
        out_shape=[jax.ShapeDtypeStruct((tiles * rows + 16, LANES), jnp.bfloat16)] * (groups * members)
        + [jax.ShapeDtypeStruct((16, LANES), jnp.bfloat16)],
        in_specs=[vmem],
        out_specs=[vmem] * (groups * members + 1),
        compiler_params=limit,
        name="pack",
    )(child_pattern)
    edge = packed[-1]
    order = list(range(groups - 1, -1, -1))

    def swap_with(array, step):
        return lax.ppermute(array, "wide", [(i, i ^ step) for i in range(n_wide)])

    def edge_swap(step):
        pairs = [(i * 2 + n, (i ^ step) * 2 + 1 - n) for i in range(n_wide) for n in range(2)]
        return lax.ppermute(edge, ("wide", "narrow"), pairs)

    edges = [edge_swap(swap) for swap in range(members)]
    tables = pl.pallas_call(
        functools.partial(prep_kernel, groups, members, boxes, piece),
        out_shape=[
            jax.ShapeDtypeStruct((groups, members * boxes, out_rows, LANES), jnp.float32),
            jax.ShapeDtypeStruct((groups, members * boxes, out_rows, LANES), jnp.float32),
            jax.ShapeDtypeStruct((parents, out_rows, LANES), jnp.float32),
            jax.ShapeDtypeStruct((parents, out_rows, LANES), jnp.float32),
            jax.ShapeDtypeStruct((groups, out_rows, LANES), jnp.float32),
        ],
        in_specs=[smem, smem, smem, vmem],
        out_specs=[vmem] * 5,
        compiler_params=limit,
        name="prep",
    )(child_parent, child_octant, parent_center, stencil_start.reshape(-1, LANES))
    cosines, sines, center_cos, center_sin, excess = tables
    bands = stencil_tables(2 * LANES, 4 * LANES)
    arrived = [None] * groups
    for step in order:
        pays = [packed[step * members]]
        pays += [swap_with(packed[step * members + swap], swap) for swap in range(1, members)]
        total = pl.pallas_call(
            functools.partial(combine_kernel, step, groups, members, boxes, sources, piece),
            out_shape=jax.ShapeDtypeStruct((2 * sources * out_rows, LANES), jnp.bfloat16 if step else jnp.float32),
            grid=(1,),
            in_specs=[pl.BlockSpec(pay.shape, lambda i: (0, 0)) for pay in pays + edges]
            + [pl.BlockSpec((None, members * boxes, out_rows, LANES), lambda i, step=step: (step, 0, 0, 0))] * 2
            + [pl.BlockSpec((None, out_rows, LANES), lambda i, step=step: (step, 0, 0))]
            + [pl.BlockSpec(bands.shape[1:], lambda i: (0, 0))] * 2,
            out_specs=pl.BlockSpec((2 * sources * out_rows, LANES), lambda i: (0, 0)),
            scratch_shapes=[
                pltpu.VMEM((members * rows, 4 * LANES), jnp.float32),
                pltpu.VMEM((2 * sources * out_rows, LANES), jnp.float32),
            ],
            compiler_params=limit,
            name="combine",
        )(*pays, *edges, cosines, sines, excess, bands[0], bands[1])
        arrived[step] = swap_with(total, step * members) if step else total
    parent_pattern, far_field = pl.pallas_call(
        functools.partial(finish_kernel, groups, members, boxes, sources, out_rows),
        out_shape=[
            jax.ShapeDtypeStruct((parents, 2 * sources * out_rows, LANES), jnp.float32),
            jax.ShapeDtypeStruct((2 * sources * out_rows, LANES), jnp.float32),
        ],
        in_specs=[smem] + [vmem] * (groups + 2),
        out_specs=[vmem] * 2,
        compiler_params=limit,
        name="finish",
    )(child_parent, *arrived, center_cos, center_sin)
    return (
        parent_pattern.reshape(parents, 2, sources, 1, 4 * piece),
        far_field.reshape(2, sources, 1, 4 * piece),
    )


def power_of_two(number):
    return number > 0 and number & (number - 1) == 0


def per_device(child_pattern, child_parent, child_octant, parent_center, stencil_start):
    n_wide, n_narrow = lax.axis_size("wide"), lax.axis_size("narrow")
    boxes, _, sources, block = child_pattern.shape
    run = child_parent.shape[0] // parent_center.shape[0]
    if run % boxes == 0 and block % n_wide == 0:
        members = run // boxes
        fits = (
            n_narrow == 2
            and n_wide == members * parent_center.shape[0]
            and power_of_two(members)
            and power_of_two(n_wide)
            and block // n_wide % LANES == 0
            and sources % 16 == 0
            and stencil_start.shape[0] == 4 * block * n_narrow
        )
        if fits:
            return grouped(child_pattern, child_parent, child_octant, parent_center, stencil_start, members)
    return exchanged(child_pattern, child_parent, child_octant, parent_center, stencil_start)


def solution(mesh):
    in_specs = (P("wide", None, None, "narrow"), P(), P(), P(), P())
    out_specs = (P(None, None, None, "narrow", "wide"), P(None, None, "narrow", "wide"))
    return jax.shard_map(
        per_device, mesh=mesh, in_specs=in_specs, out_specs=out_specs, check_vma=False
    )
```

```python
import functools
import math

import jax
import jax.numpy as jnp
import ml_dtypes
import numpy as np
from jax import lax
from jax.experimental import pallas as pl
from jax.experimental.pallas import tpu as pltpu
from jax.sharding import PartitionSpec as P

K2 = 65536


def with_halo(cells, sides, width):
    for axis, dim in sides:
        count = lax.axis_size(axis)
        head = lax.slice_in_dim(cells, 0, width, axis=dim)
        tail = lax.slice_in_dim(cells, cells.shape[dim] - width, cells.shape[dim], axis=dim)
        cells = jnp.concatenate(
            [
                lax.ppermute(tail, axis, [(i, (i + 1) % count) for i in range(count)]),
                cells,
                lax.ppermute(head, axis, [((i + 1) % count, i) for i in range(count)]),
            ],
            axis=dim,
        )
    return cells


def lagrange_taps(starts, first_out):
    sample_count = starts.shape[0]
    sample = first_out + jnp.arange(sample_count, dtype=jnp.int32)
    excess = sample // 4 - 2 - starts
    offset_u = (sample % 4).astype(jnp.float32) * 0.25 + 2.125 + excess.astype(jnp.float32)
    basis = []
    for node in range(6):
        value = jnp.ones_like(offset_u)
        for other in range(6):
            if other != node:
                value = value * (offset_u - other) / (node - other)
        basis.append(value)
    zeros = jnp.zeros_like(offset_u)
    stacked = []
    for offset in range(7):
        lower = basis[offset - 1] if offset >= 1 else zeros
        upper = basis[offset] if offset <= 5 else zeros
        stacked.append(jnp.where(excess == 0, lower, upper))
    return jnp.stack(stacked).reshape(7, sample_count // 4, 4)


def interpolate(window, tap_weights):
    block_len = tap_weights.shape[1]
    leading = window.shape[:-1]
    flat_rows = window.reshape((-1, window.shape[-1]))
    row_count = flat_rows.shape[0]
    if block_len % 64 == 0 and block_len > 64:
        group = 64
    else:
        group = block_len
    blocks = block_len // group
    taps = tap_weights.reshape(7, blocks, 4 * group)
    if blocks == 1:
        band_rows = flat_rows.shape[1]
        paired = flat_rows[:, None, :]
    else:
        band_rows = 2 * group
        extended = jnp.pad(flat_rows, ((0, 0), (0, (blocks + 1) * group - flat_rows.shape[1])))
        split_rows = extended.reshape(row_count, blocks + 1, group)
        paired = jnp.concatenate([split_rows[:, :-1], split_rows[:, 1:]], axis=2)
    column = jnp.arange(band_rows, dtype=jnp.int32)[None, :, None]
    target = (jnp.arange(4 * group, dtype=jnp.int32) // 4)[None, None, :]
    offsets = jnp.arange(7, dtype=jnp.int32)[:, None, None]
    onehot = (column == target + offsets).astype(jnp.float32)
    band = jnp.einsum("kcj,kbj->bcj", onehot, taps, precision=lax.Precision.HIGHEST)
    total = jnp.einsum(
        "rbc,bcj->rbj", paired.astype(jnp.float32), band, precision=lax.Precision.HIGHEST
    )
    return total.reshape(leading + (4 * block_len,)).astype(jnp.bfloat16)


def directions(first_out, sample_count):
    sample = first_out + jnp.arange(sample_count, dtype=jnp.int32)
    cycles = K2 // 256
    azimuth = 2.0 * math.pi * ((sample % 256).astype(jnp.float32) + 0.5) / 256.0
    polar = math.pi * ((sample // 256).astype(jnp.float32) + 0.5) / cycles
    return (jnp.sin(polar) * jnp.cos(azimuth), jnp.sin(polar) * jnp.sin(azimuth), jnp.cos(polar))


def child_phase(octant, dir_x, dir_y, dir_z):
    sign_x = (octant % 2 * 2 - 1).astype(jnp.float32)
    sign_y = (octant // 2 % 2 * 2 - 1).astype(jnp.float32)
    sign_z = (octant // 4 * 2 - 1).astype(jnp.float32)
    return (
        2.0
        * math.pi
        * 2.0
        * (sign_x[:, None] * dir_x + sign_y[:, None] * dir_y + sign_z[:, None] * dir_z)
    )


def shift_children(pattern, octant, dir_x, dir_y, dir_z):
    angle = child_phase(octant, dir_x, dir_y, dir_z)
    cosine = jnp.cos(angle)[:, None, :]
    sine_part = jnp.sin(angle)[:, None, :]
    real_part = pattern[:, 0].astype(jnp.float32)
    imag_part = pattern[:, 1].astype(jnp.float32)
    return jnp.stack(
        [cosine * real_part - sine_part * imag_part, sine_part * real_part + cosine * imag_part],
        axis=1,
    )


def exchanged(child_pattern, child_parent, child_octant, parent_center, stencil_start):
    n_wide = lax.axis_size("wide")
    box_count, _, sources, block_one = child_pattern.shape
    block_two = 4 * block_one
    piece_len = block_one // n_wide
    narrow_at = lax.axis_index("narrow")
    wide_at = lax.axis_index("wide")
    out_first = narrow_at * block_two + wide_at * (4 * piece_len)
    parent_count = parent_center.shape[0]
    parent_ids = jnp.arange(parent_count, dtype=jnp.int32)
    dir_x, dir_y, dir_z = directions(out_first, 4 * piece_len)
    padded = with_halo(child_pattern, (("narrow", 3),), 3)
    shape_pieces = (box_count, 2, sources, n_wide, piece_len)
    left_rim = padded[..., 0:block_one].reshape(shape_pieces)[..., :3]
    middle = padded[..., 3 : 3 + block_one].reshape(shape_pieces)
    right_rim = padded[..., 6 : 6 + block_one].reshape(shape_pieces)[..., piece_len - 3 :]
    windows = jnp.concatenate([left_rim, middle, right_rim], axis=-1)
    starts = lax.dynamic_slice_in_dim(stencil_start, out_first, 4 * piece_len)
    tap_weights = lagrange_taps(starts, out_first)
    gathered = interpolate(
        lax.all_to_all(windows, "wide", split_axis=3, concat_axis=0, tiled=True)[:, :, :, 0, :],
        tap_weights,
    )
    shifted = shift_children(gathered, child_octant, dir_x, dir_y, dir_z)
    selector = (child_parent[:, None] == parent_ids[None, :]).astype(jnp.float32)
    parents_total = jnp.einsum("bp,bcrj->pcrj", selector, shifted, precision=lax.Precision.HIGHEST)
    center_angle = (
        2.0
        * math.pi
        * (
            parent_center[:, 0:1] * dir_x
            + parent_center[:, 1:2] * dir_y
            + parent_center[:, 2:3] * dir_z
        )
    )
    center_cos = jnp.cos(center_angle)
    center_sin = jnp.sin(center_angle)
    real_sum = jnp.einsum(
        "pj,prj->rj", center_cos, parents_total[:, 0], precision=lax.Precision.HIGHEST
    ) - jnp.einsum("pj,prj->rj", center_sin, parents_total[:, 1], precision=lax.Precision.HIGHEST)
    imag_sum = jnp.einsum(
        "pj,prj->rj", center_sin, parents_total[:, 0], precision=lax.Precision.HIGHEST
    ) + jnp.einsum("pj,prj->rj", center_cos, parents_total[:, 1], precision=lax.Precision.HIGHEST)
    far_field = jnp.stack([real_sum, imag_sum]) / math.sqrt(parent_count)
    parent_pattern = parents_total[:, :, :, None, :]
    return (parent_pattern, far_field[:, :, None, :])


LANES = 128
HALO = 3
RIM = 16


def stencil_tables(window, columns):
    tables = np.zeros((2, window, columns), np.float32)
    for excess in range(2):
        for column in range(columns):
            offset_u = np.float32((column % 4) * 0.25 + 2.125 + excess)
            first = window // 4 + column // 4 - 2 - excess
            for node in range(6):
                value = np.float32(1.0)
                for other in range(6):
                    if other != node:
                        value = np.float32(
                            value * np.float32(np.float32(offset_u - np.float32(other)) / np.float32(node - other))
                        )
                tables[excess, first + node, column] = value
    high = tables.astype(ml_dtypes.bfloat16)
    low = (tables - high.astype(np.float32)).astype(ml_dtypes.bfloat16)
    return np.concatenate([high, low], axis=1)


def rim_masks():
    slot = lax.broadcasted_iota(jnp.int32, (RIM, LANES), 0)
    lane = lax.broadcasted_iota(jnp.int32, (RIM, LANES), 1)
    return slot, lane


def as_mask(condition):
    return jnp.where(condition, 1.0, 0.0).astype(jnp.bfloat16)


def rim_of(before, after, first_slot):
    slot, lane = rim_masks()
    slot = slot - first_slot
    pick_before = as_mask((slot >= 0) & (slot < HALO) & (lane == LANES - HALO + slot))
    pick_after = as_mask((slot >= HALO) & (slot < 2 * HALO) & (lane == slot - HALO))
    across = (((1,), (1,)), ((), ()))
    rim = lax.dot_general(pick_before, before, across, preferred_element_type=jnp.float32)
    return rim + lax.dot_general(pick_after, after, across, preferred_element_type=jnp.float32)


def first_pack_kernel(step, members, piece, cells, *refs):
    far = members - 2
    outs, edge, ends, sems = refs[:far], refs[far], refs[far + 1], refs[far + 2]
    block = cells.shape[3]
    wide_at = lax.axis_index("wide")
    group_at, member_at = wide_at // members, wide_at % members
    copies = []
    for swap in range(far):
        first = ((group_at ^ step) * members + (member_at ^ (swap + 2))) * piece
        at = pl.ds(pl.multiple_of(first, LANES), piece)
        copies.append(pltpu.make_async_copy(cells.at[:, :, :, at], outs[swap], sems.at[swap]))
    for index, at in enumerate((block - LANES, 0)):
        copies.append(
            pltpu.make_async_copy(cells.at[:, :, :, pl.ds(at, LANES)], ends.at[index], sems.at[far + index])
        )
    for copy in copies:
        copy.start()
    for copy in copies[far:]:
        copy.wait()
    rows = ends.shape[1] * ends.shape[2] * ends.shape[3]
    edge[...] = rim_of(ends[0].reshape(rows, LANES), ends[1].reshape(rows, LANES), 2 * HALO).astype(jnp.bfloat16)
    for copy in copies[:far]:
        copy.wait()


def rest_pack_kernel(groups, members, piece, cells, near, edge, near_edge, *outs):
    boxes, parts, sources, block = cells.shape
    rows = boxes * parts * sources
    tiles = piece // LANES
    wide_at = lax.axis_index("wide")
    group_at, member_at = wide_at // members, wide_at % members

    def tile(ref, at):
        return ref[:, :, :, pl.ds(pl.multiple_of(at, LANES), LANES)].reshape(rows, LANES)

    def rim_at(ref, first):
        return rim_of(tile(ref, jnp.maximum(first - LANES, 0)), tile(ref, jnp.minimum(first + piece, block - LANES)), 0)

    for part in range(1, groups):
        for swap in range(2, members, 2):
            out, base = outs[(part - 1) * (members // 2 - 1) + swap // 2 - 1], 0
            target = member_at ^ swap
            first = ((group_at ^ (groups - 1 - part)) * members + target) * piece
            for ref, rim_edge in ((cells, edge), (near, near_edge)):
                for index in range(tiles):
                    out[base : base + rows, :] = tile(ref, first + index * LANES)
                    base += rows
                out[base : base + RIM, :] = rim_at(ref, first).astype(jnp.bfloat16)
                base += RIM
                if part == 1:
                    rim = rim_at(ref, ((group_at ^ (groups - 1)) * members + target) * piece)
                    out[base : base + RIM, :] = (rim + rim_edge[...].astype(jnp.float32)).astype(jnp.bfloat16)
                    base += RIM


def prep_kernel(groups, members, boxes, piece, parent_of, octant_of, center, starts, cosines, sines, center_cos, center_sin, excess):
    wide_at = lax.axis_index("wide")
    narrow_at = lax.axis_index("narrow")
    group_at, member_at = wide_at // members, wide_at % members
    rows = 4 * piece // LANES
    all_rows = starts.shape[0]
    half_rows = all_rows // lax.axis_size("narrow")
    cycles = all_rows * LANES // 256
    row = lax.broadcasted_iota(jnp.int32, (rows, LANES), 0)
    lane = lax.broadcasted_iota(jnp.int32, (rows, LANES), 1)

    def place(group):
        first_row = narrow_at * half_rows + (group * members + member_at) * rows
        sample = (first_row + row) * LANES + lane
        azimuth = 2.0 * math.pi * ((sample & 255).astype(jnp.float32) + 0.5) / 256.0
        polar = math.pi * ((sample >> 8).astype(jnp.float32) + 0.5) / cycles
        sin_polar = jnp.sin(polar)
        return first_row, sample, sin_polar * jnp.cos(azimuth), sin_polar * jnp.sin(azimuth), jnp.cos(polar)

    for step in range(groups):
        first_row, sample, dir_x, dir_y, dir_z = place(group_at ^ step)
        here = starts[pl.ds(pl.multiple_of(first_row, 8), rows), :]
        excess[step] = ((sample >> 2) - 2 - here).astype(jnp.float32)
        for swap in range(members):
            for box in range(boxes):
                slot = (group_at * members + (member_at ^ swap)) * boxes + box
                octant = octant_of[slot]
                live = jnp.where(parent_of[slot] >= 0, 1.0, 0.0)
                sign_x = ((octant & 1) * 2 - 1).astype(jnp.float32)
                sign_y = (((octant >> 1) & 1) * 2 - 1).astype(jnp.float32)
                sign_z = ((octant >> 2) * 2 - 1).astype(jnp.float32)
                angle = 4.0 * math.pi * (sign_x * dir_x + sign_y * dir_y + sign_z * dir_z)
                cosines[step, swap * boxes + box] = jnp.cos(angle) * live
                sines[step, swap * boxes + box] = jnp.sin(angle) * live
    _, _, dir_x, dir_y, dir_z = place(group_at)
    scale = 1.0 / math.sqrt(center.shape[0])
    for parent in range(center.shape[0]):
        turns = center[parent, 0] * dir_x + center[parent, 1] * dir_y + center[parent, 2] * dir_z
        angle = 2.0 * math.pi * turns
        center_cos[parent] = jnp.cos(angle) * scale
        center_sin[parent] = jnp.sin(angle) * scale


def columns_of(windows, tiles):
    return [c for w in windows for c in range(max(0, 4 * w + 2), min(4 * tiles, 4 * w + 6))]


def combine_kernel(jobs, members, boxes, sources, tiles, count, *refs):
    data = refs[:count]
    cosines, sines, excess, band_zero, band_one = refs[count : count + 5]
    outs = refs[count + 5 : count + 5 + len(jobs)]
    spread, total = refs[count + 5 + len(jobs) :]
    for (step, *job), out in zip(jobs, outs):
        combine(
            step, *job, members, boxes, sources, tiles, data, cosines.at[step], sines.at[step], excess.at[step],
            band_zero, band_one, out, spread, total,
        )


def combine(
    step, windows, places, rims, members, boxes, sources, tiles, data, cosines, sines, excess, band_zero, band_one, out, spread, total
):
    rows = boxes * 2 * sources
    block = data[0].shape[3]
    wide_at = lax.axis_index("wide")
    last = lax.axis_size("wide") - 1
    at = ((wide_at // members) ^ step) * members + wide_at % members
    first = at * (tiles * LANES)

    def local(ref, lane):
        return ref[:, :, :, pl.ds(pl.multiple_of(lane, LANES), LANES)].reshape(rows, LANES)

    def tile(index):
        if index < 0 or index >= tiles:
            return rim_tile
        found = [local(data[member], first + index * LANES) for member in range(2)]
        for which, base in places:
            ref = data[which]
            if len(ref.shape) == 4:
                found.append(ref[:, :, :, index * LANES : (index + 1) * LANES].reshape(rows, LANES))
            else:
                found.append(ref[base + index * rows : base + (index + 1) * rows, :])
        return jnp.concatenate(found, axis=0)

    if rims is not None:
        slot, lane = rim_masks()
        from_other = slot >= 2 * HALO
        side = jnp.where(from_other, slot - 2 * HALO, slot)
        outer = ((side < HALO) & (at == 0)) | ((side >= HALO) & (at == last))
        keep = (outer == from_other) & (slot < 4 * HALO)
        place = as_mask(
            ((side < HALO) & (lane == LANES - HALO + side)) | ((side >= HALO) & (side < 2 * HALO) & (lane == side - HALO))
        )
        found = []
        for inner, (other, other_row) in rims:
            outside = data[other][other_row : other_row + RIM, :].astype(jnp.float32)
            if inner is None:
                inside = jnp.zeros((RIM, LANES), jnp.float32)
            else:
                inside = data[inner[0]][inner[1] : inner[1] + RIM, :].astype(jnp.float32)
            found.append(jnp.where(keep, jnp.where(from_other, outside, inside), 0.0).astype(jnp.bfloat16))
        rim = jnp.concatenate(found, axis=1)
        rim_tile = lax.dot_general(rim, place, (((0,), (0,)), ((), ())), preferred_element_type=jnp.float32)
        lane = lax.broadcasted_iota(jnp.int32, (rows, LANES), 1)
        from_before = (lane >= LANES - HALO) & (at != 0)
        from_after = (lane < HALO) & (at != last)
        near = []
        for member in range(2):
            before = local(data[member], jnp.maximum(first - LANES, 0)).astype(jnp.float32)
            after = local(data[member], jnp.minimum(first + tiles * LANES, block - LANES)).astype(jnp.float32)
            near.append(jnp.where(from_before, before, jnp.where(from_after, after, 0.0)))
        near = jnp.concatenate(near, axis=0)
        rim_tile = jnp.concatenate([rim_tile[: 2 * rows] + near, rim_tile[2 * rows :]], axis=0).astype(jnp.bfloat16)

    columns = columns_of(windows, tiles)
    width = len(columns)
    for turn, window in enumerate(windows):
        mine = columns_of([window], tiles)
        left, right = tile(window), tile(window + 1)
        cells = jnp.concatenate([left, right, left, right], axis=1)
        bands = []
        for column in mine:
            at_column = (column + 2) % 4 * LANES
            which = jnp.broadcast_to(excess[column : column + 1, :], (16, LANES)).astype(jnp.bfloat16)
            which = jnp.concatenate([which] * (band_zero.shape[0] // 16), axis=0)
            zero = band_zero[:, at_column : at_column + LANES]
            one = band_one[:, at_column : at_column + LANES]
            bands.append(zero * (1 - which) + one * which)
        band = jnp.concatenate(bands, axis=1)
        buffer = spread.at[turn % 2]
        buffer[:, : len(mine) * LANES] = jnp.dot(cells, band, preferred_element_type=jnp.float32)
        for number, column in enumerate(mine):
            lanes = slice(number * LANES, (number + 1) * LANES)
            real_sum = jnp.zeros((sources, LANES), jnp.float32)
            imag_sum = jnp.zeros((sources, LANES), jnp.float32)
            for child in range(members * boxes):
                start = child * 2 * sources
                real = buffer[start : start + sources, lanes].astype(jnp.bfloat16).astype(jnp.float32)
                imag = buffer[start + sources : start + 2 * sources, lanes].astype(jnp.bfloat16).astype(jnp.float32)
                cosine = cosines[child, column : column + 1, :]
                sine = sines[child, column : column + 1, :]
                real_sum = real_sum + (cosine * real - sine * imag)
                imag_sum = imag_sum + (sine * real + cosine * imag)
            at_row = columns.index(column)
            total[pl.ds(at_row, sources, stride=width), :] = real_sum
            total[pl.ds(sources * width + at_row, sources, stride=width), :] = imag_sum
    out[...] = total[: 2 * sources * width, :].astype(out.dtype)


def spans_of(columns):
    spans, begin = [], 0
    for i in range(1, len(columns) + 1):
        if i == len(columns) or columns[i] != columns[i - 1] + 1:
            spans.append((begin, columns[begin], i - begin))
            begin = i
    return spans


def finish_kernel(last, pieces, members, boxes, sources, rows, parent_of, *refs):
    arrived, refs = refs[: len(pieces)], refs[len(pieces) :]
    if last:
        center_cos, center_sin, far_in, _, parent_out, far_out, held, sems = refs
    else:
        center_cos, center_sin, parent_out, far_out = refs
    group_at = lax.axis_index("wide") // members
    names = [parent_of[(group_at ^ step) * members * boxes] for step, _ in pieces]
    turns = [(center_cos[name], center_sin[name]) for name in names]
    copies = []
    for source in range(sources):
        real_all, imag_all = (pl.ds((part * sources + source) * rows, rows) for part in range(2))
        if last:
            real_sum, imag_sum = far_in[real_all, :], far_in[imag_all, :]
        for piece, (step, columns) in enumerate(pieces):
            width = len(columns)
            for begin, column, length in spans_of(columns):
                real = arrived[piece][pl.ds(source * width + begin, length), :].astype(jnp.float32)
                imag = arrived[piece][pl.ds((sources + source) * width + begin, length), :].astype(jnp.float32)
                cosine, sine = (turn[column : column + length, :] for turn in turns[piece])
                real_at = pl.ds(source * rows + column, length)
                imag_at = pl.ds((sources + source) * rows + column, length)
                real_turned = cosine * real - sine * imag
                imag_turned = sine * real + cosine * imag
                if last:
                    held[piece, real_at, :] = real
                    held[piece, imag_at, :] = imag
                    real_sum = real_sum + real_turned
                    imag_sum = imag_sum + imag_turned
                else:
                    parent_out[names[piece], real_at, :] = real
                    parent_out[names[piece], imag_at, :] = imag
                    if piece == 0:
                        far_out[real_at, :] = real_turned
                        far_out[imag_at, :] = imag_turned
                    else:
                        far_out[real_at, :] += real_turned
                        far_out[imag_at, :] += imag_turned
        if last:
            far_out[real_all, :] = real_sum
            far_out[imag_all, :] = imag_sum
            if source % (sources // 2) == sources // 2 - 1:
                half = source // (sources // 2)
                size = sources // 2 * rows
                for piece in range(len(pieces)):
                    for part in range(2):
                        at = pl.ds(part * sources * rows + half * size, size)
                        copies.append(
                            pltpu.make_async_copy(
                                held.at[piece, at], parent_out.at[names[piece], at], sems.at[(half * len(pieces) + piece) * 2 + part]
                            )
                        )
                        copies[-1].start()
    for copy in copies:
        copy.wait()


def grouped(child_pattern, child_parent, child_octant, parent_center, stencil_start, members):
    n_wide = lax.axis_size("wide")
    boxes, _, sources, block = child_pattern.shape
    groups = n_wide // members
    piece = block // n_wide
    tiles = piece // LANES
    rows = boxes * 2 * sources
    out_rows = 4 * tiles
    parents = parent_center.shape[0]
    vmem = pl.BlockSpec(memory_space=pltpu.VMEM)
    smem = pl.BlockSpec(memory_space=pltpu.SMEM)
    hbm = pl.BlockSpec(memory_space=pltpu.HBM)
    limit = pltpu.CompilerParams(vmem_limit_bytes=16 * 1024 * 1024)

    def cost(micros):
        return pl.CostEstimate(flops=int(micros * 1e9), bytes_accessed=int(micros * 3.6e6) + 1, transcendentals=0)


    def bf16(*shape):
        return jax.ShapeDtypeStruct(shape, jnp.bfloat16)

    def f32(*shape):
        return jax.ShapeDtypeStruct(shape, jnp.float32)

    def swap_with(array, step):
        return lax.ppermute(array, "wide", [(i, i ^ step) for i in range(n_wide)])

    def tie(*arrays):
        return lax.optimization_barrier(arrays)

    far = members - 2
    *heads, edge = pl.pallas_call(
        functools.partial(first_pack_kernel, groups - 1, members, piece),
        out_shape=[bf16(boxes, 2, sources, piece)] * far + [bf16(RIM, LANES)],
        in_specs=[hbm],
        out_specs=[vmem] * (far + 1),
        scratch_shapes=[
            pltpu.VMEM((2, boxes, 2, sources, LANES), jnp.bfloat16),
            pltpu.SemaphoreType.DMA((members,)),
        ],
        compiler_params=pltpu.CompilerParams(vmem_limit_bytes=16 * 1024 * 1024),
        cost_estimate=cost(0),
        name="pack_first",
    )(child_pattern)
    near = swap_with(child_pattern, 1)
    heads = [swap_with(head, swap + 2) for swap, head in enumerate(heads)]

    def other_half(array, step):
        pairs = [(i * 2 + n, (i ^ step) * 2 + 1 - n) for i in range(n_wide) for n in range(2)]
        return lax.ppermute(array, ("wide", "narrow"), pairs)

    near_edge = other_half(edge, 1)
    edge = other_half(edge, 0)
    tables = pl.pallas_call(
        functools.partial(prep_kernel, groups, members, boxes, piece),
        out_shape=[
            f32(groups, members * boxes, out_rows, LANES),
            f32(groups, members * boxes, out_rows, LANES),
            f32(parents, out_rows, LANES),
            f32(parents, out_rows, LANES),
            f32(groups, out_rows, LANES),
        ],
        in_specs=[smem, smem, smem, vmem],
        out_specs=[vmem] * 5,
        compiler_params=limit,
            cost_estimate=cost(0),
        name="prep",
    )(child_parent, child_octant, parent_center, stencil_start.reshape(-1, LANES))
    cosines, sines, center_cos, center_sin, excess = tables
    edge, excess = tie(edge, excess)
    full = tiles * rows + RIM
    pairs = members // 2 - 1
    sends = list(pl.pallas_call(
        functools.partial(rest_pack_kernel, groups, members, piece),
        out_shape=[
            bf16(2 * (full + (RIM if part == 1 else 0)), LANES) for part in range(1, groups) for _ in range(pairs)
        ],
        in_specs=[vmem] * 4,
        out_specs=[vmem] * ((groups - 1) * pairs),
        compiler_params=limit,
        cost_estimate=cost(0),
        name="pack_rest",
    )(child_pattern, near, edge, near_edge))
    bands = stencil_tables(2 * LANES, 4 * LANES)

    def sums_of(jobs, data, dtype, micros):
        shapes = [jax.ShapeDtypeStruct((2 * sources * len(columns_of(job[1], tiles)), LANES), dtype) for job in jobs]
        inputs = [*data, cosines, sines, excess, bands[0], bands[1]]
        return pl.pallas_call(
            functools.partial(combine_kernel, jobs, members, boxes, sources, tiles, len(data)),
            out_shape=shapes,
            in_specs=[vmem] * len(inputs),
            out_specs=[vmem] * len(jobs),
            scratch_shapes=[
                pltpu.VMEM((2, members * rows, 4 * LANES), jnp.float32),
                pltpu.VMEM((2 * sources * out_rows, LANES), jnp.float32),
            ],
            compiler_params=limit,
            cost_estimate=cost(micros),
            name="combine",
        )(*inputs)

    top = groups - 1
    inner = list(range(tiles - 1))
    outer = [-1, tiles - 1]
    every = list(range(-1, tiles))
    locals_ = [child_pattern, near]
    first_data = locals_ + heads
    first_places = [(2 + member, 0) for member in range(far)]
    (total,) = sums_of([(top, inner, first_places, None)], first_data, jnp.bfloat16, 5)
    early_sends = sends[pairs : 2 * pairs]
    *early_sends, total = tie(*early_sends, total)
    sends[pairs : 2 * pairs] = early_sends
    done = [swap_with(total, top * members)]
    arrived = {}
    for part in range(1, groups):
        step = top - part
        sent = sends[(part - 1) * pairs : part * pairs]
        if part == 3:
            data[0], done[0] = tie(data[0], done[0])
        if part > 1:
            totals = sums_of(jobs, data, jnp.bfloat16, 30)
            if part < groups - 1:
                tied = tie(*sends[part * pairs : (part + 1) * pairs], *totals)
                sends[part * pairs : (part + 1) * pairs], totals = tied[:pairs], tied[pairs:]
            arrived[step + 1] = swap_with(totals[0], (step + 1) * members)
            if part == 2:
                done.append(swap_with(totals[1], top * members))
        got = [swap_with(array, 2 * pair + 2) for pair, array in enumerate(sent)]
        length = full + (RIM if part == 1 else 0)
        places = [(2 + member // 2, member % 2 * length) for member in range(far)]
        if part == 1:
            rest = got + [edge, near_edge]
            far_rims = [(which - 2, row + full) for which, row in places]
        shift = 2 + pairs if part > 1 else 2
        data = locals_ + (got if part > 1 else []) + rest
        rims = [(None, (shift + pairs + member, 0)) for member in range(2)]
        rims += [
            ((which, row + tiles * rows), (shift + other, other_row))
            for (which, row), (other, other_row) in zip(places, far_rims)
        ]
        jobs = [(step, every, places, rims)]
        if part == 1:
            outer_rims = [(None, (shift + pairs + member, 0)) for member in range(2)]
            outer_rims += [((shift + which, row),) * 2 for which, row in far_rims]
            outer_places = [(len(data) + member, 0) for member in range(far)]
            jobs.append((top, outer, outer_places, outer_rims))
            data = data + heads
    (arrived[0],) = sums_of(jobs, data, jnp.float32, 30)
    done = [(top, columns_of(inner, tiles), done[0]), (top, columns_of(outer, tiles), done[1])]
    held = arrived
    ahead = [(0, columns_of(every, tiles), held[0])] + done
    final = [(step, columns_of(every, tiles), held[step]) for step in sorted(held) if step]

    def finish(last, pieces, extra):
        shapes = [f32(parents, 2 * sources * out_rows, LANES), f32(2 * sources * out_rows, LANES)]
        return pl.pallas_call(
            functools.partial(
                finish_kernel, last, [(step, columns) for step, columns, _ in pieces], members, boxes, sources, out_rows
            ),
            out_shape=shapes,
            in_specs=[smem] + [vmem] * (len(pieces) + 2) + ([vmem, hbm] if last else []),
            out_specs=[hbm if last else vmem, vmem],
            input_output_aliases={len(pieces) + 4: 0} if last else {},
            scratch_shapes=[
                pltpu.VMEM((len(pieces),) + shapes[1].shape, jnp.float32),
                pltpu.SemaphoreType.DMA((4 * len(pieces),)),
            ]
            if last
            else [],
            compiler_params=limit,
            cost_estimate=cost(0 if last else 30),
            name="finish_last" if last else "finish_ahead",
        )(child_parent, *[array for _, _, array in pieces], center_cos, center_sin, *extra)

    parent_pattern, far_field = finish(False, ahead, [])
    parent_pattern, far_field = finish(True, final, [far_field, parent_pattern])
    return (
        parent_pattern.reshape(parents, 2, sources, 1, 4 * piece),
        far_field.reshape(2, sources, 1, 4 * piece),
    )


def power_of_two(number):
    return number > 0 and number & (number - 1) == 0


def per_device(child_pattern, child_parent, child_octant, parent_center, stencil_start):
    n_wide, n_narrow = lax.axis_size("wide"), lax.axis_size("narrow")
    boxes, _, sources, block = child_pattern.shape
    parents = parent_center.shape[0]
    run = child_parent.shape[0] // parents
    if run % boxes == 0 and block % n_wide == 0:
        members = run // boxes
        fits = (
            n_narrow == 2
            and n_wide == members * parents
            and power_of_two(members)
            and power_of_two(parents)
            and members >= 4
            and parents >= 4
            and block // n_wide % LANES == 0
            and block // n_wide // LANES >= 3
            and boxes * 2 * sources == LANES
            and sources % 16 == 0
            and stencil_start.shape[0] == 4 * block * n_narrow
        )
        if fits:
            return grouped(child_pattern, child_parent, child_octant, parent_center, stencil_start, members)
    return exchanged(child_pattern, child_parent, child_octant, parent_center, stencil_start)


def solution(mesh):
    in_specs = (P("wide", None, None, "narrow"), P(), P(), P(), P())
    out_specs = (P(None, None, None, "narrow", "wide"), P(None, None, "narrow", "wide"))
    return jax.shard_map(
        per_device, mesh=mesh, in_specs=in_specs, out_specs=out_specs, check_vma=False
    )
```

```python
import functools
import math

import jax
import jax.numpy as jnp
import ml_dtypes
import numpy as np
from jax import lax
from jax.experimental import pallas as pl
from jax.experimental.pallas import tpu as pltpu
from jax.sharding import PartitionSpec as P

K2 = 65536


def with_halo(cells, sides, width):
    for axis, dim in sides:
        count = lax.axis_size(axis)
        head = lax.slice_in_dim(cells, 0, width, axis=dim)
        tail = lax.slice_in_dim(cells, cells.shape[dim] - width, cells.shape[dim], axis=dim)
        cells = jnp.concatenate(
            [
                lax.ppermute(tail, axis, [(i, (i + 1) % count) for i in range(count)]),
                cells,
                lax.ppermute(head, axis, [((i + 1) % count, i) for i in range(count)]),
            ],
            axis=dim,
        )
    return cells


def lagrange_taps(starts, first_out):
    sample_count = starts.shape[0]
    sample = first_out + jnp.arange(sample_count, dtype=jnp.int32)
    excess = sample // 4 - 2 - starts
    offset_u = (sample % 4).astype(jnp.float32) * 0.25 + 2.125 + excess.astype(jnp.float32)
    basis = []
    for node in range(6):
        value = jnp.ones_like(offset_u)
        for other in range(6):
            if other != node:
                value = value * (offset_u - other) / (node - other)
        basis.append(value)
    zeros = jnp.zeros_like(offset_u)
    stacked = []
    for offset in range(7):
        lower = basis[offset - 1] if offset >= 1 else zeros
        upper = basis[offset] if offset <= 5 else zeros
        stacked.append(jnp.where(excess == 0, lower, upper))
    return jnp.stack(stacked).reshape(7, sample_count // 4, 4)


def interpolate(window, tap_weights):
    block_len = tap_weights.shape[1]
    leading = window.shape[:-1]
    flat_rows = window.reshape((-1, window.shape[-1]))
    row_count = flat_rows.shape[0]
    if block_len % 64 == 0 and block_len > 64:
        group = 64
    else:
        group = block_len
    blocks = block_len // group
    taps = tap_weights.reshape(7, blocks, 4 * group)
    if blocks == 1:
        band_rows = flat_rows.shape[1]
        paired = flat_rows[:, None, :]
    else:
        band_rows = 2 * group
        extended = jnp.pad(flat_rows, ((0, 0), (0, (blocks + 1) * group - flat_rows.shape[1])))
        split_rows = extended.reshape(row_count, blocks + 1, group)
        paired = jnp.concatenate([split_rows[:, :-1], split_rows[:, 1:]], axis=2)
    column = jnp.arange(band_rows, dtype=jnp.int32)[None, :, None]
    target = (jnp.arange(4 * group, dtype=jnp.int32) // 4)[None, None, :]
    offsets = jnp.arange(7, dtype=jnp.int32)[:, None, None]
    onehot = (column == target + offsets).astype(jnp.float32)
    band = jnp.einsum("kcj,kbj->bcj", onehot, taps, precision=lax.Precision.HIGHEST)
    total = jnp.einsum(
        "rbc,bcj->rbj", paired.astype(jnp.float32), band, precision=lax.Precision.HIGHEST
    )
    return total.reshape(leading + (4 * block_len,)).astype(jnp.bfloat16)


def directions(first_out, sample_count):
    sample = first_out + jnp.arange(sample_count, dtype=jnp.int32)
    cycles = K2 // 256
    azimuth = 2.0 * math.pi * ((sample % 256).astype(jnp.float32) + 0.5) / 256.0
    polar = math.pi * ((sample // 256).astype(jnp.float32) + 0.5) / cycles
    return (jnp.sin(polar) * jnp.cos(azimuth), jnp.sin(polar) * jnp.sin(azimuth), jnp.cos(polar))


def child_phase(octant, dir_x, dir_y, dir_z):
    sign_x = (octant % 2 * 2 - 1).astype(jnp.float32)
    sign_y = (octant // 2 % 2 * 2 - 1).astype(jnp.float32)
    sign_z = (octant // 4 * 2 - 1).astype(jnp.float32)
    return (
        2.0
        * math.pi
        * 2.0
        * (sign_x[:, None] * dir_x + sign_y[:, None] * dir_y + sign_z[:, None] * dir_z)
    )


def shift_children(pattern, octant, dir_x, dir_y, dir_z):
    angle = child_phase(octant, dir_x, dir_y, dir_z)
    cosine = jnp.cos(angle)[:, None, :]
    sine_part = jnp.sin(angle)[:, None, :]
    real_part = pattern[:, 0].astype(jnp.float32)
    imag_part = pattern[:, 1].astype(jnp.float32)
    return jnp.stack(
        [cosine * real_part - sine_part * imag_part, sine_part * real_part + cosine * imag_part],
        axis=1,
    )


def exchanged(child_pattern, child_parent, child_octant, parent_center, stencil_start):
    n_wide = lax.axis_size("wide")
    box_count, _, sources, block_one = child_pattern.shape
    block_two = 4 * block_one
    piece_len = block_one // n_wide
    narrow_at = lax.axis_index("narrow")
    wide_at = lax.axis_index("wide")
    out_first = narrow_at * block_two + wide_at * (4 * piece_len)
    parent_count = parent_center.shape[0]
    parent_ids = jnp.arange(parent_count, dtype=jnp.int32)
    dir_x, dir_y, dir_z = directions(out_first, 4 * piece_len)
    padded = with_halo(child_pattern, (("narrow", 3),), 3)
    shape_pieces = (box_count, 2, sources, n_wide, piece_len)
    left_rim = padded[..., 0:block_one].reshape(shape_pieces)[..., :3]
    middle = padded[..., 3 : 3 + block_one].reshape(shape_pieces)
    right_rim = padded[..., 6 : 6 + block_one].reshape(shape_pieces)[..., piece_len - 3 :]
    windows = jnp.concatenate([left_rim, middle, right_rim], axis=-1)
    starts = lax.dynamic_slice_in_dim(stencil_start, out_first, 4 * piece_len)
    tap_weights = lagrange_taps(starts, out_first)
    gathered = interpolate(
        lax.all_to_all(windows, "wide", split_axis=3, concat_axis=0, tiled=True)[:, :, :, 0, :],
        tap_weights,
    )
    shifted = shift_children(gathered, child_octant, dir_x, dir_y, dir_z)
    selector = (child_parent[:, None] == parent_ids[None, :]).astype(jnp.float32)
    parents_total = jnp.einsum("bp,bcrj->pcrj", selector, shifted, precision=lax.Precision.HIGHEST)
    center_angle = (
        2.0
        * math.pi
        * (
            parent_center[:, 0:1] * dir_x
            + parent_center[:, 1:2] * dir_y
            + parent_center[:, 2:3] * dir_z
        )
    )
    center_cos = jnp.cos(center_angle)
    center_sin = jnp.sin(center_angle)
    real_sum = jnp.einsum(
        "pj,prj->rj", center_cos, parents_total[:, 0], precision=lax.Precision.HIGHEST
    ) - jnp.einsum("pj,prj->rj", center_sin, parents_total[:, 1], precision=lax.Precision.HIGHEST)
    imag_sum = jnp.einsum(
        "pj,prj->rj", center_sin, parents_total[:, 0], precision=lax.Precision.HIGHEST
    ) + jnp.einsum("pj,prj->rj", center_cos, parents_total[:, 1], precision=lax.Precision.HIGHEST)
    far_field = jnp.stack([real_sum, imag_sum]) / math.sqrt(parent_count)
    parent_pattern = parents_total[:, :, :, None, :]
    return (parent_pattern, far_field[:, :, None, :])


LANES = 128
HALO = 3
RIM = 16


def stencil_tables(window, columns):
    tables = np.zeros((2, window, columns), np.float32)
    for excess in range(2):
        for column in range(columns):
            offset_u = np.float32((column % 4) * 0.25 + 2.125 + excess)
            first = window // 4 + column // 4 - 2 - excess
            for node in range(6):
                value = np.float32(1.0)
                for other in range(6):
                    if other != node:
                        value = np.float32(
                            value * np.float32(np.float32(offset_u - np.float32(other)) / np.float32(node - other))
                        )
                tables[excess, first + node, column] = value
    high = tables.astype(ml_dtypes.bfloat16)
    low = (tables - high.astype(np.float32)).astype(ml_dtypes.bfloat16)
    return np.concatenate([high, low], axis=1)


def rim_masks():
    slot = lax.broadcasted_iota(jnp.int32, (RIM, LANES), 0)
    lane = lax.broadcasted_iota(jnp.int32, (RIM, LANES), 1)
    return slot, lane


def as_mask(condition):
    return jnp.where(condition, 1.0, 0.0).astype(jnp.bfloat16)


def rim_of(before, after, first_slot):
    slot, lane = rim_masks()
    slot = slot - first_slot
    pick_before = as_mask((slot >= 0) & (slot < HALO) & (lane == LANES - HALO + slot))
    pick_after = as_mask((slot >= HALO) & (slot < 2 * HALO) & (lane == slot - HALO))
    across = (((1,), (1,)), ((), ()))
    rim = lax.dot_general(pick_before, before, across, preferred_element_type=jnp.float32)
    return rim + lax.dot_general(pick_after, after, across, preferred_element_type=jnp.float32)


def rest_pack_kernel(groups, members, piece, cells, near, *outs):
    boxes, parts, sources, block = cells.shape
    rows = boxes * parts * sources
    tiles = piece // LANES
    wide_at = lax.axis_index("wide")
    group_at, member_at = wide_at // members, wide_at % members

    def tile(ref, at):
        return ref[:, :, :, pl.ds(pl.multiple_of(at, LANES), LANES)].reshape(rows, LANES)

    def rim_at(ref, first):
        return rim_of(tile(ref, jnp.maximum(first - LANES, 0)), tile(ref, jnp.minimum(first + piece, block - LANES)), 0)

    edges = outs[-1]
    for half, ref in enumerate((cells, near)):
        rim = rim_of(tile(ref, block - LANES), tile(ref, 0), 2 * HALO)
        edges[half * RIM : (half + 1) * RIM, :] = rim.astype(jnp.bfloat16)
    for part in range(1, groups):
        for swap in range(2, members, 2):
            out, base = outs[(part - 1) * (members // 2 - 1) + swap // 2 - 1], 0
            target = member_at ^ swap
            first = ((group_at ^ (groups - 1 - part)) * members + target) * piece
            for ref in (cells, near):
                for index in range(tiles):
                    out[base : base + rows, :] = tile(ref, first + index * LANES)
                    base += rows
                out[base : base + RIM, :] = rim_at(ref, first).astype(jnp.bfloat16)
                base += RIM
                if part == 1:
                    rim = rim_at(ref, ((group_at ^ (groups - 1)) * members + target) * piece)
                    out[base : base + RIM, :] = rim.astype(jnp.bfloat16)
                    base += RIM


def turned(cycles):
    half = math.pi * (cycles - jnp.floor(cycles + 0.5))
    square = half * half
    sine, cosine = jnp.zeros_like(half), jnp.zeros_like(half)
    for order in range(13, 0, -2):
        sine = sine * square + (-1) ** (order // 2) / math.factorial(order)
        cosine = cosine * square + (-1) ** (order // 2) / math.factorial(order - 1)
    sine = sine * half
    return 1.0 - 2.0 * sine * sine, 2.0 * sine * cosine


def axes_kernel(groups, members, piece, sample_count, cosines, sines, center_dirs):
    wide_at = lax.axis_index("wide")
    group_at, member_at = wide_at // members, wide_at % members
    rows = 4 * piece // LANES
    half_rows = sample_count // LANES // lax.axis_size("narrow")
    row = lax.broadcasted_iota(jnp.int32, (rows, LANES), 0)
    lane = lax.broadcasted_iota(jnp.int32, (rows, LANES), 1)
    cos_azimuth, sin_azimuth = turned((((row * LANES + lane) & 255).astype(jnp.float32) + 0.5) / 256.0)
    for step in range(groups):
        first_row = lax.axis_index("narrow") * half_rows + ((group_at ^ step) * members + member_at) * rows
        ring = ((first_row + row) * LANES + lane) >> 8
        dir_z, sin_polar = turned((ring.astype(jnp.float32) + 0.5) / (2 * (sample_count // 256)))
        for axis, direction in enumerate((sin_polar * cos_azimuth, sin_polar * sin_azimuth, dir_z)):
            cosines[step, axis], sines[step, axis] = turned(2.0 * direction)
            if step == 0:
                center_dirs[axis] = direction


def prep_kernel(
    groups, members, boxes, piece, parent_of, octant_of, center, starts, axis_cos, axis_sin, center_dirs,
    cosines, sines, center_cos, center_sin, excess, held, sems,
):
    wide_at = lax.axis_index("wide")
    group_at, member_at = wide_at // members, wide_at % members
    rows = 4 * piece // LANES
    half_rows = starts.shape[0] // lax.axis_size("narrow")
    row = lax.broadcasted_iota(jnp.int32, (rows, LANES), 0)
    lane = lax.broadcasted_iota(jnp.int32, (rows, LANES), 1)
    first_rows = [
        pl.multiple_of(lax.axis_index("narrow") * half_rows + ((group_at ^ step) * members + member_at) * rows, 8)
        for step in range(groups)
    ]
    copies = [
        pltpu.make_async_copy(starts.at[pl.ds(first_rows[step], rows)], held.at[step], sems.at[step]) for step in range(groups)
    ]
    for copy in copies:
        copy.start()
    scale = 1.0 / math.sqrt(center.shape[0])
    for step in range(groups):
        parent = parent_of[(group_at ^ step) * members * boxes]
        turns = sum(center[parent, axis] * center_dirs[axis] for axis in range(3))
        turn_cos, turn_sin = turned(turns)
        center_cos[step] = turn_cos * scale
        center_sin[step] = turn_sin * scale
    for step in range(groups):
        (cos_x, cos_y, cos_z), (sin_x, sin_y, sin_z) = ([table[step, axis] for axis in range(3)] for table in (axis_cos, axis_sin))
        both_cos, both_sin, sin_cos, cos_sin = cos_x * cos_y, sin_x * sin_y, sin_x * cos_y, cos_x * sin_y
        for swap in range(members):
            for box in range(boxes):
                slot = (group_at * members + (member_at ^ swap)) * boxes + box
                octant = octant_of[slot]
                live = jnp.where(parent_of[slot] >= 0, 1.0, 0.0)
                sign_x = ((octant & 1) * 2 - 1).astype(jnp.float32)
                sign_y = (((octant >> 1) & 1) * 2 - 1).astype(jnp.float32)
                sign_z = ((octant >> 2) * 2 - 1).astype(jnp.float32)
                real = both_cos - (sign_x * sign_y) * both_sin
                imag = sign_x * sin_cos + sign_y * cos_sin
                turn_cos, turn_sin = live * cos_z, (live * sign_z) * sin_z
                cosines[step, swap * boxes + box] = real * turn_cos - imag * turn_sin
                sines[step, swap * boxes + box] = real * turn_sin + imag * turn_cos
    for step in range(groups):
        copies[step].wait()
        child = ((first_rows[step] + row) * LANES + lane) >> 2
        excess[step] = (child - 2 - held[step]).astype(jnp.float32)


def columns_of(windows):
    return [2 * window + half for window in windows for half in range(2)]


def combine_kernel(jobs, members, boxes, sources, tiles, count, *refs):
    data = refs[:count]
    cosines, sines, excess, band_zero, band_one = refs[count : count + 5]
    *outs, spread, total = refs[count + 5 :]
    for (step, *job), out in zip(jobs, outs):
        combine(
            step, *job, members, boxes, sources, tiles, data, cosines.at[step], sines.at[step], excess.at[step],
            band_zero, band_one, out, spread, total,
        )


def combine(
    step, windows, places, rims, members, boxes, sources, tiles, data, cosines, sines, excess, band_zero, band_one, out, spread, total
):
    rows = boxes * 2 * sources
    block = data[0].shape[3]
    wide_at = lax.axis_index("wide")
    last = lax.axis_size("wide") - 1
    at = ((wide_at // members) ^ step) * members + wide_at % members
    first = at * (tiles * LANES)

    def local(ref, lane):
        return ref[:, :, :, pl.ds(pl.multiple_of(lane, LANES), LANES)].reshape(rows, LANES)

    def tile(index):
        if index < 0 or index >= tiles:
            return rim_tile
        found = [local(data[member], first + index * LANES) for member in range(2)]
        for which, base in places:
            ref = data[which]
            if len(ref.shape) == 4:
                found.append(ref[:, :, :, index * LANES : (index + 1) * LANES].reshape(rows, LANES))
            else:
                found.append(ref[base + index * rows : base + (index + 1) * rows, :])
        return jnp.concatenate(found, axis=0)

    if rims is not None:
        slot, lane = rim_masks()
        from_other = slot >= 2 * HALO
        side = jnp.where(from_other, slot - 2 * HALO, slot)
        outer = ((side < HALO) & (at == 0)) | ((side >= HALO) & (at == last))
        keep = (outer == from_other) & (slot < 4 * HALO)
        place = as_mask(
            ((side < HALO) & (lane == LANES - HALO + side)) | ((side >= HALO) & (side < 2 * HALO) & (lane == side - HALO))
        )
        found = []
        for inner, (other, other_row) in rims:
            outside = data[other][other_row : other_row + RIM, :].astype(jnp.float32)
            if inner is None:
                inside = jnp.zeros((RIM, LANES), jnp.float32)
            else:
                inside = data[inner[0]][inner[1] : inner[1] + RIM, :].astype(jnp.float32)
            found.append(jnp.where(keep, jnp.where(from_other, outside, inside), 0.0).astype(jnp.bfloat16))
        rim = jnp.concatenate(found, axis=1)
        rim_tile = lax.dot_general(rim, place, (((0,), (0,)), ((), ())), preferred_element_type=jnp.float32)
        lane = lax.broadcasted_iota(jnp.int32, (rows, LANES), 1)
        from_before = (lane >= LANES - HALO) & (at != 0)
        from_after = (lane < HALO) & (at != last)
        near = []
        for member in range(2):
            before = local(data[member], jnp.maximum(first - LANES, 0)).astype(jnp.float32)
            after = local(data[member], jnp.minimum(first + tiles * LANES, block - LANES)).astype(jnp.float32)
            near.append(jnp.where(from_before, before, jnp.where(from_after, after, 0.0)))
        near = jnp.concatenate(near, axis=0)
        rim_tile = jnp.concatenate([rim_tile[: 2 * rows] + near, rim_tile[2 * rows :]], axis=0).astype(jnp.bfloat16)

    def window_of(window):
        cut = 32 if window % 2 else 96
        left, right = tile((window - 1 + window % 2) // 2), tile((window + 1) // 2)
        cells = jnp.concatenate([left[:, cut:], right[:, :cut]], axis=1)
        return jnp.concatenate([cells, cells], axis=1)

    columns = columns_of(windows)
    width = len(columns)

    def spread_window(turn):
        bands = []
        for half, column in enumerate(columns[2 * turn : 2 * turn + 2]):
            which = jnp.broadcast_to(excess[column : column + 1, :], (16, LANES)).astype(jnp.bfloat16)
            which = jnp.concatenate([which] * (band_zero.shape[0] // 16), axis=0)
            lanes = slice(half * LANES, (half + 1) * LANES)
            bands.append(band_zero[:, lanes] * (1 - which) + band_one[:, lanes] * which)
        spread[turn % 2] = jnp.dot(
            window_of(windows[turn]), jnp.concatenate(bands, axis=1), preferred_element_type=jnp.float32
        )

    def sum_window(turn):
        for half, column in enumerate(columns[2 * turn : 2 * turn + 2]):
            lanes = slice(half * LANES, (half + 1) * LANES)
            real_sum = jnp.zeros((sources, LANES), jnp.float32)
            imag_sum = jnp.zeros((sources, LANES), jnp.float32)
            for child in range(members * boxes):
                start = child * 2 * sources
                real = spread[turn % 2, start : start + sources, lanes].astype(jnp.bfloat16).astype(jnp.float32)
                imag = spread[turn % 2, start + sources : start + 2 * sources, lanes]
                imag = imag.astype(jnp.bfloat16).astype(jnp.float32)
                cosine = cosines[child, column : column + 1, :]
                sine = sines[child, column : column + 1, :]
                real_sum = real_sum + (cosine * real - sine * imag)
                imag_sum = imag_sum + (sine * real + cosine * imag)
            at_row = 2 * turn + half
            total[pl.ds(at_row, sources, stride=width), :] = real_sum
            total[pl.ds(sources * width + at_row, sources, stride=width), :] = imag_sum

    for turn in range(len(windows) + 1):
        if turn < len(windows):
            spread_window(turn)
        if turn:
            sum_window(turn - 1)
    out[: 2 * sources * width, :] = total[: 2 * sources * width, :].astype(out.dtype)
    if out.shape[0] > 2 * sources * width:
        out[2 * sources * width :, :] = jnp.zeros((out.shape[0] - 2 * sources * width, LANES), out.dtype)


def spans_of(columns):
    spans, begin = [], 0
    for i in range(1, len(columns) + 1):
        if i == len(columns) or columns[i] != columns[i - 1] + 1:
            spans.append((begin, columns[begin], i - begin))
            begin = i
    return spans


def finish_ahead_kernel(own_step, early_step, columns, members, boxes, sources, rows, parent_of, own, early, center_cos, center_sin, parent_out, far_out, early_out):
    name = parent_of[((lax.axis_index("wide") // members) ^ own_step) * members * boxes]
    width = len(columns)
    for source in range(sources):
        real_at, imag_at = (pl.ds((half * sources + source) * rows, rows) for half in range(2))
        real, imag = own[real_at, :], own[imag_at, :]
        cosine, sine = center_cos[own_step], center_sin[own_step]
        parent_out[name, real_at, :] = real
        parent_out[name, imag_at, :] = imag
        far_out[real_at, :] = cosine * real - sine * imag
        far_out[imag_at, :] = sine * real + cosine * imag
        for begin, column, length in spans_of(columns):
            real, imag = (early[pl.ds((half * sources + source) * width + begin, length), :].astype(jnp.float32) for half in range(2))
            cosine, sine = (table[early_step, column : column + length, :] for table in (center_cos, center_sin))
            real_at, imag_at = (pl.ds((half * sources + source) * rows + column, length) for half in range(2))
            early_out[real_at, :] = real
            early_out[imag_at, :] = imag
            far_out[real_at, :] += cosine * real - sine * imag
            far_out[imag_at, :] += sine * real + cosine * imag


def finish_kernel(steps, early_step, columns, members, boxes, sources, rows, parts, parent_of, *refs):
    whole, refs = refs[: len(steps)], refs[len(steps) :]
    late, early, center_cos, center_sin, far_in, _, parent_out, far_out, names, held, far_held, name_sem, sems = refs
    name_copy = pltpu.make_async_copy(parent_of, names, name_sem)
    name_copy.start()
    width = len(columns)
    group_at = lax.axis_index("wide") // members
    copies = []
    each = sources // parts
    for part in range(parts):
        for source in range(part * each, (part + 1) * each):
            real_at, imag_at = (pl.ds((half * sources + source) * rows, rows) for half in range(2))
            far_real, far_imag = far_in[real_at, :], far_in[imag_at, :]
            for index, step in enumerate(steps):
                real, imag = whole[index][real_at, :].astype(jnp.float32), whole[index][imag_at, :].astype(jnp.float32)
                cosine, sine = center_cos[step], center_sin[step]
                held[index, real_at, :] = real
                held[index, imag_at, :] = imag
                far_real = far_real + (cosine * real - sine * imag)
                far_imag = far_imag + (sine * real + cosine * imag)
            far_held[real_at, :] = far_real
            far_held[imag_at, :] = far_imag
            index = len(steps)
            held[index, real_at, :] = early[real_at, :]
            held[index, imag_at, :] = early[imag_at, :]
            for begin, column, length in spans_of(columns):
                real, imag = (late[pl.ds((half * sources + source) * width + begin, length), :].astype(jnp.float32) for half in range(2))
                cosine, sine = (table[early_step, column : column + length, :] for table in (center_cos, center_sin))
                real_at, imag_at = (pl.ds((half * sources + source) * rows + column, length) for half in range(2))
                held[index, real_at, :] = real
                held[index, imag_at, :] = imag
                far_held[real_at, :] += cosine * real - sine * imag
                far_held[imag_at, :] += sine * real + cosine * imag
        if part == 0:
            name_copy.wait()
            places = [names[(group_at ^ step) * members * boxes] for step in (*steps, early_step)]
        for half in range(2):
            at = pl.ds((half * sources + part * each) * rows, each * rows)
            moves = [(held.at[index, at], parent_out.at[place, at]) for index, place in enumerate(places)]
            for source, target in moves + [(far_held.at[at], far_out.at[at])]:
                copies.append(pltpu.make_async_copy(source, target, sems.at[len(copies)]))
                copies[-1].start()
    for copy in copies:
        copy.wait()


def grouped(child_pattern, child_parent, child_octant, parent_center, stencil_start, members):
    n_wide = lax.axis_size("wide")
    boxes, _, sources, block = child_pattern.shape
    groups = n_wide // members
    piece = block // n_wide
    tiles = piece // LANES
    rows = boxes * 2 * sources
    out_rows = 4 * tiles
    parents = parent_center.shape[0]
    vmem = pl.BlockSpec(memory_space=pltpu.VMEM)
    smem = pl.BlockSpec(memory_space=pltpu.SMEM)
    hbm = pl.BlockSpec(memory_space=pltpu.HBM)
    limit = pltpu.CompilerParams(vmem_limit_bytes=16 * 1024 * 1024)

    def cost(micros):
        return pl.CostEstimate(flops=int(micros * 1e9), bytes_accessed=int(micros * 3.6e6) + 1, transcendentals=0)


    def bf16(*shape):
        return jax.ShapeDtypeStruct(shape, jnp.bfloat16)

    def f32(*shape):
        return jax.ShapeDtypeStruct(shape, jnp.float32)

    def swap_with(array, step):
        return lax.ppermute(array, "wide", [(i, i ^ step) for i in range(n_wide)])

    def tie(*arrays):
        return lax.optimization_barrier(arrays)

    far = members - 2
    wide_at = lax.axis_index("wide")
    heads = []
    for swap in range(2, members):
        first = (((wide_at // members) ^ (groups - 1)) * members + ((wide_at % members) ^ swap)) * piece
        heads.append(lax.dynamic_slice_in_dim(child_pattern, first, piece, 3))
    near = swap_with(child_pattern, 1)
    heads = [swap_with(head, swap + 2) for swap, head in enumerate(heads)]

    def other_half(array, step):
        pairs = [(i * 2 + n, (i ^ step) * 2 + 1 - n) for i in range(n_wide) for n in range(2)]
        return lax.ppermute(array, ("wide", "narrow"), pairs)

    axes = pl.pallas_call(
        functools.partial(axes_kernel, groups, members, piece, stencil_start.shape[0]),
        out_shape=[f32(groups, 3, out_rows, LANES)] * 2 + [f32(3, out_rows, LANES)],
        out_specs=[vmem] * 3,
        compiler_params=limit,
        cost_estimate=cost(1),
        name="axes",
    )()
    tables = pl.pallas_call(
        functools.partial(prep_kernel, groups, members, boxes, piece),
        out_shape=[
            f32(groups, members * boxes, out_rows, LANES),
            f32(groups, members * boxes, out_rows, LANES),
            f32(parents, out_rows, LANES),
            f32(parents, out_rows, LANES),
            f32(groups, out_rows, LANES),
        ],
        in_specs=[smem, smem, smem, hbm] + [vmem] * 3,
        out_specs=[vmem] * 5,
        scratch_shapes=[pltpu.VMEM((groups, out_rows, LANES), jnp.int32), pltpu.SemaphoreType.DMA((groups,))],
        compiler_params=limit,
            cost_estimate=cost(1),
        name="prep",
    )(child_parent, child_octant, parent_center, stencil_start.reshape(-1, LANES), *axes)
    cosines, sines, center_cos, center_sin, excess = tables
    full = tiles * rows + RIM
    pairs = members // 2 - 1
    *sends, edges = pl.pallas_call(
        functools.partial(rest_pack_kernel, groups, members, piece),
        out_shape=[
            bf16(2 * (full + (RIM if part == 1 else 0)), LANES) for part in range(1, groups) for _ in range(pairs)
        ]
        + [bf16(2 * RIM, LANES)],
        in_specs=[vmem] * 2,
        out_specs=[vmem] * ((groups - 1) * pairs + 1),
        compiler_params=limit,
        cost_estimate=cost(1),
        name="pack",
    )(child_pattern, near)
    common = [other_half(edges, 2 * pair) for pair in range(pairs + 1)]
    bands = stencil_tables(LANES, 2 * LANES)

    top = groups - 1

    def sums_of(jobs, data, dtype, micros):
        shapes = [
            jax.ShapeDtypeStruct((2 * sources * len(columns_of(job[1])) + (RIM if job[0] == top - 1 else 0), LANES), dtype)
            for job in jobs
        ]
        inputs = [*data, cosines, sines, excess, bands[0], bands[1]]
        return pl.pallas_call(
            functools.partial(combine_kernel, jobs, members, boxes, sources, tiles, len(data)),
            out_shape=shapes,
            in_specs=[vmem] * len(inputs),
            out_specs=[vmem] * len(shapes),
            scratch_shapes=[
                pltpu.VMEM((2, members * rows, 2 * LANES), jnp.float32),
                pltpu.VMEM((2 * sources * out_rows, LANES), jnp.float32),
            ],
            compiler_params=limit,
            cost_estimate=cost(micros),
            name="combine",
        )(*inputs)

    inner = list(range(1, 2 * tiles - 1))
    outer = [0, 2 * tiles - 1]
    every = list(range(2 * tiles))
    locals_ = [child_pattern, near]
    first_data = locals_ + heads
    first_places = [(2 + member, 0) for member in range(far)]
    (total,) = sums_of([(top, inner, first_places, None)], first_data, jnp.bfloat16, 5)
    early_sends = sends[pairs : 2 * pairs]
    *early_sends, total = tie(*early_sends, total)
    sends[pairs : 2 * pairs] = early_sends
    done = [swap_with(total, top * members)]
    arrived = {}
    for part in range(1, groups):
        step = top - part
        sent = sends[(part - 1) * pairs : part * pairs]
        if part > 1:
            totals = list(sums_of(jobs, data, jnp.bfloat16, 30 if part == 2 else 2))
            if part < groups - 1:
                tied = tie(*sends[part * pairs : (part + 1) * pairs], *totals)
                sends[part * pairs : (part + 1) * pairs], totals = tied[:pairs], list(tied[pairs:])
            arrived[step + 1] = swap_with(totals[0], (step + 1) * members)
            if part == 2:
                done.append(swap_with(totals[1], top * members))
        got = [swap_with(array, 2 * pair + 2) for pair, array in enumerate(sent)]
        length = full + (RIM if part == 1 else 0)
        places = [(2 + member // 2, member % 2 * length) for member in range(far)]
        data = locals_ + got + common
        shift = 2 + pairs
        edge_at = [(shift + member // 2, member % 2 * RIM) for member in range(members)]
        rims = [None, None] + [(which, row + tiles * rows) for which, row in places]
        jobs = [(step, every, places, list(zip(rims, edge_at)))]
        if part == 1:
            rims = [None, None] + [(which, row + full) for which, row in places]
            outer_places = [(len(data) + member, 0) for member in range(far)]
            jobs.append((top, outer, outer_places, list(zip(rims, edge_at))))
            data = data + heads
    data[0], done[0] = tie(data[0], done[0])
    (arrived[0],) = sums_of(jobs, data, jnp.float32, 1)
    done = [(top, columns_of(inner), done[0]), (top, columns_of(outer), done[1])]
    held = arrived
    whole = f32(2 * sources * out_rows, LANES)
    (_, early_columns, early_array), (_, late_columns, late_array) = done
    parent_pattern, far_field, early_pattern = pl.pallas_call(
        functools.partial(finish_ahead_kernel, 0, top, early_columns, members, boxes, sources, out_rows),
        out_shape=[f32(parents, *whole.shape), whole, whole],
        in_specs=[smem] + [vmem] * 4,
        out_specs=[vmem] * 3,
        compiler_params=limit,
        cost_estimate=cost(0),
        name="finish_ahead",
    )(child_parent, held[0], early_array, center_cos, center_sin)
    steps = sorted((step for step in held if step), reverse=True)
    parts = 4
    parent_pattern, far_field = pl.pallas_call(
        functools.partial(finish_kernel, steps, top, late_columns, members, boxes, sources, out_rows, parts),
        out_shape=[f32(parents, *whole.shape), whole],
        in_specs=[hbm] + [vmem] * (len(steps) + 5) + [hbm],
        out_specs=[hbm, hbm],
        input_output_aliases={len(steps) + 6: 0},
        scratch_shapes=[
            pltpu.SMEM(child_parent.shape, jnp.int32),
            pltpu.VMEM((len(steps) + 1, *whole.shape), jnp.float32),
            pltpu.VMEM(whole.shape, jnp.float32),
            pltpu.SemaphoreType.DMA,
            pltpu.SemaphoreType.DMA((2 * parts * (len(steps) + 2),)),
        ],
        compiler_params=limit,
        cost_estimate=cost(30),
        name="finish_last",
    )(child_parent, *[held[step] for step in steps], late_array, early_pattern, center_cos, center_sin, far_field, parent_pattern)
    return (
        parent_pattern.reshape(parents, 2, sources, 1, 4 * piece),
        far_field.reshape(2, sources, 1, 4 * piece),
    )


def power_of_two(number):
    return number > 0 and number & (number - 1) == 0


def per_device(child_pattern, child_parent, child_octant, parent_center, stencil_start):
    n_wide, n_narrow = lax.axis_size("wide"), lax.axis_size("narrow")
    boxes, _, sources, block = child_pattern.shape
    parents = parent_center.shape[0]
    run = child_parent.shape[0] // parents
    if run % boxes == 0 and block % n_wide == 0:
        members = run // boxes
        fits = (
            n_narrow == 2
            and n_wide == members * parents
            and power_of_two(members)
            and power_of_two(parents)
            and members >= 4
            and parents >= 4
            and block // n_wide % LANES == 0
            and block // n_wide // LANES >= 3
            and boxes * 2 * sources == LANES
            and sources % 16 == 0
            and stencil_start.shape[0] == 4 * block * n_narrow
        )
        if fits:
            return grouped(child_pattern, child_parent, child_octant, parent_center, stencil_start, members)
    return exchanged(child_pattern, child_parent, child_octant, parent_center, stencil_start)


def solution(mesh):
    in_specs = (P("wide", None, None, "narrow"), P(), P(), P(), P())
    out_specs = (P(None, None, None, "narrow", "wide"), P(None, None, "narrow", "wide"))
    return jax.shard_map(
        per_device, mesh=mesh, in_specs=in_specs, out_specs=out_specs, check_vma=False
    )
```

```python
import functools
import math

import jax
import jax.numpy as jnp
import ml_dtypes
import numpy as np
from jax import lax
from jax.experimental import pallas as pl
from jax.experimental.pallas import tpu as pltpu
from jax.sharding import PartitionSpec as P

K2 = 65536


def with_halo(cells, sides, width):
    for axis, dim in sides:
        count = lax.axis_size(axis)
        head = lax.slice_in_dim(cells, 0, width, axis=dim)
        tail = lax.slice_in_dim(cells, cells.shape[dim] - width, cells.shape[dim], axis=dim)
        cells = jnp.concatenate(
            [
                lax.ppermute(tail, axis, [(i, (i + 1) % count) for i in range(count)]),
                cells,
                lax.ppermute(head, axis, [((i + 1) % count, i) for i in range(count)]),
            ],
            axis=dim,
        )
    return cells


def lagrange_taps(starts, first_out):
    sample_count = starts.shape[0]
    sample = first_out + jnp.arange(sample_count, dtype=jnp.int32)
    excess = sample // 4 - 2 - starts
    offset_u = (sample % 4).astype(jnp.float32) * 0.25 + 2.125 + excess.astype(jnp.float32)
    basis = []
    for node in range(6):
        value = jnp.ones_like(offset_u)
        for other in range(6):
            if other != node:
                value = value * (offset_u - other) / (node - other)
        basis.append(value)
    zeros = jnp.zeros_like(offset_u)
    stacked = []
    for offset in range(7):
        lower = basis[offset - 1] if offset >= 1 else zeros
        upper = basis[offset] if offset <= 5 else zeros
        stacked.append(jnp.where(excess == 0, lower, upper))
    return jnp.stack(stacked).reshape(7, sample_count // 4, 4)


def interpolate(window, tap_weights):
    block_len = tap_weights.shape[1]
    leading = window.shape[:-1]
    flat_rows = window.reshape((-1, window.shape[-1]))
    row_count = flat_rows.shape[0]
    if block_len % 64 == 0 and block_len > 64:
        group = 64
    else:
        group = block_len
    blocks = block_len // group
    taps = tap_weights.reshape(7, blocks, 4 * group)
    if blocks == 1:
        band_rows = flat_rows.shape[1]
        paired = flat_rows[:, None, :]
    else:
        band_rows = 2 * group
        extended = jnp.pad(flat_rows, ((0, 0), (0, (blocks + 1) * group - flat_rows.shape[1])))
        split_rows = extended.reshape(row_count, blocks + 1, group)
        paired = jnp.concatenate([split_rows[:, :-1], split_rows[:, 1:]], axis=2)
    column = jnp.arange(band_rows, dtype=jnp.int32)[None, :, None]
    target = (jnp.arange(4 * group, dtype=jnp.int32) // 4)[None, None, :]
    offsets = jnp.arange(7, dtype=jnp.int32)[:, None, None]
    onehot = (column == target + offsets).astype(jnp.float32)
    band = jnp.einsum("kcj,kbj->bcj", onehot, taps, precision=lax.Precision.HIGHEST)
    total = jnp.einsum(
        "rbc,bcj->rbj", paired.astype(jnp.float32), band, precision=lax.Precision.HIGHEST
    )
    return total.reshape(leading + (4 * block_len,)).astype(jnp.bfloat16)


def directions(first_out, sample_count):
    sample = first_out + jnp.arange(sample_count, dtype=jnp.int32)
    cycles = K2 // 256
    azimuth = 2.0 * math.pi * ((sample % 256).astype(jnp.float32) + 0.5) / 256.0
    polar = math.pi * ((sample // 256).astype(jnp.float32) + 0.5) / cycles
    return (jnp.sin(polar) * jnp.cos(azimuth), jnp.sin(polar) * jnp.sin(azimuth), jnp.cos(polar))


def child_phase(octant, dir_x, dir_y, dir_z):
    sign_x = (octant % 2 * 2 - 1).astype(jnp.float32)
    sign_y = (octant // 2 % 2 * 2 - 1).astype(jnp.float32)
    sign_z = (octant // 4 * 2 - 1).astype(jnp.float32)
    return (
        2.0
        * math.pi
        * 2.0
        * (sign_x[:, None] * dir_x + sign_y[:, None] * dir_y + sign_z[:, None] * dir_z)
    )


def shift_children(pattern, octant, dir_x, dir_y, dir_z):
    angle = child_phase(octant, dir_x, dir_y, dir_z)
    cosine = jnp.cos(angle)[:, None, :]
    sine_part = jnp.sin(angle)[:, None, :]
    real_part = pattern[:, 0].astype(jnp.float32)
    imag_part = pattern[:, 1].astype(jnp.float32)
    return jnp.stack(
        [cosine * real_part - sine_part * imag_part, sine_part * real_part + cosine * imag_part],
        axis=1,
    )


def exchanged(child_pattern, child_parent, child_octant, parent_center, stencil_start):
    n_wide = lax.axis_size("wide")
    box_count, _, sources, block_one = child_pattern.shape
    block_two = 4 * block_one
    piece_len = block_one // n_wide
    narrow_at = lax.axis_index("narrow")
    wide_at = lax.axis_index("wide")
    out_first = narrow_at * block_two + wide_at * (4 * piece_len)
    parent_count = parent_center.shape[0]
    parent_ids = jnp.arange(parent_count, dtype=jnp.int32)
    dir_x, dir_y, dir_z = directions(out_first, 4 * piece_len)
    padded = with_halo(child_pattern, (("narrow", 3),), 3)
    shape_pieces = (box_count, 2, sources, n_wide, piece_len)
    left_rim = padded[..., 0:block_one].reshape(shape_pieces)[..., :3]
    middle = padded[..., 3 : 3 + block_one].reshape(shape_pieces)
    right_rim = padded[..., 6 : 6 + block_one].reshape(shape_pieces)[..., piece_len - 3 :]
    windows = jnp.concatenate([left_rim, middle, right_rim], axis=-1)
    starts = lax.dynamic_slice_in_dim(stencil_start, out_first, 4 * piece_len)
    tap_weights = lagrange_taps(starts, out_first)
    gathered = interpolate(
        lax.all_to_all(windows, "wide", split_axis=3, concat_axis=0, tiled=True)[:, :, :, 0, :],
        tap_weights,
    )
    shifted = shift_children(gathered, child_octant, dir_x, dir_y, dir_z)
    selector = (child_parent[:, None] == parent_ids[None, :]).astype(jnp.float32)
    parents_total = jnp.einsum("bp,bcrj->pcrj", selector, shifted, precision=lax.Precision.HIGHEST)
    center_angle = (
        2.0
        * math.pi
        * (
            parent_center[:, 0:1] * dir_x
            + parent_center[:, 1:2] * dir_y
            + parent_center[:, 2:3] * dir_z
        )
    )
    center_cos = jnp.cos(center_angle)
    center_sin = jnp.sin(center_angle)
    real_sum = jnp.einsum(
        "pj,prj->rj", center_cos, parents_total[:, 0], precision=lax.Precision.HIGHEST
    ) - jnp.einsum("pj,prj->rj", center_sin, parents_total[:, 1], precision=lax.Precision.HIGHEST)
    imag_sum = jnp.einsum(
        "pj,prj->rj", center_sin, parents_total[:, 0], precision=lax.Precision.HIGHEST
    ) + jnp.einsum("pj,prj->rj", center_cos, parents_total[:, 1], precision=lax.Precision.HIGHEST)
    far_field = jnp.stack([real_sum, imag_sum]) / math.sqrt(parent_count)
    parent_pattern = parents_total[:, :, :, None, :]
    return (parent_pattern, far_field[:, :, None, :])


LANES = 128
HALO = 3
RIM = 16


def stencil_tables(window, columns):
    tables = np.zeros((2, window, columns), np.float32)
    for excess in range(2):
        for column in range(columns):
            offset_u = np.float32((column % 4) * 0.25 + 2.125 + excess)
            first = window // 4 + column // 4 - 2 - excess
            for node in range(6):
                value = np.float32(1.0)
                for other in range(6):
                    if other != node:
                        value = np.float32(
                            value * np.float32(np.float32(offset_u - np.float32(other)) / np.float32(node - other))
                        )
                tables[excess, first + node, column] = value
    high = tables.astype(ml_dtypes.bfloat16)
    low = (tables - high.astype(np.float32)).astype(ml_dtypes.bfloat16)
    return np.concatenate([high, low], axis=1)


def rim_masks():
    slot = lax.broadcasted_iota(jnp.int32, (RIM, LANES), 0)
    lane = lax.broadcasted_iota(jnp.int32, (RIM, LANES), 1)
    return slot, lane


def as_mask(condition):
    return jnp.where(condition, 1.0, 0.0).astype(jnp.bfloat16)


def rim_of(before, after, first_slot):
    slot, lane = rim_masks()
    slot = slot - first_slot
    pick_before = as_mask((slot >= 0) & (slot < HALO) & (lane == LANES - HALO + slot))
    pick_after = as_mask((slot >= HALO) & (slot < 2 * HALO) & (lane == slot - HALO))
    across = (((1,), (1,)), ((), ()))
    rim = lax.dot_general(pick_before, before, across, preferred_element_type=jnp.float32)
    return rim + lax.dot_general(pick_after, after, across, preferred_element_type=jnp.float32)


def rest_pack_kernel(groups, members, piece, cells, near, *outs):
    boxes, parts, sources, block = cells.shape
    rows = boxes * parts * sources
    tiles = piece // LANES
    wide_at = lax.axis_index("wide")
    group_at, member_at = wide_at // members, wide_at % members

    def tile(ref, at):
        return ref[:, :, :, pl.ds(pl.multiple_of(at, LANES), LANES)].reshape(rows, LANES)

    def rim_at(ref, first):
        return rim_of(tile(ref, jnp.maximum(first - LANES, 0)), tile(ref, jnp.minimum(first + piece, block - LANES)), 0)

    edges = outs[-1]
    for half, ref in enumerate((cells, near)):
        rim = rim_of(tile(ref, block - LANES), tile(ref, 0), 2 * HALO)
        edges[half * RIM : (half + 1) * RIM, :] = rim.astype(jnp.bfloat16)
    for part in range(1, groups):
        for swap in range(2, members, 2):
            out, base = outs[(part - 1) * (members // 2 - 1) + swap // 2 - 1], 0
            target = member_at ^ swap
            first = ((group_at ^ (groups - 1 - part)) * members + target) * piece
            for ref in (cells, near):
                for index in range(tiles):
                    out[base : base + rows, :] = tile(ref, first + index * LANES)
                    base += rows
                out[base : base + RIM, :] = rim_at(ref, first).astype(jnp.bfloat16)
                base += RIM
                if part == 1:
                    rim = rim_at(ref, ((group_at ^ (groups - 1)) * members + target) * piece)
                    out[base : base + RIM, :] = rim.astype(jnp.bfloat16)
                    base += RIM


def turned(cycles):
    half = math.pi * (cycles - jnp.floor(cycles + 0.5))
    square = half * half
    sine, cosine = jnp.zeros_like(half), jnp.zeros_like(half)
    for order in range(13, 0, -2):
        sine = sine * square + (-1) ** (order // 2) / math.factorial(order)
        cosine = cosine * square + (-1) ** (order // 2) / math.factorial(order - 1)
    sine = sine * half
    return 1.0 - 2.0 * sine * sine, 2.0 * sine * cosine


def axes_kernel(groups, members, piece, sample_count, cosines, sines, center_dirs):
    wide_at = lax.axis_index("wide")
    group_at, member_at = wide_at // members, wide_at % members
    rows = 4 * piece // LANES
    half_rows = sample_count // LANES // lax.axis_size("narrow")
    row = lax.broadcasted_iota(jnp.int32, (rows, LANES), 0)
    lane = lax.broadcasted_iota(jnp.int32, (rows, LANES), 1)
    cos_azimuth, sin_azimuth = turned((((row * LANES + lane) & 255).astype(jnp.float32) + 0.5) / 256.0)
    for step in range(groups):
        first_row = lax.axis_index("narrow") * half_rows + ((group_at ^ step) * members + member_at) * rows
        ring = ((first_row + row) * LANES + lane) >> 8
        dir_z, sin_polar = turned((ring.astype(jnp.float32) + 0.5) / (2 * (sample_count // 256)))
        for axis, direction in enumerate((sin_polar * cos_azimuth, sin_polar * sin_azimuth, dir_z)):
            cosines[step, axis], sines[step, axis] = turned(2.0 * direction)
            if step == 0:
                center_dirs[axis] = direction


def prep_kernel(
    groups, members, boxes, piece, parent_of, octant_of, center, starts, axis_cos, axis_sin, center_dirs,
    cosines, sines, center_cos, center_sin, excess, held, sems,
):
    wide_at = lax.axis_index("wide")
    group_at, member_at = wide_at // members, wide_at % members
    rows = 4 * piece // LANES
    half_rows = starts.shape[0] // lax.axis_size("narrow")
    row = lax.broadcasted_iota(jnp.int32, (rows, LANES), 0)
    lane = lax.broadcasted_iota(jnp.int32, (rows, LANES), 1)
    first_rows = [
        pl.multiple_of(lax.axis_index("narrow") * half_rows + ((group_at ^ step) * members + member_at) * rows, 8)
        for step in range(groups)
    ]
    copies = [
        pltpu.make_async_copy(starts.at[pl.ds(first_rows[step], rows)], held.at[step], sems.at[step]) for step in range(groups)
    ]
    for copy in copies:
        copy.start()
    scale = 1.0 / math.sqrt(center.shape[0])
    for step in range(groups):
        parent = parent_of[(group_at ^ step) * members * boxes]
        turns = sum(center[parent, axis] * center_dirs[axis] for axis in range(3))
        turn_cos, turn_sin = turned(turns)
        center_cos[step] = turn_cos * scale
        center_sin[step] = turn_sin * scale
    for step in range(groups):
        (cos_x, cos_y, cos_z), (sin_x, sin_y, sin_z) = ([table[step, axis] for axis in range(3)] for table in (axis_cos, axis_sin))
        both_cos, both_sin, sin_cos, cos_sin = cos_x * cos_y, sin_x * sin_y, sin_x * cos_y, cos_x * sin_y
        for swap in range(members):
            for box in range(boxes):
                slot = (group_at * members + (member_at ^ swap)) * boxes + box
                octant = octant_of[slot]
                live = jnp.where(parent_of[slot] >= 0, 1.0, 0.0)
                sign_x = ((octant & 1) * 2 - 1).astype(jnp.float32)
                sign_y = (((octant >> 1) & 1) * 2 - 1).astype(jnp.float32)
                sign_z = ((octant >> 2) * 2 - 1).astype(jnp.float32)
                real = both_cos - (sign_x * sign_y) * both_sin
                imag = sign_x * sin_cos + sign_y * cos_sin
                turn_cos, turn_sin = live * cos_z, (live * sign_z) * sin_z
                cosines[step, swap * boxes + box] = real * turn_cos - imag * turn_sin
                sines[step, swap * boxes + box] = real * turn_sin + imag * turn_cos
    for step in range(groups):
        copies[step].wait()
        child = ((first_rows[step] + row) * LANES + lane) >> 2
        excess[step] = (child - 2 - held[step]).astype(jnp.float32)


def columns_of(windows):
    return [2 * window + half for window in windows for half in range(2)]


def combine_kernel(jobs, members, boxes, sources, tiles, count, *refs):
    data = refs[:count]
    cosines, sines, excess, band_zero, band_one = refs[count : count + 5]
    *outs, spread, total = refs[count + 5 :]
    for (step, *job), out in zip(jobs, outs):
        combine(
            step, *job, members, boxes, sources, tiles, data, cosines.at[step], sines.at[step], excess.at[step],
            band_zero, band_one, out, spread, total,
        )


def combine(
    step, windows, places, rims, members, boxes, sources, tiles, data, cosines, sines, excess, band_zero, band_one, out, spread, total
):
    rows = boxes * 2 * sources
    block = data[0].shape[3]
    wide_at = lax.axis_index("wide")
    last = lax.axis_size("wide") - 1
    at = ((wide_at // members) ^ step) * members + wide_at % members
    first = at * (tiles * LANES)

    def local(ref, lane):
        return ref[:, :, :, pl.ds(pl.multiple_of(lane, LANES), LANES)].reshape(rows, LANES)

    def tile(index):
        if index < 0 or index >= tiles:
            return rim_tile
        found = [local(data[member], first + index * LANES) for member in range(2)]
        for which, base in places:
            ref = data[which]
            if len(ref.shape) == 4:
                found.append(ref[:, :, :, index * LANES : (index + 1) * LANES].reshape(rows, LANES))
            else:
                found.append(ref[base + index * rows : base + (index + 1) * rows, :])
        return jnp.concatenate(found, axis=0)

    if rims is not None:
        slot, lane = rim_masks()
        from_other = slot >= 2 * HALO
        side = jnp.where(from_other, slot - 2 * HALO, slot)
        outer = ((side < HALO) & (at == 0)) | ((side >= HALO) & (at == last))
        keep = (outer == from_other) & (slot < 4 * HALO)
        place = as_mask(
            ((side < HALO) & (lane == LANES - HALO + side)) | ((side >= HALO) & (side < 2 * HALO) & (lane == side - HALO))
        )
        found = []
        for inner, (other, other_row) in rims:
            outside = data[other][other_row : other_row + RIM, :].astype(jnp.float32)
            if inner is None:
                inside = jnp.zeros((RIM, LANES), jnp.float32)
            else:
                inside = data[inner[0]][inner[1] : inner[1] + RIM, :].astype(jnp.float32)
            found.append(jnp.where(keep, jnp.where(from_other, outside, inside), 0.0).astype(jnp.bfloat16))
        rim = jnp.concatenate(found, axis=1)
        rim_tile = lax.dot_general(rim, place, (((0,), (0,)), ((), ())), preferred_element_type=jnp.float32)
        lane = lax.broadcasted_iota(jnp.int32, (rows, LANES), 1)
        from_before = (lane >= LANES - HALO) & (at != 0)
        from_after = (lane < HALO) & (at != last)
        near = []
        for member in range(2):
            before = local(data[member], jnp.maximum(first - LANES, 0)).astype(jnp.float32)
            after = local(data[member], jnp.minimum(first + tiles * LANES, block - LANES)).astype(jnp.float32)
            near.append(jnp.where(from_before, before, jnp.where(from_after, after, 0.0)))
        near = jnp.concatenate(near, axis=0)
        rim_tile = jnp.concatenate([rim_tile[: 2 * rows] + near, rim_tile[2 * rows :]], axis=0).astype(jnp.bfloat16)

    def window_of(window):
        cut = 32 if window % 2 else 96
        left, right = tile((window - 1 + window % 2) // 2), tile((window + 1) // 2)
        cells = jnp.concatenate([left[:, cut:], right[:, :cut]], axis=1)
        return jnp.concatenate([cells, cells], axis=1)

    columns = columns_of(windows)
    width = len(columns)
    whole = width == 4 * tiles

    def spread_window(turn):
        bands = []
        for half, column in enumerate(columns[2 * turn : 2 * turn + 2]):
            which = jnp.broadcast_to(excess[column : column + 1, :], (16, LANES)).astype(jnp.bfloat16)
            which = jnp.concatenate([which] * (band_zero.shape[0] // 16), axis=0)
            lanes = slice(half * LANES, (half + 1) * LANES)
            bands.append(band_zero[:, lanes] * (1 - which) + band_one[:, lanes] * which)
        spread[turn % 2] = jnp.dot(
            window_of(windows[turn]), jnp.concatenate(bands, axis=1), preferred_element_type=jnp.float32
        )

    def sum_window(turn):
        for half, column in enumerate(columns[2 * turn : 2 * turn + 2]):
            lanes = slice(half * LANES, (half + 1) * LANES)
            real_sum = jnp.zeros((sources, LANES), jnp.float32)
            imag_sum = jnp.zeros((sources, LANES), jnp.float32)
            for child in range(members * boxes):
                start = child * 2 * sources
                real = spread[turn % 2, start : start + sources, lanes].astype(jnp.bfloat16).astype(jnp.float32)
                imag = spread[turn % 2, start + sources : start + 2 * sources, lanes]
                imag = imag.astype(jnp.bfloat16).astype(jnp.float32)
                cosine = cosines[child, column : column + 1, :]
                sine = sines[child, column : column + 1, :]
                real_sum = real_sum + (cosine * real - sine * imag)
                imag_sum = imag_sum + (sine * real + cosine * imag)
            if whole:
                total[pl.ds(column, sources, stride=width), :] = real_sum
                total[pl.ds(sources * width + column, sources, stride=width), :] = imag_sum
            else:
                at_row = (2 * turn + half) * 2 * sources
                out[at_row : at_row + sources, :] = real_sum.astype(out.dtype)
                out[at_row + sources : at_row + 2 * sources, :] = imag_sum.astype(out.dtype)

    for turn in range(len(windows) + 1):
        if turn < len(windows):
            spread_window(turn)
        if turn:
            sum_window(turn - 1)
    if whole:
        out[: 2 * sources * width, :] = total[: 2 * sources * width, :].astype(out.dtype)
    if out.shape[0] > 2 * sources * width:
        out[2 * sources * width :, :] = jnp.zeros((out.shape[0] - 2 * sources * width, LANES), out.dtype)


def place_columns(arrived, columns, sources, rows, cosines, sines, pattern, far):
    for index, column in enumerate(columns):
        real, imag = (
            arrived[pl.ds((2 * index + half) * sources, sources), :].astype(jnp.float32) for half in range(2)
        )
        at = pl.ds(column, sources, stride=rows)
        pattern[0, at, :] = real
        pattern[1, at, :] = imag
        cosine, sine = cosines[column : column + 1, :], sines[column : column + 1, :]
        far[0, at, :] += cosine * real - sine * imag
        far[1, at, :] += sine * real + cosine * imag


def finish_ahead_kernel(
    own_step, early_step, columns, members, boxes, sources, rows,
    parent_of, own, early, center_cos, center_sin, parent_out, far_out, early_out,
):
    name = parent_of[((lax.axis_index("wide") // members) ^ own_step) * members * boxes]
    cosine, sine = center_cos[own_step], center_sin[own_step]
    for source in range(sources):
        at = pl.ds(source * rows, rows)
        real, imag = (own[pl.ds((half * sources + source) * rows, rows), :] for half in range(2))
        parent_out[name, 0, at, :] = real
        parent_out[name, 1, at, :] = imag
        far_out[0, at, :] = cosine * real - sine * imag
        far_out[1, at, :] = sine * real + cosine * imag
    place_columns(
        early, columns, sources, rows, center_cos.at[early_step], center_sin.at[early_step], early_out, far_out
    )


def finish_kernel(steps, early_step, columns, members, boxes, sources, rows, parts, parent_of, *refs):
    whole, refs = refs[: len(steps)], refs[len(steps) :]
    late, early, center_cos, center_sin, far_in, _, parent_out, far_out, names, held, far_held, name_sem, sems = refs
    name_copy = pltpu.make_async_copy(parent_of, names, name_sem)
    name_copy.start()
    group_at = lax.axis_index("wide") // members
    copies = []

    def send(source, target):
        copies.append(pltpu.make_async_copy(source, target, sems.at[len(copies)]))
        copies[-1].start()

    last = len(steps)
    held[last] = early[...]
    far_held[...] = far_in[...]
    place_columns(
        late, columns, sources, rows, center_cos.at[early_step], center_sin.at[early_step], held.at[last], far_held
    )
    name_copy.wait()
    places = [names[(group_at ^ step) * members * boxes] for step in (*steps, early_step)]
    send(held.at[last], parent_out.at[places[last]])
    each = sources // parts
    for part in range(parts):
        for source in range(part * each, (part + 1) * each):
            at = pl.ds(source * rows, rows)
            far_real, far_imag = far_held[0, at, :], far_held[1, at, :]
            for index, step in enumerate(steps):
                real, imag = (
                    whole[index][pl.ds((half * sources + source) * rows, rows), :].astype(jnp.float32) for half in range(2)
                )
                cosine, sine = center_cos[step], center_sin[step]
                held[index, 0, at, :] = real
                held[index, 1, at, :] = imag
                far_real = far_real + (cosine * real - sine * imag)
                far_imag = far_imag + (sine * real + cosine * imag)
            far_held[0, at, :] = far_real
            far_held[1, at, :] = far_imag
        at = pl.ds(part * each * rows, each * rows)
        for index in range(last):
            send(held.at[index, :, at], parent_out.at[places[index], :, at])
        send(far_held.at[:, at], far_out.at[:, at])
    for copy in copies:
        copy.wait()


def grouped(child_pattern, child_parent, child_octant, parent_center, stencil_start, members):
    n_wide = lax.axis_size("wide")
    boxes, _, sources, block = child_pattern.shape
    groups = n_wide // members
    piece = block // n_wide
    tiles = piece // LANES
    rows = boxes * 2 * sources
    out_rows = 4 * tiles
    parents = parent_center.shape[0]
    vmem = pl.BlockSpec(memory_space=pltpu.VMEM)
    smem = pl.BlockSpec(memory_space=pltpu.SMEM)
    hbm = pl.BlockSpec(memory_space=pltpu.HBM)
    limit = pltpu.CompilerParams(vmem_limit_bytes=16 * 1024 * 1024)

    def cost(micros):
        return pl.CostEstimate(flops=int(micros * 1e9), bytes_accessed=int(micros * 3.6e6) + 1, transcendentals=0)


    def bf16(*shape):
        return jax.ShapeDtypeStruct(shape, jnp.bfloat16)

    def f32(*shape):
        return jax.ShapeDtypeStruct(shape, jnp.float32)

    def swap_with(array, step):
        return lax.ppermute(array, "wide", [(i, i ^ step) for i in range(n_wide)])

    def tie(*arrays):
        return lax.optimization_barrier(arrays)

    far = members - 2
    wide_at = lax.axis_index("wide")
    heads = []
    for swap in range(2, members):
        first = (wide_at ^ ((groups - 1) * members + swap)) * piece
        heads.append(lax.dynamic_slice_in_dim(child_pattern, first, piece, 3))
    near = swap_with(child_pattern, 1)
    heads = [swap_with(head, swap + 2) for swap, head in enumerate(heads)]

    def other_half(array, step):
        pairs = [(i * 2 + n, (i ^ step) * 2 + 1 - n) for i in range(n_wide) for n in range(2)]
        return lax.ppermute(array, ("wide", "narrow"), pairs)

    axes = pl.pallas_call(
        functools.partial(axes_kernel, groups, members, piece, stencil_start.shape[0]),
        out_shape=[f32(groups, 3, out_rows, LANES)] * 2 + [f32(3, out_rows, LANES)],
        out_specs=[vmem] * 3,
        compiler_params=limit,
        cost_estimate=cost(1),
        name="axes",
    )()
    tables = pl.pallas_call(
        functools.partial(prep_kernel, groups, members, boxes, piece),
        out_shape=[
            f32(groups, members * boxes, out_rows, LANES),
            f32(groups, members * boxes, out_rows, LANES),
            f32(parents, out_rows, LANES),
            f32(parents, out_rows, LANES),
            f32(groups, out_rows, LANES),
        ],
        in_specs=[smem, smem, smem, hbm] + [vmem] * 3,
        out_specs=[vmem] * 5,
        scratch_shapes=[pltpu.VMEM((groups, out_rows, LANES), jnp.int32), pltpu.SemaphoreType.DMA((groups,))],
        compiler_params=limit,
            cost_estimate=cost(1),
        name="prep",
    )(child_parent, child_octant, parent_center, stencil_start.reshape(-1, LANES), *axes)
    cosines, sines, center_cos, center_sin, excess = tables
    full = tiles * rows + RIM
    pairs = members // 2 - 1
    *sends, edges = pl.pallas_call(
        functools.partial(rest_pack_kernel, groups, members, piece),
        out_shape=[
            bf16(2 * (full + (RIM if part == 1 else 0)), LANES) for part in range(1, groups) for _ in range(pairs)
        ]
        + [bf16(2 * RIM, LANES)],
        in_specs=[vmem] * 2,
        out_specs=[vmem] * ((groups - 1) * pairs + 1),
        compiler_params=limit,
        cost_estimate=cost(1),
        name="pack",
    )(child_pattern, near)
    common = [other_half(edges, 2 * pair) for pair in range(pairs + 1)]
    bands = stencil_tables(LANES, 2 * LANES)

    top = groups - 1

    def sums_of(jobs, data, dtype, micros):
        shapes = [
            jax.ShapeDtypeStruct((2 * sources * len(columns_of(job[1])) + (RIM if job[0] == top - 1 else 0), LANES), dtype)
            for job in jobs
        ]
        inputs = [*data, cosines, sines, excess, bands[0], bands[1]]
        return pl.pallas_call(
            functools.partial(combine_kernel, jobs, members, boxes, sources, tiles, len(data)),
            out_shape=shapes,
            in_specs=[vmem] * len(inputs),
            out_specs=[vmem] * len(shapes),
            scratch_shapes=[
                pltpu.VMEM((2, members * rows, 2 * LANES), jnp.float32),
                pltpu.VMEM((2 * sources * out_rows, LANES), jnp.float32),
            ],
            compiler_params=limit,
            cost_estimate=cost(micros),
            name="combine",
        )(*inputs)

    inner = list(range(1, 2 * tiles - 1))
    outer = [0, 2 * tiles - 1]
    every = list(range(2 * tiles))
    locals_ = [child_pattern, near]
    first_data = locals_ + heads
    first_places = [(2 + member, 0) for member in range(far)]
    (total,) = sums_of([(top, inner, first_places, None)], first_data, jnp.bfloat16, 5)
    early_sends = sends[pairs : 2 * pairs]
    *early_sends, total = tie(*early_sends, total)
    sends[pairs : 2 * pairs] = early_sends
    done = [swap_with(total, top * members)]
    arrived = {}
    for part in range(1, groups):
        step = top - part
        sent = sends[(part - 1) * pairs : part * pairs]
        if part > 1:
            totals = list(sums_of(jobs, data, jnp.bfloat16, 30 if part == 2 else 2))
            if part < groups - 1:
                tied = tie(*sends[part * pairs : (part + 1) * pairs], *totals)
                sends[part * pairs : (part + 1) * pairs], totals = tied[:pairs], list(tied[pairs:])
            arrived[step + 1] = swap_with(totals[0], (step + 1) * members)
            if part == 2:
                done.append(swap_with(totals[1], top * members))
        got = [swap_with(array, 2 * pair + 2) for pair, array in enumerate(sent)]
        length = full + (RIM if part == 1 else 0)
        places = [(2 + member // 2, member % 2 * length) for member in range(far)]
        data = locals_ + got + common
        shift = 2 + pairs
        edge_at = [(shift + member // 2, member % 2 * RIM) for member in range(members)]
        rims = [None, None] + [(which, row + tiles * rows) for which, row in places]
        jobs = [(step, every, places, list(zip(rims, edge_at)))]
        if part == 1:
            rims = [None, None] + [(which, row + full) for which, row in places]
            outer_places = [(len(data) + member, 0) for member in range(far)]
            jobs.append((top, outer, outer_places, list(zip(rims, edge_at))))
            data = data + heads
    data[0], done[0] = tie(data[0], done[0])
    (arrived[0],) = sums_of(jobs, data, jnp.float32, 1)
    done = [(top, columns_of(inner), done[0]), (top, columns_of(outer), done[1])]
    held = arrived
    whole = f32(2, sources * out_rows, LANES)
    (_, early_columns, early_array), (_, late_columns, late_array) = done
    parent_pattern, far_field, early_pattern = pl.pallas_call(
        functools.partial(finish_ahead_kernel, 0, top, early_columns, members, boxes, sources, out_rows),
        out_shape=[f32(parents, *whole.shape), whole, whole],
        in_specs=[smem] + [vmem] * 4,
        out_specs=[vmem] * 3,
        compiler_params=limit,
        cost_estimate=cost(0),
        name="finish_ahead",
    )(child_parent, held[0], early_array, center_cos, center_sin)
    steps = sorted((step for step in held if step), reverse=True)
    parts = 4
    parent_pattern, far_field = pl.pallas_call(
        functools.partial(finish_kernel, steps, top, late_columns, members, boxes, sources, out_rows, parts),
        out_shape=[f32(parents, *whole.shape), whole],
        in_specs=[hbm] + [vmem] * (len(steps) + 5) + [hbm],
        out_specs=[hbm, hbm],
        input_output_aliases={len(steps) + 6: 0},
        scratch_shapes=[
            pltpu.SMEM(child_parent.shape, jnp.int32),
            pltpu.VMEM((len(steps) + 1, *whole.shape), jnp.float32),
            pltpu.VMEM(whole.shape, jnp.float32),
            pltpu.SemaphoreType.DMA,
            pltpu.SemaphoreType.DMA((1 + parts * (len(steps) + 1),)),
        ],
        compiler_params=limit,
        cost_estimate=cost(30),
        name="finish_last",
    )(child_parent, *[held[step] for step in steps], late_array, early_pattern, center_cos, center_sin, far_field, parent_pattern)
    return (
        parent_pattern.reshape(parents, 2, sources, 1, 4 * piece),
        far_field.reshape(2, sources, 1, 4 * piece),
    )


def power_of_two(number):
    return number > 0 and number & (number - 1) == 0


def per_device(child_pattern, child_parent, child_octant, parent_center, stencil_start):
    n_wide, n_narrow = lax.axis_size("wide"), lax.axis_size("narrow")
    boxes, _, sources, block = child_pattern.shape
    parents = parent_center.shape[0]
    run = child_parent.shape[0] // parents
    if run % boxes == 0 and block % n_wide == 0:
        members = run // boxes
        fits = (
            n_narrow == 2
            and n_wide == members * parents
            and power_of_two(members)
            and power_of_two(parents)
            and members >= 4
            and parents >= 4
            and block // n_wide % LANES == 0
            and block // n_wide // LANES >= 3
            and boxes * 2 * sources == LANES
            and sources % 16 == 0
            and stencil_start.shape[0] == 4 * block * n_narrow
        )
        if fits:
            return grouped(child_pattern, child_parent, child_octant, parent_center, stencil_start, members)
    return exchanged(child_pattern, child_parent, child_octant, parent_center, stencil_start)


def solution(mesh):
    in_specs = (P("wide", None, None, "narrow"), P(), P(), P(), P())
    out_specs = (P(None, None, None, "narrow", "wide"), P(None, None, "narrow", "wide"))
    return jax.shard_map(
        per_device, mesh=mesh, in_specs=in_specs, out_specs=out_specs, check_vma=False
    )
```

```python
import functools
import math

import jax
import jax.numpy as jnp
import ml_dtypes
import numpy as np
from jax import lax
from jax.experimental import pallas as pl
from jax.experimental.pallas import tpu as pltpu
from jax.sharding import PartitionSpec as P

K2 = 65536


def with_halo(cells, sides, width):
    for axis, dim in sides:
        count = lax.axis_size(axis)
        head = lax.slice_in_dim(cells, 0, width, axis=dim)
        tail = lax.slice_in_dim(cells, cells.shape[dim] - width, cells.shape[dim], axis=dim)
        cells = jnp.concatenate(
            [
                lax.ppermute(tail, axis, [(i, (i + 1) % count) for i in range(count)]),
                cells,
                lax.ppermute(head, axis, [((i + 1) % count, i) for i in range(count)]),
            ],
            axis=dim,
        )
    return cells


def lagrange_taps(starts, first_out):
    sample_count = starts.shape[0]
    sample = first_out + jnp.arange(sample_count, dtype=jnp.int32)
    excess = sample // 4 - 2 - starts
    offset_u = (sample % 4).astype(jnp.float32) * 0.25 + 2.125 + excess.astype(jnp.float32)
    basis = []
    for node in range(6):
        value = jnp.ones_like(offset_u)
        for other in range(6):
            if other != node:
                value = value * (offset_u - other) / (node - other)
        basis.append(value)
    zeros = jnp.zeros_like(offset_u)
    stacked = []
    for offset in range(7):
        lower = basis[offset - 1] if offset >= 1 else zeros
        upper = basis[offset] if offset <= 5 else zeros
        stacked.append(jnp.where(excess == 0, lower, upper))
    return jnp.stack(stacked).reshape(7, sample_count // 4, 4)


def interpolate(window, tap_weights):
    block_len = tap_weights.shape[1]
    leading = window.shape[:-1]
    flat_rows = window.reshape((-1, window.shape[-1]))
    row_count = flat_rows.shape[0]
    if block_len % 64 == 0 and block_len > 64:
        group = 64
    else:
        group = block_len
    blocks = block_len // group
    taps = tap_weights.reshape(7, blocks, 4 * group)
    if blocks == 1:
        band_rows = flat_rows.shape[1]
        paired = flat_rows[:, None, :]
    else:
        band_rows = 2 * group
        extended = jnp.pad(flat_rows, ((0, 0), (0, (blocks + 1) * group - flat_rows.shape[1])))
        split_rows = extended.reshape(row_count, blocks + 1, group)
        paired = jnp.concatenate([split_rows[:, :-1], split_rows[:, 1:]], axis=2)
    column = jnp.arange(band_rows, dtype=jnp.int32)[None, :, None]
    target = (jnp.arange(4 * group, dtype=jnp.int32) // 4)[None, None, :]
    offsets = jnp.arange(7, dtype=jnp.int32)[:, None, None]
    onehot = (column == target + offsets).astype(jnp.float32)
    band = jnp.einsum("kcj,kbj->bcj", onehot, taps, precision=lax.Precision.HIGHEST)
    total = jnp.einsum(
        "rbc,bcj->rbj", paired.astype(jnp.float32), band, precision=lax.Precision.HIGHEST
    )
    return total.reshape(leading + (4 * block_len,)).astype(jnp.bfloat16)


def directions(first_out, sample_count):
    sample = first_out + jnp.arange(sample_count, dtype=jnp.int32)
    cycles = K2 // 256
    azimuth = 2.0 * math.pi * ((sample % 256).astype(jnp.float32) + 0.5) / 256.0
    polar = math.pi * ((sample // 256).astype(jnp.float32) + 0.5) / cycles
    return (jnp.sin(polar) * jnp.cos(azimuth), jnp.sin(polar) * jnp.sin(azimuth), jnp.cos(polar))


def child_phase(octant, dir_x, dir_y, dir_z):
    sign_x = (octant % 2 * 2 - 1).astype(jnp.float32)
    sign_y = (octant // 2 % 2 * 2 - 1).astype(jnp.float32)
    sign_z = (octant // 4 * 2 - 1).astype(jnp.float32)
    return (
        2.0
        * math.pi
        * 2.0
        * (sign_x[:, None] * dir_x + sign_y[:, None] * dir_y + sign_z[:, None] * dir_z)
    )


def shift_children(pattern, octant, dir_x, dir_y, dir_z):
    angle = child_phase(octant, dir_x, dir_y, dir_z)
    cosine = jnp.cos(angle)[:, None, :]
    sine_part = jnp.sin(angle)[:, None, :]
    real_part = pattern[:, 0].astype(jnp.float32)
    imag_part = pattern[:, 1].astype(jnp.float32)
    return jnp.stack(
        [cosine * real_part - sine_part * imag_part, sine_part * real_part + cosine * imag_part],
        axis=1,
    )


def exchanged(child_pattern, child_parent, child_octant, parent_center, stencil_start):
    n_wide = lax.axis_size("wide")
    box_count, _, sources, block_one = child_pattern.shape
    block_two = 4 * block_one
    piece_len = block_one // n_wide
    narrow_at = lax.axis_index("narrow")
    wide_at = lax.axis_index("wide")
    out_first = narrow_at * block_two + wide_at * (4 * piece_len)
    parent_count = parent_center.shape[0]
    parent_ids = jnp.arange(parent_count, dtype=jnp.int32)
    dir_x, dir_y, dir_z = directions(out_first, 4 * piece_len)
    padded = with_halo(child_pattern, (("narrow", 3),), 3)
    shape_pieces = (box_count, 2, sources, n_wide, piece_len)
    left_rim = padded[..., 0:block_one].reshape(shape_pieces)[..., :3]
    middle = padded[..., 3 : 3 + block_one].reshape(shape_pieces)
    right_rim = padded[..., 6 : 6 + block_one].reshape(shape_pieces)[..., piece_len - 3 :]
    windows = jnp.concatenate([left_rim, middle, right_rim], axis=-1)
    starts = lax.dynamic_slice_in_dim(stencil_start, out_first, 4 * piece_len)
    tap_weights = lagrange_taps(starts, out_first)
    gathered = interpolate(
        lax.all_to_all(windows, "wide", split_axis=3, concat_axis=0, tiled=True)[:, :, :, 0, :],
        tap_weights,
    )
    shifted = shift_children(gathered, child_octant, dir_x, dir_y, dir_z)
    selector = (child_parent[:, None] == parent_ids[None, :]).astype(jnp.float32)
    parents_total = jnp.einsum("bp,bcrj->pcrj", selector, shifted, precision=lax.Precision.HIGHEST)
    center_angle = (
        2.0
        * math.pi
        * (
            parent_center[:, 0:1] * dir_x
            + parent_center[:, 1:2] * dir_y
            + parent_center[:, 2:3] * dir_z
        )
    )
    center_cos = jnp.cos(center_angle)
    center_sin = jnp.sin(center_angle)
    real_sum = jnp.einsum(
        "pj,prj->rj", center_cos, parents_total[:, 0], precision=lax.Precision.HIGHEST
    ) - jnp.einsum("pj,prj->rj", center_sin, parents_total[:, 1], precision=lax.Precision.HIGHEST)
    imag_sum = jnp.einsum(
        "pj,prj->rj", center_sin, parents_total[:, 0], precision=lax.Precision.HIGHEST
    ) + jnp.einsum("pj,prj->rj", center_cos, parents_total[:, 1], precision=lax.Precision.HIGHEST)
    far_field = jnp.stack([real_sum, imag_sum]) / math.sqrt(parent_count)
    parent_pattern = parents_total[:, :, :, None, :]
    return (parent_pattern, far_field[:, :, None, :])


LANES = 128
HALO = 3
RIM = 16


def stencil_tables(window, columns):
    tables = np.zeros((2, window, columns), np.float32)
    for excess in range(2):
        for column in range(columns):
            offset_u = np.float32((column % 4) * 0.25 + 2.125 + excess)
            first = window // 4 + column // 4 - 2 - excess
            for node in range(6):
                value = np.float32(1.0)
                for other in range(6):
                    if other != node:
                        value = np.float32(
                            value * np.float32(np.float32(offset_u - np.float32(other)) / np.float32(node - other))
                        )
                tables[excess, first + node, column] = value
    high = tables.astype(ml_dtypes.bfloat16)
    low = (tables - high.astype(np.float32)).astype(ml_dtypes.bfloat16)
    return np.concatenate([high, low], axis=1)


def shift_of(step, groups):
    half = groups // 2
    return ([0] + [half, *(shift for shift in range(1, groups) if shift != half)][::-1])[step]


def group_after(group, step, groups):
    return (group + shift_of(step, groups)) & (groups - 1)


def group_before(group, step, groups):
    return (group + groups - shift_of(step, groups)) & (groups - 1)


def rim_masks():
    slot = lax.broadcasted_iota(jnp.int32, (RIM, LANES), 0)
    lane = lax.broadcasted_iota(jnp.int32, (RIM, LANES), 1)
    return slot, lane


def as_mask(condition):
    return jnp.where(condition, 1.0, 0.0).astype(jnp.bfloat16)


def rim_of(before, after, first_slot):
    slot, lane = rim_masks()
    slot = slot - first_slot
    pick_before = as_mask((slot >= 0) & (slot < HALO) & (lane == LANES - HALO + slot))
    pick_after = as_mask((slot >= HALO) & (slot < 2 * HALO) & (lane == slot - HALO))
    across = (((1,), (1,)), ((), ()))
    rim = lax.dot_general(pick_before, before, across, preferred_element_type=jnp.float32)
    return rim + lax.dot_general(pick_after, after, across, preferred_element_type=jnp.float32)


def rest_pack_kernel(groups, members, piece, cells, near, *outs):
    boxes, parts, sources, block = cells.shape
    rows = boxes * parts * sources
    tiles = piece // LANES
    wide_at = lax.axis_index("wide")
    group_at, member_at = wide_at // members, wide_at % members

    def tile(ref, at):
        return ref[:, :, :, pl.ds(pl.multiple_of(at, LANES), LANES)].reshape(rows, LANES)

    def rim_at(ref, first):
        return rim_of(tile(ref, jnp.maximum(first - LANES, 0)), tile(ref, jnp.minimum(first + piece, block - LANES)), 0)

    edges = outs[-1]
    for half, ref in enumerate((cells, near)):
        rim = rim_of(tile(ref, block - LANES), tile(ref, 0), 2 * HALO)
        edges[half * RIM : (half + 1) * RIM, :] = rim.astype(jnp.bfloat16)
    for part in range(1, groups):
        for swap in range(2, members, 2):
            out, base = outs[(part - 1) * (members // 2 - 1) + swap // 2 - 1], 0
            target = member_at ^ swap
            first = (group_after(group_at, groups - 1 - part, groups) * members + target) * piece
            for ref in (cells, near):
                for index in range(tiles):
                    out[base : base + rows, :] = tile(ref, first + index * LANES)
                    base += rows
                out[base : base + RIM, :] = rim_at(ref, first).astype(jnp.bfloat16)
                base += RIM
                if part == 1:
                    rim = rim_at(ref, (group_after(group_at, groups - 1, groups) * members + target) * piece)
                    out[base : base + RIM, :] = rim.astype(jnp.bfloat16)
                    base += RIM


def turned(cycles):
    half = math.pi * (cycles - jnp.floor(cycles + 0.5))
    square = half * half
    sine, cosine = jnp.zeros_like(half), jnp.zeros_like(half)
    for order in range(13, 0, -2):
        sine = sine * square + (-1) ** (order // 2) / math.factorial(order)
        cosine = cosine * square + (-1) ** (order // 2) / math.factorial(order - 1)
    sine = sine * half
    return 1.0 - 2.0 * sine * sine, 2.0 * sine * cosine


def axes_kernel(groups, members, piece, sample_count, cosines, sines, center_dirs):
    wide_at = lax.axis_index("wide")
    group_at, member_at = wide_at // members, wide_at % members
    rows = 4 * piece // LANES
    half_rows = sample_count // LANES // lax.axis_size("narrow")
    row = lax.broadcasted_iota(jnp.int32, (rows, LANES), 0)
    lane = lax.broadcasted_iota(jnp.int32, (rows, LANES), 1)
    cos_azimuth, sin_azimuth = turned((((row * LANES + lane) & 255).astype(jnp.float32) + 0.5) / 256.0)
    for step in range(groups):
        at = group_after(group_at, step, groups) * members + member_at
        first_row = lax.axis_index("narrow") * half_rows + at * rows
        ring = ((first_row + row) * LANES + lane) >> 8
        dir_z, sin_polar = turned((ring.astype(jnp.float32) + 0.5) / (2 * (sample_count // 256)))
        for axis, direction in enumerate((sin_polar * cos_azimuth, sin_polar * sin_azimuth, dir_z)):
            cosines[step, axis], sines[step, axis] = turned(2.0 * direction)
            if step == 0:
                center_dirs[axis] = direction


def prep_kernel(
    groups, members, boxes, piece, parent_of, octant_of, center, starts, axis_cos, axis_sin, center_dirs,
    cosines, sines, center_cos, center_sin, excess, held, sems,
):
    wide_at = lax.axis_index("wide")
    group_at, member_at = wide_at // members, wide_at % members
    rows = 4 * piece // LANES
    half_rows = starts.shape[0] // lax.axis_size("narrow")
    row = lax.broadcasted_iota(jnp.int32, (rows, LANES), 0)
    lane = lax.broadcasted_iota(jnp.int32, (rows, LANES), 1)
    first_rows = [
        pl.multiple_of(
            lax.axis_index("narrow") * half_rows + (group_after(group_at, step, groups) * members + member_at) * rows, 8
        )
        for step in range(groups)
    ]
    copies = [
        pltpu.make_async_copy(starts.at[pl.ds(first_rows[step], rows)], held.at[step], sems.at[step]) for step in range(groups)
    ]
    for copy in copies:
        copy.start()
    scale = 1.0 / math.sqrt(center.shape[0])
    for step in range(groups):
        parent = parent_of[group_before(group_at, step, groups) * members * boxes]
        turns = sum(center[parent, axis] * center_dirs[axis] for axis in range(3))
        turn_cos, turn_sin = turned(turns)
        center_cos[step] = turn_cos * scale
        center_sin[step] = turn_sin * scale
    for step in range(groups):
        (cos_x, cos_y, cos_z), (sin_x, sin_y, sin_z) = ([table[step, axis] for axis in range(3)] for table in (axis_cos, axis_sin))
        both_cos, both_sin, sin_cos, cos_sin = cos_x * cos_y, sin_x * sin_y, sin_x * cos_y, cos_x * sin_y
        for swap in range(members):
            for box in range(boxes):
                slot = (group_at * members + (member_at ^ swap)) * boxes + box
                octant = octant_of[slot]
                live = jnp.where(parent_of[slot] >= 0, 1.0, 0.0)
                sign_x = ((octant & 1) * 2 - 1).astype(jnp.float32)
                sign_y = (((octant >> 1) & 1) * 2 - 1).astype(jnp.float32)
                sign_z = ((octant >> 2) * 2 - 1).astype(jnp.float32)
                real = both_cos - (sign_x * sign_y) * both_sin
                imag = sign_x * sin_cos + sign_y * cos_sin
                turn_cos, turn_sin = live * cos_z, (live * sign_z) * sin_z
                cosines[step, swap * boxes + box] = real * turn_cos - imag * turn_sin
                sines[step, swap * boxes + box] = real * turn_sin + imag * turn_cos
    for step in range(groups):
        copies[step].wait()
        child = ((first_rows[step] + row) * LANES + lane) >> 2
        excess[step] = (child - 2 - held[step]).astype(jnp.float32)


def columns_of(windows):
    return [2 * window + half for window in windows for half in range(2)]


def combine_kernel(jobs, members, boxes, sources, tiles, count, *refs):
    data = refs[:count]
    cosines, sines, excess, band_zero, band_one = refs[count : count + 5]
    *outs, spread, total = refs[count + 5 :]
    for (step, *job), out in zip(jobs, outs):
        combine(
            step, *job, members, boxes, sources, tiles, data, cosines.at[step], sines.at[step], excess.at[step],
            band_zero, band_one, out, spread, total,
        )


def combine(
    step, windows, places, rims, members, boxes, sources, tiles, data, cosines, sines, excess, band_zero, band_one, out, spread, total
):
    rows = boxes * 2 * sources
    block = data[0].shape[3]
    wide_at = lax.axis_index("wide")
    last = lax.axis_size("wide") - 1
    groups = lax.axis_size("wide") // members
    at = group_after(wide_at // members, step, groups) * members + wide_at % members
    first = at * (tiles * LANES)

    def local(ref, lane):
        return ref[:, :, :, pl.ds(pl.multiple_of(lane, LANES), LANES)].reshape(rows, LANES)

    def tile(index):
        if index < 0 or index >= tiles:
            return rim_tile
        found = [local(data[member], first + index * LANES) for member in range(2)]
        for which, base in places:
            ref = data[which]
            if len(ref.shape) == 4:
                found.append(ref[:, :, :, index * LANES : (index + 1) * LANES].reshape(rows, LANES))
            else:
                found.append(ref[base + index * rows : base + (index + 1) * rows, :])
        return jnp.concatenate(found, axis=0)

    if rims is not None:
        slot, lane = rim_masks()
        from_other = slot >= 2 * HALO
        side = jnp.where(from_other, slot - 2 * HALO, slot)
        outer = ((side < HALO) & (at == 0)) | ((side >= HALO) & (at == last))
        keep = (outer == from_other) & (slot < 4 * HALO)
        place = as_mask(
            ((side < HALO) & (lane == LANES - HALO + side)) | ((side >= HALO) & (side < 2 * HALO) & (lane == side - HALO))
        )
        found = []
        for inner, (other, other_row) in rims:
            outside = data[other][other_row : other_row + RIM, :].astype(jnp.float32)
            if inner is None:
                inside = jnp.zeros((RIM, LANES), jnp.float32)
            else:
                inside = data[inner[0]][inner[1] : inner[1] + RIM, :].astype(jnp.float32)
            found.append(jnp.where(keep, jnp.where(from_other, outside, inside), 0.0).astype(jnp.bfloat16))
        rim = jnp.concatenate(found, axis=1)
        rim_tile = lax.dot_general(rim, place, (((0,), (0,)), ((), ())), preferred_element_type=jnp.float32)
        lane = lax.broadcasted_iota(jnp.int32, (rows, LANES), 1)
        from_before = (lane >= LANES - HALO) & (at != 0)
        from_after = (lane < HALO) & (at != last)
        near = []
        for member in range(2):
            before = local(data[member], jnp.maximum(first - LANES, 0)).astype(jnp.float32)
            after = local(data[member], jnp.minimum(first + tiles * LANES, block - LANES)).astype(jnp.float32)
            near.append(jnp.where(from_before, before, jnp.where(from_after, after, 0.0)))
        near = jnp.concatenate(near, axis=0)
        rim_tile = jnp.concatenate([rim_tile[: 2 * rows] + near, rim_tile[2 * rows :]], axis=0).astype(jnp.bfloat16)

    def window_of(window):
        cut = 32 if window % 2 else 96
        left, right = tile((window - 1 + window % 2) // 2), tile((window + 1) // 2)
        cells = jnp.concatenate([left[:, cut:], right[:, :cut]], axis=1)
        return jnp.concatenate([cells, cells], axis=1)

    columns = columns_of(windows)
    width = len(columns)
    whole = width == 4 * tiles

    def spread_window(turn):
        bands = []
        for half, column in enumerate(columns[2 * turn : 2 * turn + 2]):
            which = jnp.broadcast_to(excess[column : column + 1, :], (16, LANES)).astype(jnp.bfloat16)
            which = jnp.concatenate([which] * (band_zero.shape[0] // 16), axis=0)
            lanes = slice(half * LANES, (half + 1) * LANES)
            bands.append(band_zero[:, lanes] * (1 - which) + band_one[:, lanes] * which)
        spread[turn % 2] = jnp.dot(
            window_of(windows[turn]), jnp.concatenate(bands, axis=1), preferred_element_type=jnp.float32
        )

    def sum_window(turn):
        for half, column in enumerate(columns[2 * turn : 2 * turn + 2]):
            lanes = slice(half * LANES, (half + 1) * LANES)
            real_sum = jnp.zeros((sources, LANES), jnp.float32)
            imag_sum = jnp.zeros((sources, LANES), jnp.float32)
            for child in range(members * boxes):
                start = child * 2 * sources
                real = spread[turn % 2, start : start + sources, lanes].astype(jnp.bfloat16).astype(jnp.float32)
                imag = spread[turn % 2, start + sources : start + 2 * sources, lanes]
                imag = imag.astype(jnp.bfloat16).astype(jnp.float32)
                cosine = cosines[child, column : column + 1, :]
                sine = sines[child, column : column + 1, :]
                real_sum = real_sum + (cosine * real - sine * imag)
                imag_sum = imag_sum + (sine * real + cosine * imag)
            if whole:
                total[pl.ds(column, sources, stride=width), :] = real_sum
                total[pl.ds(sources * width + column, sources, stride=width), :] = imag_sum
            else:
                at_row = (2 * turn + half) * 2 * sources
                out[at_row : at_row + sources, :] = real_sum.astype(out.dtype)
                out[at_row + sources : at_row + 2 * sources, :] = imag_sum.astype(out.dtype)

    for turn in range(len(windows) + 1):
        if turn < len(windows):
            spread_window(turn)
        if turn:
            sum_window(turn - 1)
    if whole:
        out[...] = total[...].astype(out.dtype)


def place_columns(arrived, columns, sources, rows, cosines, sines, pattern, far):
    for index, column in enumerate(columns):
        real, imag = (
            arrived[pl.ds((2 * index + half) * sources, sources), :].astype(jnp.float32) for half in range(2)
        )
        at = pl.ds(column, sources, stride=rows)
        pattern[0, at, :] = real
        pattern[1, at, :] = imag
        cosine, sine = cosines[column : column + 1, :], sines[column : column + 1, :]
        far[0, at, :] += cosine * real - sine * imag
        far[1, at, :] += sine * real + cosine * imag


def finish_ahead_kernel(steps, early_step, columns, members, boxes, sources, rows, parent_of, *refs):
    whole, (early, center_cos, center_sin, parent_out, far_out, early_out) = refs[: len(steps)], refs[len(steps) :]
    groups = lax.axis_size("wide") // members
    group_at = lax.axis_index("wide") // members
    names = [parent_of[group_before(group_at, step, groups) * members * boxes] for step in steps]
    for source in range(sources):
        at = pl.ds(source * rows, rows)
        far_real = far_imag = 0.0
        for index, step in enumerate(steps):
            real, imag = (
                whole[index][pl.ds((half * sources + source) * rows, rows), :].astype(jnp.float32) for half in range(2)
            )
            cosine, sine = center_cos[step], center_sin[step]
            parent_out[names[index], 0, at, :] = real
            parent_out[names[index], 1, at, :] = imag
            far_real = far_real + (cosine * real - sine * imag)
            far_imag = far_imag + (sine * real + cosine * imag)
        far_out[0, at, :] = far_real
        far_out[1, at, :] = far_imag
    place_columns(
        early, columns, sources, rows, center_cos.at[early_step], center_sin.at[early_step], early_out, far_out
    )


def finish_kernel(steps, early_step, columns, members, boxes, sources, rows, parts, parent_of, *refs):
    whole, refs = refs[: len(steps)], refs[len(steps) :]
    late, early, center_cos, center_sin, far_in, _, parent_out, far_out, names, held, far_held, name_sem, sems = refs
    name_copy = pltpu.make_async_copy(parent_of, names, name_sem)
    name_copy.start()
    group_at = lax.axis_index("wide") // members
    copies = []

    def send(source, target):
        copies.append(pltpu.make_async_copy(source, target, sems.at[len(copies)]))
        copies[-1].start()

    last = len(steps)
    held[last] = early[...]
    far_held[...] = far_in[...]
    place_columns(
        late, columns, sources, rows, center_cos.at[early_step], center_sin.at[early_step], held.at[last], far_held
    )
    name_copy.wait()
    groups = lax.axis_size("wide") // members
    places = [names[group_before(group_at, step, groups) * members * boxes] for step in (*steps, early_step)]
    send(held.at[last], parent_out.at[places[last]])
    each = sources // parts
    for part in range(parts):
        for source in range(part * each, (part + 1) * each):
            at = pl.ds(source * rows, rows)
            far_real, far_imag = far_held[0, at, :], far_held[1, at, :]
            for index, step in enumerate(steps):
                real, imag = (
                    whole[index][pl.ds((half * sources + source) * rows, rows), :].astype(jnp.float32) for half in range(2)
                )
                cosine, sine = center_cos[step], center_sin[step]
                held[index, 0, at, :] = real
                held[index, 1, at, :] = imag
                far_real = far_real + (cosine * real - sine * imag)
                far_imag = far_imag + (sine * real + cosine * imag)
            far_held[0, at, :] = far_real
            far_held[1, at, :] = far_imag
        at = pl.ds(part * each * rows, each * rows)
        for index in range(last):
            send(held.at[index, :, at], parent_out.at[places[index], :, at])
        send(far_held.at[:, at], far_out.at[:, at])
    for copy in copies:
        copy.wait()


def grouped(child_pattern, child_parent, child_octant, parent_center, stencil_start, members):
    n_wide = lax.axis_size("wide")
    boxes, _, sources, block = child_pattern.shape
    groups = n_wide // members
    piece = block // n_wide
    tiles = piece // LANES
    rows = boxes * 2 * sources
    out_rows = 4 * tiles
    parents = parent_center.shape[0]
    vmem = pl.BlockSpec(memory_space=pltpu.VMEM)
    smem = pl.BlockSpec(memory_space=pltpu.SMEM)
    hbm = pl.BlockSpec(memory_space=pltpu.HBM)
    limit = pltpu.CompilerParams(vmem_limit_bytes=16 * 1024 * 1024)

    def cost(micros):
        return pl.CostEstimate(flops=int(micros * 1e9), bytes_accessed=int(micros * 3.6e6) + 1, transcendentals=0)


    def bf16(*shape):
        return jax.ShapeDtypeStruct(shape, jnp.bfloat16)

    def f32(*shape):
        return jax.ShapeDtypeStruct(shape, jnp.float32)

    def swap_with(array, step):
        return lax.ppermute(array, "wide", [(i, i ^ step) for i in range(n_wide)])

    def move_by(array, step):
        shift = shift_of(step, groups) * members
        return lax.ppermute(array, "wide", [(i, (i + shift) % n_wide) for i in range(n_wide)])

    def tie(*arrays):
        return lax.optimization_barrier(arrays)

    far = members - 2
    wide_at = lax.axis_index("wide")
    heads = []
    for swap in range(2, members):
        first = (wide_at ^ (groups // 2 * members + swap)) * piece
        heads.append(lax.dynamic_slice_in_dim(child_pattern, first, piece, 3))
    near = swap_with(child_pattern, 1)
    heads = [swap_with(head, swap + 2) for swap, head in enumerate(heads)]

    def other_half(array, step):
        pairs = [(i * 2 + n, (i ^ step) * 2 + 1 - n) for i in range(n_wide) for n in range(2)]
        return lax.ppermute(array, ("wide", "narrow"), pairs)

    axes = pl.pallas_call(
        functools.partial(axes_kernel, groups, members, piece, stencil_start.shape[0]),
        out_shape=[f32(groups, 3, out_rows, LANES)] * 2 + [f32(3, out_rows, LANES)],
        out_specs=[vmem] * 3,
        compiler_params=limit,
        cost_estimate=cost(1),
        name="axes",
    )()
    tables = pl.pallas_call(
        functools.partial(prep_kernel, groups, members, boxes, piece),
        out_shape=[
            f32(groups, members * boxes, out_rows, LANES),
            f32(groups, members * boxes, out_rows, LANES),
            f32(parents, out_rows, LANES),
            f32(parents, out_rows, LANES),
            f32(groups, out_rows, LANES),
        ],
        in_specs=[smem, smem, smem, hbm] + [vmem] * 3,
        out_specs=[vmem] * 5,
        scratch_shapes=[pltpu.VMEM((groups, out_rows, LANES), jnp.int32), pltpu.SemaphoreType.DMA((groups,))],
        compiler_params=limit,
            cost_estimate=cost(1),
        name="prep",
    )(child_parent, child_octant, parent_center, stencil_start.reshape(-1, LANES), *axes)
    cosines, sines, center_cos, center_sin, excess = tables
    full = tiles * rows + RIM
    pairs = members // 2 - 1
    *sends, edges = pl.pallas_call(
        functools.partial(rest_pack_kernel, groups, members, piece),
        out_shape=[
            bf16(2 * (full + (RIM if part == 1 else 0)), LANES) for part in range(1, groups) for _ in range(pairs)
        ]
        + [bf16(2 * RIM, LANES)],
        in_specs=[vmem] * 2,
        out_specs=[vmem] * ((groups - 1) * pairs + 1),
        compiler_params=limit,
        cost_estimate=cost(1),
        name="pack",
    )(child_pattern, near)
    common = [other_half(edges, 2 * pair) for pair in range(pairs + 1)]
    bands = stencil_tables(LANES, 2 * LANES)

    top = groups - 1

    def sums_of(jobs, data, dtype, micros):
        shapes = [jax.ShapeDtypeStruct((2 * sources * len(columns_of(job[1])), LANES), dtype) for job in jobs]
        inputs = [*data, cosines, sines, excess, bands[0], bands[1]]
        return pl.pallas_call(
            functools.partial(combine_kernel, jobs, members, boxes, sources, tiles, len(data)),
            out_shape=shapes,
            in_specs=[vmem] * len(inputs),
            out_specs=[vmem] * len(shapes),
            scratch_shapes=[
                pltpu.VMEM((2, members * rows, 2 * LANES), jnp.float32),
                pltpu.VMEM((2 * sources * out_rows, LANES), jnp.float32),
            ],
            compiler_params=limit,
            cost_estimate=cost(micros),
            name="combine",
        )(*inputs)

    inner = list(range(1, 2 * tiles - 1))
    outer = [0, 2 * tiles - 1]
    every = list(range(2 * tiles))
    locals_ = [child_pattern, near]
    first_data = locals_ + heads
    first_places = [(2 + member, 0) for member in range(far)]
    (total,) = sums_of([(top, inner, first_places, None)], first_data, jnp.bfloat16, 5)
    early_sends = sends[pairs : 2 * pairs]
    *early_sends, total = tie(*early_sends, total)
    sends[pairs : 2 * pairs] = early_sends
    done = [move_by(total, top)]
    arrived = {}
    for part in range(1, groups):
        step = top - part
        sent = sends[(part - 1) * pairs : part * pairs]
        if part > 1:
            totals = list(sums_of(jobs, data, jnp.bfloat16, 30 if part == 2 else 2))
            if part < groups - 1:
                tied = tie(*sends[part * pairs : (part + 1) * pairs], *totals)
                sends[part * pairs : (part + 1) * pairs], totals = tied[:pairs], list(tied[pairs:])
            arrived[step + 1] = move_by(totals[0], step + 1)
            if part == 2:
                done.append(move_by(totals[1], top))
        got = [swap_with(array, 2 * pair + 2) for pair, array in enumerate(sent)]
        length = full + (RIM if part == 1 else 0)
        places = [(2 + member // 2, member % 2 * length) for member in range(far)]
        data = locals_ + got + common
        shift = 2 + pairs
        edge_at = [(shift + member // 2, member % 2 * RIM) for member in range(members)]
        rims = [None, None] + [(which, row + tiles * rows) for which, row in places]
        jobs = [(step, every, places, list(zip(rims, edge_at)))]
        if part == 1:
            rims = [None, None] + [(which, row + full) for which, row in places]
            outer_places = [(len(data) + member, 0) for member in range(far)]
            jobs.append((top, outer, outer_places, list(zip(rims, edge_at))))
            data = data + heads
    data[0], done[0] = tie(data[0], done[0])
    (arrived[0],) = sums_of(jobs, data, jnp.float32, 1)
    done = [(top, columns_of(inner), done[0]), (top, columns_of(outer), done[1])]
    held = arrived
    whole = f32(2, sources * out_rows, LANES)
    (_, early_columns, early_array), (_, late_columns, late_array) = done
    ahead = [0, *range(2, top)]
    parent_pattern, far_field, early_pattern = pl.pallas_call(
        functools.partial(finish_ahead_kernel, ahead, top, early_columns, members, boxes, sources, out_rows),
        out_shape=[f32(parents, *whole.shape), whole, whole],
        in_specs=[smem] + [vmem] * (len(ahead) + 3),
        out_specs=[vmem] * 3,
        compiler_params=limit,
        cost_estimate=cost(0),
        name="finish_ahead",
    )(child_parent, *[held[step] for step in ahead], early_array, center_cos, center_sin)
    steps = [1]
    parts = 4
    parent_pattern, far_field = pl.pallas_call(
        functools.partial(finish_kernel, steps, top, late_columns, members, boxes, sources, out_rows, parts),
        out_shape=[f32(parents, *whole.shape), whole],
        in_specs=[hbm] + [vmem] * (len(steps) + 5) + [hbm],
        out_specs=[hbm, hbm],
        input_output_aliases={len(steps) + 6: 0},
        scratch_shapes=[
            pltpu.SMEM(child_parent.shape, jnp.int32),
            pltpu.VMEM((len(steps) + 1, *whole.shape), jnp.float32),
            pltpu.VMEM(whole.shape, jnp.float32),
            pltpu.SemaphoreType.DMA,
            pltpu.SemaphoreType.DMA((1 + parts * (len(steps) + 1),)),
        ],
        compiler_params=limit,
        cost_estimate=cost(30),
        name="finish_last",
    )(child_parent, *[held[step] for step in steps], late_array, early_pattern, center_cos, center_sin, far_field, parent_pattern)
    return (
        parent_pattern.reshape(parents, 2, sources, 1, 4 * piece),
        far_field.reshape(2, sources, 1, 4 * piece),
    )


def power_of_two(number):
    return number > 0 and number & (number - 1) == 0


def per_device(child_pattern, child_parent, child_octant, parent_center, stencil_start):
    n_wide, n_narrow = lax.axis_size("wide"), lax.axis_size("narrow")
    boxes, _, sources, block = child_pattern.shape
    parents = parent_center.shape[0]
    run = child_parent.shape[0] // parents
    if run % boxes == 0 and block % n_wide == 0:
        members = run // boxes
        fits = (
            n_narrow == 2
            and n_wide == members * parents
            and power_of_two(members)
            and power_of_two(parents)
            and members >= 4
            and parents >= 4
            and block // n_wide % LANES == 0
            and block // n_wide // LANES >= 3
            and boxes * 2 * sources == LANES
            and sources % 16 == 0
            and stencil_start.shape[0] == 4 * block * n_narrow
        )
        if fits:
            return grouped(child_pattern, child_parent, child_octant, parent_center, stencil_start, members)
    return exchanged(child_pattern, child_parent, child_octant, parent_center, stencil_start)


def solution(mesh):
    in_specs = (P("wide", None, None, "narrow"), P(), P(), P(), P())
    out_specs = (P(None, None, None, "narrow", "wide"), P(None, None, "narrow", "wide"))
    return jax.shard_map(
        per_device, mesh=mesh, in_specs=in_specs, out_specs=out_specs, check_vma=False
    )
```

```python
import functools
import math

import jax
import jax.numpy as jnp
import ml_dtypes
import numpy as np
from jax import lax
from jax.experimental import pallas as pl
from jax.experimental.pallas import tpu as pltpu
from jax.sharding import PartitionSpec as P

K2 = 65536


def with_halo(cells, sides, width):
    for axis, dim in sides:
        count = lax.axis_size(axis)
        head = lax.slice_in_dim(cells, 0, width, axis=dim)
        tail = lax.slice_in_dim(cells, cells.shape[dim] - width, cells.shape[dim], axis=dim)
        cells = jnp.concatenate(
            [
                lax.ppermute(tail, axis, [(i, (i + 1) % count) for i in range(count)]),
                cells,
                lax.ppermute(head, axis, [((i + 1) % count, i) for i in range(count)]),
            ],
            axis=dim,
        )
    return cells


def lagrange_taps(starts, first_out):
    sample_count = starts.shape[0]
    sample = first_out + jnp.arange(sample_count, dtype=jnp.int32)
    excess = sample // 4 - 2 - starts
    offset_u = (sample % 4).astype(jnp.float32) * 0.25 + 2.125 + excess.astype(jnp.float32)
    basis = []
    for node in range(6):
        value = jnp.ones_like(offset_u)
        for other in range(6):
            if other != node:
                value = value * (offset_u - other) / (node - other)
        basis.append(value)
    zeros = jnp.zeros_like(offset_u)
    stacked = []
    for offset in range(7):
        lower = basis[offset - 1] if offset >= 1 else zeros
        upper = basis[offset] if offset <= 5 else zeros
        stacked.append(jnp.where(excess == 0, lower, upper))
    return jnp.stack(stacked).reshape(7, sample_count // 4, 4)


def interpolate(window, tap_weights):
    block_len = tap_weights.shape[1]
    leading = window.shape[:-1]
    flat_rows = window.reshape((-1, window.shape[-1]))
    row_count = flat_rows.shape[0]
    if block_len % 64 == 0 and block_len > 64:
        group = 64
    else:
        group = block_len
    blocks = block_len // group
    taps = tap_weights.reshape(7, blocks, 4 * group)
    if blocks == 1:
        band_rows = flat_rows.shape[1]
        paired = flat_rows[:, None, :]
    else:
        band_rows = 2 * group
        extended = jnp.pad(flat_rows, ((0, 0), (0, (blocks + 1) * group - flat_rows.shape[1])))
        split_rows = extended.reshape(row_count, blocks + 1, group)
        paired = jnp.concatenate([split_rows[:, :-1], split_rows[:, 1:]], axis=2)
    column = jnp.arange(band_rows, dtype=jnp.int32)[None, :, None]
    target = (jnp.arange(4 * group, dtype=jnp.int32) // 4)[None, None, :]
    offsets = jnp.arange(7, dtype=jnp.int32)[:, None, None]
    onehot = (column == target + offsets).astype(jnp.float32)
    band = jnp.einsum("kcj,kbj->bcj", onehot, taps, precision=lax.Precision.HIGHEST)
    total = jnp.einsum(
        "rbc,bcj->rbj", paired.astype(jnp.float32), band, precision=lax.Precision.HIGHEST
    )
    return total.reshape(leading + (4 * block_len,)).astype(jnp.bfloat16)


def directions(first_out, sample_count):
    sample = first_out + jnp.arange(sample_count, dtype=jnp.int32)
    cycles = K2 // 256
    azimuth = 2.0 * math.pi * ((sample % 256).astype(jnp.float32) + 0.5) / 256.0
    polar = math.pi * ((sample // 256).astype(jnp.float32) + 0.5) / cycles
    return (jnp.sin(polar) * jnp.cos(azimuth), jnp.sin(polar) * jnp.sin(azimuth), jnp.cos(polar))


def child_phase(octant, dir_x, dir_y, dir_z):
    sign_x = (octant % 2 * 2 - 1).astype(jnp.float32)
    sign_y = (octant // 2 % 2 * 2 - 1).astype(jnp.float32)
    sign_z = (octant // 4 * 2 - 1).astype(jnp.float32)
    return (
        2.0
        * math.pi
        * 2.0
        * (sign_x[:, None] * dir_x + sign_y[:, None] * dir_y + sign_z[:, None] * dir_z)
    )


def shift_children(pattern, octant, dir_x, dir_y, dir_z):
    angle = child_phase(octant, dir_x, dir_y, dir_z)
    cosine = jnp.cos(angle)[:, None, :]
    sine_part = jnp.sin(angle)[:, None, :]
    real_part = pattern[:, 0].astype(jnp.float32)
    imag_part = pattern[:, 1].astype(jnp.float32)
    return jnp.stack(
        [cosine * real_part - sine_part * imag_part, sine_part * real_part + cosine * imag_part],
        axis=1,
    )


def exchanged(child_pattern, child_parent, child_octant, parent_center, stencil_start):
    n_wide = lax.axis_size("wide")
    box_count, _, sources, block_one = child_pattern.shape
    block_two = 4 * block_one
    piece_len = block_one // n_wide
    narrow_at = lax.axis_index("narrow")
    wide_at = lax.axis_index("wide")
    out_first = narrow_at * block_two + wide_at * (4 * piece_len)
    parent_count = parent_center.shape[0]
    parent_ids = jnp.arange(parent_count, dtype=jnp.int32)
    dir_x, dir_y, dir_z = directions(out_first, 4 * piece_len)
    padded = with_halo(child_pattern, (("narrow", 3),), 3)
    shape_pieces = (box_count, 2, sources, n_wide, piece_len)
    left_rim = padded[..., 0:block_one].reshape(shape_pieces)[..., :3]
    middle = padded[..., 3 : 3 + block_one].reshape(shape_pieces)
    right_rim = padded[..., 6 : 6 + block_one].reshape(shape_pieces)[..., piece_len - 3 :]
    windows = jnp.concatenate([left_rim, middle, right_rim], axis=-1)
    starts = lax.dynamic_slice_in_dim(stencil_start, out_first, 4 * piece_len)
    tap_weights = lagrange_taps(starts, out_first)
    gathered = interpolate(
        lax.all_to_all(windows, "wide", split_axis=3, concat_axis=0, tiled=True)[:, :, :, 0, :],
        tap_weights,
    )
    shifted = shift_children(gathered, child_octant, dir_x, dir_y, dir_z)
    selector = (child_parent[:, None] == parent_ids[None, :]).astype(jnp.float32)
    parents_total = jnp.einsum("bp,bcrj->pcrj", selector, shifted, precision=lax.Precision.HIGHEST)
    center_angle = (
        2.0
        * math.pi
        * (
            parent_center[:, 0:1] * dir_x
            + parent_center[:, 1:2] * dir_y
            + parent_center[:, 2:3] * dir_z
        )
    )
    center_cos = jnp.cos(center_angle)
    center_sin = jnp.sin(center_angle)
    real_sum = jnp.einsum(
        "pj,prj->rj", center_cos, parents_total[:, 0], precision=lax.Precision.HIGHEST
    ) - jnp.einsum("pj,prj->rj", center_sin, parents_total[:, 1], precision=lax.Precision.HIGHEST)
    imag_sum = jnp.einsum(
        "pj,prj->rj", center_sin, parents_total[:, 0], precision=lax.Precision.HIGHEST
    ) + jnp.einsum("pj,prj->rj", center_cos, parents_total[:, 1], precision=lax.Precision.HIGHEST)
    far_field = jnp.stack([real_sum, imag_sum]) / math.sqrt(parent_count)
    parent_pattern = parents_total[:, :, :, None, :]
    return (parent_pattern, far_field[:, :, None, :])


LANES = 128
HALO = 3
RIM = 16


def stencil_tables(window, columns):
    tables = np.zeros((2, window, columns), np.float32)
    for excess in range(2):
        for column in range(columns):
            offset_u = np.float32((column % 4) * 0.25 + 2.125 + excess)
            first = window // 4 + column // 4 - 2 - excess
            for node in range(6):
                value = np.float32(1.0)
                for other in range(6):
                    if other != node:
                        value = np.float32(
                            value * np.float32(np.float32(offset_u - np.float32(other)) / np.float32(node - other))
                        )
                tables[excess, first + node, column] = value
    high = tables.astype(ml_dtypes.bfloat16)
    low = (tables - high.astype(np.float32)).astype(ml_dtypes.bfloat16)
    return np.concatenate([high, low], axis=1)


def shift_of(step, groups):
    half = groups // 2
    return ([0] + [half, *(shift for shift in range(1, groups) if shift != half)][::-1])[step]


def group_after(group, step, groups):
    return (group + shift_of(step, groups)) & (groups - 1)


def group_before(group, step, groups):
    return (group + groups - shift_of(step, groups)) & (groups - 1)


def rim_masks():
    slot = lax.broadcasted_iota(jnp.int32, (RIM, LANES), 0)
    lane = lax.broadcasted_iota(jnp.int32, (RIM, LANES), 1)
    return slot, lane


def as_mask(condition):
    return jnp.where(condition, 1.0, 0.0).astype(jnp.bfloat16)


def rim_of(before, after, first_slot):
    slot, lane = rim_masks()
    slot = slot - first_slot
    pick_before = as_mask((slot >= 0) & (slot < HALO) & (lane == LANES - HALO + slot))
    pick_after = as_mask((slot >= HALO) & (slot < 2 * HALO) & (lane == slot - HALO))
    across = (((1,), (1,)), ((), ()))
    rim = lax.dot_general(pick_before, before, across, preferred_element_type=jnp.float32)
    return rim + lax.dot_general(pick_after, after, across, preferred_element_type=jnp.float32)


def rest_pack_kernel(groups, members, piece, cells, near, *outs):
    boxes, parts, sources, block = cells.shape
    rows = boxes * parts * sources
    tiles = piece // LANES
    wide_at = lax.axis_index("wide")
    group_at, member_at = wide_at // members, wide_at % members

    def tile(ref, at):
        return ref[:, :, :, pl.ds(pl.multiple_of(at, LANES), LANES)].reshape(rows, LANES)

    def rim_at(ref, first):
        return rim_of(tile(ref, jnp.maximum(first - LANES, 0)), tile(ref, jnp.minimum(first + piece, block - LANES)), 0)

    edges = outs[-1]
    for half, ref in enumerate((cells, near)):
        rim = rim_of(tile(ref, block - LANES), tile(ref, 0), 2 * HALO)
        edges[half * RIM : (half + 1) * RIM, :] = rim.astype(jnp.bfloat16)
    for part in range(1, groups):
        for swap in range(2, members, 2):
            out, base = outs[(part - 1) * (members // 2 - 1) + swap // 2 - 1], 0
            target = member_at ^ swap
            first = (group_after(group_at, groups - 1 - part, groups) * members + target) * piece
            for ref in (cells, near):
                for index in range(tiles):
                    out[base : base + rows, :] = tile(ref, first + index * LANES)
                    base += rows
                out[base : base + RIM, :] = rim_at(ref, first).astype(jnp.bfloat16)
                base += RIM
                if part == 1:
                    rim = rim_at(ref, (group_after(group_at, groups - 1, groups) * members + target) * piece)
                    out[base : base + RIM, :] = rim.astype(jnp.bfloat16)
                    base += RIM


def turned(cycles):
    half = math.pi * (cycles - jnp.floor(cycles + 0.5))
    square = half * half
    sine, cosine = jnp.zeros_like(half), jnp.zeros_like(half)
    for order in range(13, 0, -2):
        sine = sine * square + (-1) ** (order // 2) / math.factorial(order)
        cosine = cosine * square + (-1) ** (order // 2) / math.factorial(order - 1)
    sine = sine * half
    return 1.0 - 2.0 * sine * sine, 2.0 * sine * cosine


def axes_kernel(groups, members, piece, sample_count, cosines, sines, center_dirs):
    wide_at = lax.axis_index("wide")
    group_at, member_at = wide_at // members, wide_at % members
    rows = 4 * piece // LANES
    half_rows = sample_count // LANES // lax.axis_size("narrow")
    row = lax.broadcasted_iota(jnp.int32, (rows, LANES), 0)
    lane = lax.broadcasted_iota(jnp.int32, (rows, LANES), 1)
    cos_azimuth, sin_azimuth = turned((((row * LANES + lane) & 255).astype(jnp.float32) + 0.5) / 256.0)
    for step in range(groups):
        at = group_after(group_at, step, groups) * members + member_at
        first_row = lax.axis_index("narrow") * half_rows + at * rows
        ring = ((first_row + row) * LANES + lane) >> 8
        dir_z, sin_polar = turned((ring.astype(jnp.float32) + 0.5) / (2 * (sample_count // 256)))
        for axis, direction in enumerate((sin_polar * cos_azimuth, sin_polar * sin_azimuth, dir_z)):
            cosines[step, axis], sines[step, axis] = turned(2.0 * direction)
            if step == 0:
                center_dirs[axis] = direction


def prep_kernel(
    groups, members, boxes, piece, parent_of, octant_of, center, starts, axis_cos, axis_sin, center_dirs,
    cosines, sines, center_cos, center_sin, excess, held, sems,
):
    wide_at = lax.axis_index("wide")
    group_at, member_at = wide_at // members, wide_at % members
    rows = 4 * piece // LANES
    half_rows = starts.shape[0] // lax.axis_size("narrow")
    row = lax.broadcasted_iota(jnp.int32, (rows, LANES), 0)
    lane = lax.broadcasted_iota(jnp.int32, (rows, LANES), 1)
    first_rows = [
        pl.multiple_of(
            lax.axis_index("narrow") * half_rows + (group_after(group_at, step, groups) * members + member_at) * rows, 8
        )
        for step in range(groups)
    ]
    copies = [
        pltpu.make_async_copy(starts.at[pl.ds(first_rows[step], rows)], held.at[step], sems.at[step]) for step in range(groups)
    ]
    for copy in copies:
        copy.start()
    scale = 1.0 / math.sqrt(center.shape[0])
    for step in range(groups):
        parent = parent_of[group_before(group_at, step, groups) * members * boxes]
        turns = sum(center[parent, axis] * center_dirs[axis] for axis in range(3))
        turn_cos, turn_sin = turned(turns)
        center_cos[step] = turn_cos * scale
        center_sin[step] = turn_sin * scale
    for step in range(groups):
        (cos_x, cos_y, cos_z), (sin_x, sin_y, sin_z) = ([table[step, axis] for axis in range(3)] for table in (axis_cos, axis_sin))
        both_cos, both_sin, sin_cos, cos_sin = cos_x * cos_y, sin_x * sin_y, sin_x * cos_y, cos_x * sin_y
        for swap in range(members):
            for box in range(boxes):
                slot = (group_at * members + (member_at ^ swap)) * boxes + box
                octant = octant_of[slot]
                live = jnp.where(parent_of[slot] >= 0, 1.0, 0.0)
                sign_x = ((octant & 1) * 2 - 1).astype(jnp.float32)
                sign_y = (((octant >> 1) & 1) * 2 - 1).astype(jnp.float32)
                sign_z = ((octant >> 2) * 2 - 1).astype(jnp.float32)
                real = both_cos - (sign_x * sign_y) * both_sin
                imag = sign_x * sin_cos + sign_y * cos_sin
                turn_cos, turn_sin = live * cos_z, (live * sign_z) * sin_z
                cosines[step, swap * boxes + box] = real * turn_cos - imag * turn_sin
                sines[step, swap * boxes + box] = real * turn_sin + imag * turn_cos
    for step in range(groups):
        copies[step].wait()
        child = ((first_rows[step] + row) * LANES + lane) >> 2
        excess[step] = (child - 2 - held[step]).astype(jnp.float32)


def columns_of(windows):
    return [2 * window + half for window in windows for half in range(2)]


def combine_kernel(jobs, members, boxes, sources, tiles, count, *refs):
    data = refs[:count]
    cosines, sines, excess, band_zero, band_one = refs[count : count + 5]
    *outs, spread, total = refs[count + 5 :]
    for (step, *job), out in zip(jobs, outs):
        combine(
            step, *job, members, boxes, sources, tiles, data, cosines.at[step], sines.at[step], excess.at[step],
            band_zero, band_one, out, spread, total,
        )


def combine(
    step, windows, places, rims, members, boxes, sources, tiles, data, cosines, sines, excess, band_zero, band_one, out, spread, total
):
    rows = boxes * 2 * sources
    block = data[0].shape[3]
    wide_at = lax.axis_index("wide")
    last = lax.axis_size("wide") - 1
    groups = lax.axis_size("wide") // members
    at = group_after(wide_at // members, step, groups) * members + wide_at % members
    first = at * (tiles * LANES)

    def local(ref, lane):
        return ref[:, :, :, pl.ds(pl.multiple_of(lane, LANES), LANES)].reshape(rows, LANES)

    def tile(index):
        if index < 0 or index >= tiles:
            return rim_tile
        found = [local(data[member], first + index * LANES) for member in range(2)]
        for which, base in places:
            ref = data[which]
            if len(ref.shape) == 4:
                found.append(ref[:, :, :, index * LANES : (index + 1) * LANES].reshape(rows, LANES))
            else:
                found.append(ref[base + index * rows : base + (index + 1) * rows, :])
        return jnp.concatenate(found, axis=0)

    if rims is not None:
        slot, lane = rim_masks()
        from_other = slot >= 2 * HALO
        side = jnp.where(from_other, slot - 2 * HALO, slot)
        outer = ((side < HALO) & (at == 0)) | ((side >= HALO) & (at == last))
        keep = (outer == from_other) & (slot < 4 * HALO)
        place = as_mask(
            ((side < HALO) & (lane == LANES - HALO + side)) | ((side >= HALO) & (side < 2 * HALO) & (lane == side - HALO))
        )
        found = []
        for inner, (other, other_row) in rims:
            outside = data[other][other_row : other_row + RIM, :].astype(jnp.float32)
            if inner is None:
                inside = jnp.zeros((RIM, LANES), jnp.float32)
            else:
                inside = data[inner[0]][inner[1] : inner[1] + RIM, :].astype(jnp.float32)
            found.append(jnp.where(keep, jnp.where(from_other, outside, inside), 0.0).astype(jnp.bfloat16))
        rim = jnp.concatenate(found, axis=1)
        rim_tile = lax.dot_general(rim, place, (((0,), (0,)), ((), ())), preferred_element_type=jnp.float32)
        lane = lax.broadcasted_iota(jnp.int32, (rows, LANES), 1)
        from_before = (lane >= LANES - HALO) & (at != 0)
        from_after = (lane < HALO) & (at != last)
        near = []
        for member in range(2):
            before = local(data[member], jnp.maximum(first - LANES, 0)).astype(jnp.float32)
            after = local(data[member], jnp.minimum(first + tiles * LANES, block - LANES)).astype(jnp.float32)
            near.append(jnp.where(from_before, before, jnp.where(from_after, after, 0.0)))
        near = jnp.concatenate(near, axis=0)
        rim_tile = jnp.concatenate([rim_tile[: 2 * rows] + near, rim_tile[2 * rows :]], axis=0).astype(jnp.bfloat16)

    def window_of(window):
        cut = 32 if window % 2 else 96
        left, right = tile((window - 1 + window % 2) // 2), tile((window + 1) // 2)
        cells = jnp.concatenate([left[:, cut:], right[:, :cut]], axis=1)
        return jnp.concatenate([cells, cells], axis=1)

    columns = columns_of(windows)
    width = len(columns)
    whole = width == 4 * tiles

    def spread_window(turn):
        bands = []
        for half, column in enumerate(columns[2 * turn : 2 * turn + 2]):
            which = jnp.broadcast_to(excess[column : column + 1, :], (16, LANES)).astype(jnp.bfloat16)
            which = jnp.concatenate([which] * (band_zero.shape[0] // 16), axis=0)
            lanes = slice(half * LANES, (half + 1) * LANES)
            bands.append(band_zero[:, lanes] * (1 - which) + band_one[:, lanes] * which)
        spread[turn % 2] = jnp.dot(
            window_of(windows[turn]), jnp.concatenate(bands, axis=1), preferred_element_type=jnp.float32
        )

    def sum_window(turn):
        for half, column in enumerate(columns[2 * turn : 2 * turn + 2]):
            lanes = slice(half * LANES, (half + 1) * LANES)
            real_sum = jnp.zeros((sources, LANES), jnp.float32)
            imag_sum = jnp.zeros((sources, LANES), jnp.float32)
            for child in range(members * boxes):
                start = child * 2 * sources
                real = spread[turn % 2, start : start + sources, lanes].astype(jnp.bfloat16).astype(jnp.float32)
                imag = spread[turn % 2, start + sources : start + 2 * sources, lanes]
                imag = imag.astype(jnp.bfloat16).astype(jnp.float32)
                cosine = cosines[child, column : column + 1, :]
                sine = sines[child, column : column + 1, :]
                real_sum = real_sum + (cosine * real - sine * imag)
                imag_sum = imag_sum + (sine * real + cosine * imag)
            if whole:
                total[pl.ds(column, sources, stride=width), :] = real_sum
                total[pl.ds(sources * width + column, sources, stride=width), :] = imag_sum
            else:
                at_row = (2 * turn + half) * 2 * sources
                out[at_row : at_row + sources, :] = real_sum.astype(out.dtype)
                out[at_row + sources : at_row + 2 * sources, :] = imag_sum.astype(out.dtype)

    for turn in range(len(windows) + 1):
        if turn < len(windows):
            spread_window(turn)
        if turn:
            sum_window(turn - 1)
    if whole:
        out[...] = total[...].astype(out.dtype)


def place_columns(arrived, columns, sources, rows, cosines, sines, pattern, far):
    for index, column in enumerate(columns):
        real, imag = (
            arrived[pl.ds((2 * index + half) * sources, sources), :].astype(jnp.float32) for half in range(2)
        )
        at = pl.ds(column, sources, stride=rows)
        pattern[0, at, :] = real
        pattern[1, at, :] = imag
        cosine, sine = cosines[column : column + 1, :], sines[column : column + 1, :]
        far[0, at, :] += cosine * real - sine * imag
        far[1, at, :] += sine * real + cosine * imag


def finish_ahead_kernel(steps, early_step, columns, members, boxes, sources, rows, parent_of, *refs):
    whole, (early, center_cos, center_sin, parent_out, far_out, early_out) = refs[: len(steps)], refs[len(steps) :]
    groups = lax.axis_size("wide") // members
    group_at = lax.axis_index("wide") // members
    names = [parent_of[group_before(group_at, step, groups) * members * boxes] for step in steps]
    for source in range(sources):
        at = pl.ds(source * rows, rows)
        far_real = far_imag = 0.0
        for index, step in enumerate(steps):
            real, imag = (
                whole[index][pl.ds((half * sources + source) * rows, rows), :].astype(jnp.float32) for half in range(2)
            )
            cosine, sine = center_cos[step], center_sin[step]
            parent_out[names[index], 0, at, :] = real
            parent_out[names[index], 1, at, :] = imag
            far_real = far_real + (cosine * real - sine * imag)
            far_imag = far_imag + (sine * real + cosine * imag)
        far_out[0, at, :] = far_real
        far_out[1, at, :] = far_imag
    place_columns(
        early, columns, sources, rows, center_cos.at[early_step], center_sin.at[early_step], early_out, far_out
    )


def join_kernel(steps, early_step, columns, members, boxes, sources, rows, parent_of, *refs):
    whole, refs = refs[: len(steps)], refs[len(steps) :]
    late, early, center_cos, center_sin, far_in, _, parent_out, far_out, names, patterns, name_sem, sems = refs
    name_copy = pltpu.make_async_copy(parent_of, names, name_sem)
    name_copy.start()
    last = len(steps)
    patterns[last] = early[...]
    for source in range(sources):
        at = pl.ds(source * rows, rows)
        far_real, far_imag = far_in[0, at, :], far_in[1, at, :]
        for index, step in enumerate(steps):
            real, imag = (
                whole[index][pl.ds((half * sources + source) * rows, rows), :].astype(jnp.float32) for half in range(2)
            )
            cosine, sine = center_cos[step], center_sin[step]
            patterns[index, 0, at, :] = real
            patterns[index, 1, at, :] = imag
            far_real = far_real + (cosine * real - sine * imag)
            far_imag = far_imag + (sine * real + cosine * imag)
        far_out[0, at, :] = far_real
        far_out[1, at, :] = far_imag
    place_columns(
        late, columns, sources, rows, center_cos.at[early_step], center_sin.at[early_step], patterns.at[last], far_out
    )
    name_copy.wait()
    groups = lax.axis_size("wide") // members
    group_at = lax.axis_index("wide") // members
    copies = []
    for index, step in enumerate((*steps, early_step)):
        name = names[group_before(group_at, step, groups) * members * boxes]
        copies.append(pltpu.make_async_copy(patterns.at[index], parent_out.at[name], sems.at[index]))
        copies[-1].start()
    for copy in copies:
        copy.wait()


def finish_kernel(steps, members, boxes, sources, rows, parts, parent_of, *refs):
    whole, refs = refs[: len(steps)], refs[len(steps) :]
    center_cos, center_sin, far_in, _, parent_out, far_out, names, held, far_held, name_sem, sems = refs
    name_copy = pltpu.make_async_copy(parent_of, names, name_sem)
    name_copy.start()
    group_at = lax.axis_index("wide") // members
    copies = []

    def send(source, target):
        copies.append(pltpu.make_async_copy(source, target, sems.at[len(copies)]))
        copies[-1].start()

    last = len(steps)
    name_copy.wait()
    groups = lax.axis_size("wide") // members
    places = [names[group_before(group_at, step, groups) * members * boxes] for step in steps]
    each = sources // parts
    for part in range(parts):
        for source in range(part * each, (part + 1) * each):
            at = pl.ds(source * rows, rows)
            far_real, far_imag = far_in[0, at, :], far_in[1, at, :]
            for index, step in enumerate(steps):
                real, imag = (
                    whole[index][pl.ds((half * sources + source) * rows, rows), :].astype(jnp.float32) for half in range(2)
                )
                cosine, sine = center_cos[step], center_sin[step]
                held[index, 0, at, :] = real
                held[index, 1, at, :] = imag
                far_real = far_real + (cosine * real - sine * imag)
                far_imag = far_imag + (sine * real + cosine * imag)
            far_held[0, at, :] = far_real
            far_held[1, at, :] = far_imag
        at = pl.ds(part * each * rows, each * rows)
        for index in range(last):
            send(held.at[index, :, at], parent_out.at[places[index], :, at])
        send(far_held.at[:, at], far_out.at[:, at])
    for copy in copies:
        copy.wait()


def grouped(child_pattern, child_parent, child_octant, parent_center, stencil_start, members):
    n_wide = lax.axis_size("wide")
    boxes, _, sources, block = child_pattern.shape
    groups = n_wide // members
    piece = block // n_wide
    tiles = piece // LANES
    rows = boxes * 2 * sources
    out_rows = 4 * tiles
    parents = parent_center.shape[0]
    vmem = pl.BlockSpec(memory_space=pltpu.VMEM)
    smem = pl.BlockSpec(memory_space=pltpu.SMEM)
    hbm = pl.BlockSpec(memory_space=pltpu.HBM)
    limit = pltpu.CompilerParams(vmem_limit_bytes=16 * 1024 * 1024)

    def cost(micros):
        return pl.CostEstimate(flops=int(micros * 1e9), bytes_accessed=int(micros * 3.6e6) + 1, transcendentals=0)


    def bf16(*shape):
        return jax.ShapeDtypeStruct(shape, jnp.bfloat16)

    def f32(*shape):
        return jax.ShapeDtypeStruct(shape, jnp.float32)

    def swap_with(array, step):
        return lax.ppermute(array, "wide", [(i, i ^ step) for i in range(n_wide)])

    def move_by(array, step):
        shift = shift_of(step, groups) * members
        return lax.ppermute(array, "wide", [(i, (i + shift) % n_wide) for i in range(n_wide)])

    def tie(*arrays):
        return lax.optimization_barrier(arrays)

    far = members - 2
    wide_at = lax.axis_index("wide")
    heads = []
    for swap in range(2, members):
        first = (wide_at ^ (groups // 2 * members + swap)) * piece
        heads.append(lax.dynamic_slice_in_dim(child_pattern, first, piece, 3))
    near = swap_with(child_pattern, 1)
    heads = [swap_with(head, swap + 2) for swap, head in enumerate(heads)]

    def other_half(array, step):
        pairs = [(i * 2 + n, (i ^ step) * 2 + 1 - n) for i in range(n_wide) for n in range(2)]
        return lax.ppermute(array, ("wide", "narrow"), pairs)

    axes = pl.pallas_call(
        functools.partial(axes_kernel, groups, members, piece, stencil_start.shape[0]),
        out_shape=[f32(groups, 3, out_rows, LANES)] * 2 + [f32(3, out_rows, LANES)],
        out_specs=[vmem] * 3,
        compiler_params=limit,
        cost_estimate=cost(1),
        name="axes",
    )()
    tables = pl.pallas_call(
        functools.partial(prep_kernel, groups, members, boxes, piece),
        out_shape=[
            f32(groups, members * boxes, out_rows, LANES),
            f32(groups, members * boxes, out_rows, LANES),
            f32(parents, out_rows, LANES),
            f32(parents, out_rows, LANES),
            f32(groups, out_rows, LANES),
        ],
        in_specs=[smem, smem, smem, hbm] + [vmem] * 3,
        out_specs=[vmem] * 5,
        scratch_shapes=[pltpu.VMEM((groups, out_rows, LANES), jnp.int32), pltpu.SemaphoreType.DMA((groups,))],
        compiler_params=limit,
            cost_estimate=cost(1),
        name="prep",
    )(child_parent, child_octant, parent_center, stencil_start.reshape(-1, LANES), *axes)
    cosines, sines, center_cos, center_sin, excess = tables
    full = tiles * rows + RIM
    pairs = members // 2 - 1
    *sends, edges = pl.pallas_call(
        functools.partial(rest_pack_kernel, groups, members, piece),
        out_shape=[
            bf16(2 * (full + (RIM if part == 1 else 0)), LANES) for part in range(1, groups) for _ in range(pairs)
        ]
        + [bf16(2 * RIM, LANES)],
        in_specs=[vmem] * 2,
        out_specs=[vmem] * ((groups - 1) * pairs + 1),
        compiler_params=limit,
        cost_estimate=cost(1),
        name="pack",
    )(child_pattern, near)
    common = [other_half(edges, 2 * pair) for pair in range(pairs + 1)]
    bands = stencil_tables(LANES, 2 * LANES)

    top = groups - 1

    def sums_of(jobs, data, dtype, micros):
        shapes = [jax.ShapeDtypeStruct((2 * sources * len(columns_of(job[1])), LANES), dtype) for job in jobs]
        inputs = [*data, cosines, sines, excess, bands[0], bands[1]]
        return pl.pallas_call(
            functools.partial(combine_kernel, jobs, members, boxes, sources, tiles, len(data)),
            out_shape=shapes,
            in_specs=[vmem] * len(inputs),
            out_specs=[vmem] * len(shapes),
            scratch_shapes=[
                pltpu.VMEM((2, members * rows, 2 * LANES), jnp.float32),
                pltpu.VMEM((2 * sources * out_rows, LANES), jnp.float32),
            ],
            compiler_params=limit,
            cost_estimate=cost(micros),
            name="combine",
        )(*inputs)

    inner = list(range(1, 2 * tiles - 1))
    outer = [0, 2 * tiles - 1]
    every = list(range(2 * tiles))
    locals_ = [child_pattern, near]
    first_data = locals_ + heads
    first_places = [(2 + member, 0) for member in range(far)]
    (total,) = sums_of([(top, inner, first_places, None)], first_data, jnp.bfloat16, 5)
    early_sends = sends[pairs : 2 * pairs]
    *early_sends, total = tie(*early_sends, total)
    sends[pairs : 2 * pairs] = early_sends
    done = [move_by(total, top)]
    arrived = {}
    for part in range(1, groups):
        step = top - part
        sent = sends[(part - 1) * pairs : part * pairs]
        if part > 1:
            totals = list(sums_of(jobs, data, jnp.bfloat16, 30 if part == 2 else 2))
            if part < groups - 1:
                tied = tie(*sends[part * pairs : (part + 1) * pairs], *totals)
                sends[part * pairs : (part + 1) * pairs], totals = tied[:pairs], list(tied[pairs:])
            arrived[step + 1] = move_by(totals[0], step + 1)
            if part == 2:
                done.append(move_by(totals[1], top))
        got = [swap_with(array, 2 * pair + 2) for pair, array in enumerate(sent)]
        length = full + (RIM if part == 1 else 0)
        places = [(2 + member // 2, member % 2 * length) for member in range(far)]
        data = locals_ + got + common
        shift = 2 + pairs
        edge_at = [(shift + member // 2, member % 2 * RIM) for member in range(members)]
        rims = [None, None] + [(which, row + tiles * rows) for which, row in places]
        jobs = [(step, every, places, list(zip(rims, edge_at)))]
        if part == 1:
            rims = [None, None] + [(which, row + full) for which, row in places]
            outer_places = [(len(data) + member, 0) for member in range(far)]
            jobs.append((top, outer, outer_places, list(zip(rims, edge_at))))
            data = data + heads
    data[0], done[0] = tie(data[0], done[0])
    (arrived[0],) = sums_of(jobs, data, jnp.float32, 0)
    done = [(top, columns_of(inner), done[0]), (top, columns_of(outer), done[1])]
    held = arrived
    whole = f32(2, sources * out_rows, LANES)
    (_, early_columns, early_array), (_, late_columns, late_array) = done
    ahead = [0]
    parent_pattern, far_field, early_pattern = pl.pallas_call(
        functools.partial(finish_ahead_kernel, ahead, top, early_columns, members, boxes, sources, out_rows),
        out_shape=[f32(parents, *whole.shape), whole, whole],
        in_specs=[smem] + [vmem] * (len(ahead) + 3),
        out_specs=[vmem] * 3,
        compiler_params=limit,
        cost_estimate=cost(0),
        name="finish_ahead",
    )(child_parent, *[held[step] for step in ahead], early_array, center_cos, center_sin)
    between = list(range(2, top))
    parent_pattern, far_field = pl.pallas_call(
        functools.partial(join_kernel, between, top, late_columns, members, boxes, sources, out_rows),
        out_shape=[f32(parents, *whole.shape), whole],
        in_specs=[hbm] + [vmem] * (len(between) + 5) + [hbm],
        out_specs=[hbm, vmem],
        input_output_aliases={len(between) + 6: 0},
        scratch_shapes=[
            pltpu.SMEM(child_parent.shape, jnp.int32),
            pltpu.VMEM((len(between) + 1, *whole.shape), jnp.float32),
            pltpu.SemaphoreType.DMA,
            pltpu.SemaphoreType.DMA((len(between) + 1,)),
        ],
        compiler_params=limit,
        cost_estimate=cost(5),
        name="join",
    )(
        child_parent, *[held[step] for step in between], late_array, early_pattern, center_cos, center_sin, far_field,
        parent_pattern,
    )
    steps = [1]
    parts = 4
    parent_pattern, far_field = pl.pallas_call(
        functools.partial(finish_kernel, steps, members, boxes, sources, out_rows, parts),
        out_shape=[f32(parents, *whole.shape), whole],
        in_specs=[hbm] + [vmem] * (len(steps) + 3) + [hbm],
        out_specs=[hbm, hbm],
        input_output_aliases={len(steps) + 4: 0},
        scratch_shapes=[
            pltpu.SMEM(child_parent.shape, jnp.int32),
            pltpu.VMEM((len(steps), *whole.shape), jnp.float32),
            pltpu.VMEM(whole.shape, jnp.float32),
            pltpu.SemaphoreType.DMA,
            pltpu.SemaphoreType.DMA((parts * (len(steps) + 1),)),
        ],
        compiler_params=limit,
        cost_estimate=cost(30),
        name="finish_last",
    )(child_parent, *[held[step] for step in steps], center_cos, center_sin, far_field, parent_pattern)
    return (
        parent_pattern.reshape(parents, 2, sources, 1, 4 * piece),
        far_field.reshape(2, sources, 1, 4 * piece),
    )


def power_of_two(number):
    return number > 0 and number & (number - 1) == 0


def per_device(child_pattern, child_parent, child_octant, parent_center, stencil_start):
    n_wide, n_narrow = lax.axis_size("wide"), lax.axis_size("narrow")
    boxes, _, sources, block = child_pattern.shape
    parents = parent_center.shape[0]
    run = child_parent.shape[0] // parents
    if run % boxes == 0 and block % n_wide == 0:
        members = run // boxes
        fits = (
            n_narrow == 2
            and n_wide == members * parents
            and power_of_two(members)
            and power_of_two(parents)
            and members >= 4
            and parents >= 4
            and block // n_wide % LANES == 0
            and block // n_wide // LANES >= 3
            and boxes * 2 * sources == LANES
            and sources % 16 == 0
            and stencil_start.shape[0] == 4 * block * n_narrow
        )
        if fits:
            return grouped(child_pattern, child_parent, child_octant, parent_center, stencil_start, members)
    return exchanged(child_pattern, child_parent, child_octant, parent_center, stencil_start)


def solution(mesh):
    in_specs = (P("wide", None, None, "narrow"), P(), P(), P(), P())
    out_specs = (P(None, None, None, "narrow", "wide"), P(None, None, "narrow", "wide"))
    return jax.shard_map(
        per_device, mesh=mesh, in_specs=in_specs, out_specs=out_specs, check_vma=False
    )
```

```python
import functools
import math

import jax
import jax.numpy as jnp
import ml_dtypes
import numpy as np
from jax import lax
from jax.experimental import pallas as pl
from jax.experimental.pallas import tpu as pltpu
from jax.sharding import PartitionSpec as P

K2 = 65536


def with_halo(cells, sides, width):
    for axis, dim in sides:
        count = lax.axis_size(axis)
        head = lax.slice_in_dim(cells, 0, width, axis=dim)
        tail = lax.slice_in_dim(cells, cells.shape[dim] - width, cells.shape[dim], axis=dim)
        cells = jnp.concatenate(
            [
                lax.ppermute(tail, axis, [(i, (i + 1) % count) for i in range(count)]),
                cells,
                lax.ppermute(head, axis, [((i + 1) % count, i) for i in range(count)]),
            ],
            axis=dim,
        )
    return cells


def lagrange_taps(starts, first_out):
    sample_count = starts.shape[0]
    sample = first_out + jnp.arange(sample_count, dtype=jnp.int32)
    excess = sample // 4 - 2 - starts
    offset_u = (sample % 4).astype(jnp.float32) * 0.25 + 2.125 + excess.astype(jnp.float32)
    basis = []
    for node in range(6):
        value = jnp.ones_like(offset_u)
        for other in range(6):
            if other != node:
                value = value * (offset_u - other) / (node - other)
        basis.append(value)
    zeros = jnp.zeros_like(offset_u)
    stacked = []
    for offset in range(7):
        lower = basis[offset - 1] if offset >= 1 else zeros
        upper = basis[offset] if offset <= 5 else zeros
        stacked.append(jnp.where(excess == 0, lower, upper))
    return jnp.stack(stacked).reshape(7, sample_count // 4, 4)


def interpolate(window, tap_weights):
    block_len = tap_weights.shape[1]
    leading = window.shape[:-1]
    flat_rows = window.reshape((-1, window.shape[-1]))
    row_count = flat_rows.shape[0]
    if block_len % 64 == 0 and block_len > 64:
        group = 64
    else:
        group = block_len
    blocks = block_len // group
    taps = tap_weights.reshape(7, blocks, 4 * group)
    if blocks == 1:
        band_rows = flat_rows.shape[1]
        paired = flat_rows[:, None, :]
    else:
        band_rows = 2 * group
        extended = jnp.pad(flat_rows, ((0, 0), (0, (blocks + 1) * group - flat_rows.shape[1])))
        split_rows = extended.reshape(row_count, blocks + 1, group)
        paired = jnp.concatenate([split_rows[:, :-1], split_rows[:, 1:]], axis=2)
    column = jnp.arange(band_rows, dtype=jnp.int32)[None, :, None]
    target = (jnp.arange(4 * group, dtype=jnp.int32) // 4)[None, None, :]
    offsets = jnp.arange(7, dtype=jnp.int32)[:, None, None]
    onehot = (column == target + offsets).astype(jnp.float32)
    band = jnp.einsum("kcj,kbj->bcj", onehot, taps, precision=lax.Precision.HIGHEST)
    total = jnp.einsum(
        "rbc,bcj->rbj", paired.astype(jnp.float32), band, precision=lax.Precision.HIGHEST
    )
    return total.reshape(leading + (4 * block_len,)).astype(jnp.bfloat16)


def directions(first_out, sample_count):
    sample = first_out + jnp.arange(sample_count, dtype=jnp.int32)
    cycles = K2 // 256
    azimuth = 2.0 * math.pi * ((sample % 256).astype(jnp.float32) + 0.5) / 256.0
    polar = math.pi * ((sample // 256).astype(jnp.float32) + 0.5) / cycles
    return (jnp.sin(polar) * jnp.cos(azimuth), jnp.sin(polar) * jnp.sin(azimuth), jnp.cos(polar))


def child_phase(octant, dir_x, dir_y, dir_z):
    sign_x = (octant % 2 * 2 - 1).astype(jnp.float32)
    sign_y = (octant // 2 % 2 * 2 - 1).astype(jnp.float32)
    sign_z = (octant // 4 * 2 - 1).astype(jnp.float32)
    return (
        2.0
        * math.pi
        * 2.0
        * (sign_x[:, None] * dir_x + sign_y[:, None] * dir_y + sign_z[:, None] * dir_z)
    )


def shift_children(pattern, octant, dir_x, dir_y, dir_z):
    angle = child_phase(octant, dir_x, dir_y, dir_z)
    cosine = jnp.cos(angle)[:, None, :]
    sine_part = jnp.sin(angle)[:, None, :]
    real_part = pattern[:, 0].astype(jnp.float32)
    imag_part = pattern[:, 1].astype(jnp.float32)
    return jnp.stack(
        [cosine * real_part - sine_part * imag_part, sine_part * real_part + cosine * imag_part],
        axis=1,
    )


def exchanged(child_pattern, child_parent, child_octant, parent_center, stencil_start):
    n_wide = lax.axis_size("wide")
    box_count, _, sources, block_one = child_pattern.shape
    block_two = 4 * block_one
    piece_len = block_one // n_wide
    narrow_at = lax.axis_index("narrow")
    wide_at = lax.axis_index("wide")
    out_first = narrow_at * block_two + wide_at * (4 * piece_len)
    parent_count = parent_center.shape[0]
    parent_ids = jnp.arange(parent_count, dtype=jnp.int32)
    dir_x, dir_y, dir_z = directions(out_first, 4 * piece_len)
    padded = with_halo(child_pattern, (("narrow", 3),), 3)
    shape_pieces = (box_count, 2, sources, n_wide, piece_len)
    left_rim = padded[..., 0:block_one].reshape(shape_pieces)[..., :3]
    middle = padded[..., 3 : 3 + block_one].reshape(shape_pieces)
    right_rim = padded[..., 6 : 6 + block_one].reshape(shape_pieces)[..., piece_len - 3 :]
    windows = jnp.concatenate([left_rim, middle, right_rim], axis=-1)
    starts = lax.dynamic_slice_in_dim(stencil_start, out_first, 4 * piece_len)
    tap_weights = lagrange_taps(starts, out_first)
    gathered = interpolate(
        lax.all_to_all(windows, "wide", split_axis=3, concat_axis=0, tiled=True)[:, :, :, 0, :],
        tap_weights,
    )
    shifted = shift_children(gathered, child_octant, dir_x, dir_y, dir_z)
    selector = (child_parent[:, None] == parent_ids[None, :]).astype(jnp.float32)
    parents_total = jnp.einsum("bp,bcrj->pcrj", selector, shifted, precision=lax.Precision.HIGHEST)
    center_angle = (
        2.0
        * math.pi
        * (
            parent_center[:, 0:1] * dir_x
            + parent_center[:, 1:2] * dir_y
            + parent_center[:, 2:3] * dir_z
        )
    )
    center_cos = jnp.cos(center_angle)
    center_sin = jnp.sin(center_angle)
    real_sum = jnp.einsum(
        "pj,prj->rj", center_cos, parents_total[:, 0], precision=lax.Precision.HIGHEST
    ) - jnp.einsum("pj,prj->rj", center_sin, parents_total[:, 1], precision=lax.Precision.HIGHEST)
    imag_sum = jnp.einsum(
        "pj,prj->rj", center_sin, parents_total[:, 0], precision=lax.Precision.HIGHEST
    ) + jnp.einsum("pj,prj->rj", center_cos, parents_total[:, 1], precision=lax.Precision.HIGHEST)
    far_field = jnp.stack([real_sum, imag_sum]) / math.sqrt(parent_count)
    parent_pattern = parents_total[:, :, :, None, :]
    return (parent_pattern, far_field[:, :, None, :])


LANES = 128
HALO = 3
RIM = 16


def stencil_tables(window, columns):
    tables = np.zeros((2, window, columns), np.float32)
    for excess in range(2):
        for column in range(columns):
            offset_u = np.float32((column % 4) * 0.25 + 2.125 + excess)
            first = window // 4 + column // 4 - 2 - excess
            for node in range(6):
                value = np.float32(1.0)
                for other in range(6):
                    if other != node:
                        value = np.float32(
                            value * np.float32(np.float32(offset_u - np.float32(other)) / np.float32(node - other))
                        )
                tables[excess, first + node, column] = value
    high = tables.astype(ml_dtypes.bfloat16)
    low = (tables - high.astype(np.float32)).astype(ml_dtypes.bfloat16)
    return np.concatenate([high, low], axis=1)


def shift_of(step, groups):
    half = groups // 2
    return ([0] + [half, *(shift for shift in range(1, groups) if shift != half)][::-1])[step]


def group_after(group, step, groups):
    return (group + shift_of(step, groups)) & (groups - 1)


def group_before(group, step, groups):
    return (group + groups - shift_of(step, groups)) & (groups - 1)


def rim_masks():
    slot = lax.broadcasted_iota(jnp.int32, (RIM, LANES), 0)
    lane = lax.broadcasted_iota(jnp.int32, (RIM, LANES), 1)
    return slot, lane


def as_mask(condition):
    return jnp.where(condition, 1.0, 0.0).astype(jnp.bfloat16)


def rim_of(before, after, first_slot):
    slot, lane = rim_masks()
    slot = slot - first_slot
    pick_before = as_mask((slot >= 0) & (slot < HALO) & (lane == LANES - HALO + slot))
    pick_after = as_mask((slot >= HALO) & (slot < 2 * HALO) & (lane == slot - HALO))
    across = (((1,), (1,)), ((), ()))
    rim = lax.dot_general(pick_before, before, across, preferred_element_type=jnp.float32)
    return rim + lax.dot_general(pick_after, after, across, preferred_element_type=jnp.float32)


def rest_pack_kernel(groups, members, piece, cells, near, *outs):
    boxes, parts, sources, block = cells.shape
    rows = boxes * parts * sources
    tiles = piece // LANES
    wide_at = lax.axis_index("wide")
    group_at, member_at = wide_at // members, wide_at % members

    def tile(ref, at):
        return ref[:, :, :, pl.ds(pl.multiple_of(at, LANES), LANES)].reshape(rows, LANES)

    def rim_at(ref, first):
        return rim_of(tile(ref, jnp.maximum(first - LANES, 0)), tile(ref, jnp.minimum(first + piece, block - LANES)), 0)

    edges = outs[-1]
    for half, ref in enumerate((cells, near)):
        rim = rim_of(tile(ref, block - LANES), tile(ref, 0), 2 * HALO)
        edges[half * RIM : (half + 1) * RIM, :] = rim.astype(jnp.bfloat16)
    for part in range(1, groups):
        for swap in range(2, members, 2):
            out, base = outs[(part - 1) * (members // 2 - 1) + swap // 2 - 1], 0
            target = member_at ^ swap
            first = (group_after(group_at, groups - 1 - part, groups) * members + target) * piece
            for ref in (cells, near):
                for index in range(tiles):
                    out[base : base + rows, :] = tile(ref, first + index * LANES)
                    base += rows
                out[base : base + RIM, :] = rim_at(ref, first).astype(jnp.bfloat16)
                base += RIM
                if part == 1:
                    rim = rim_at(ref, (group_after(group_at, groups - 1, groups) * members + target) * piece)
                    out[base : base + RIM, :] = rim.astype(jnp.bfloat16)
                    base += RIM


def turned(cycles):
    half = math.pi * (cycles - jnp.floor(cycles + 0.5))
    square = half * half
    sine, cosine = jnp.zeros_like(half), jnp.zeros_like(half)
    for order in range(13, 0, -2):
        sine = sine * square + (-1) ** (order // 2) / math.factorial(order)
        cosine = cosine * square + (-1) ** (order // 2) / math.factorial(order - 1)
    sine = sine * half
    return 1.0 - 2.0 * sine * sine, 2.0 * sine * cosine


def axes_kernel(groups, members, piece, sample_count, cosines, sines, center_dirs):
    wide_at = lax.axis_index("wide")
    group_at, member_at = wide_at // members, wide_at % members
    rows = 4 * piece // LANES
    half_rows = sample_count // LANES // lax.axis_size("narrow")
    row = lax.broadcasted_iota(jnp.int32, (rows, LANES), 0)
    lane = lax.broadcasted_iota(jnp.int32, (rows, LANES), 1)
    cos_azimuth, sin_azimuth = turned((((row * LANES + lane) & 255).astype(jnp.float32) + 0.5) / 256.0)
    for step in range(groups):
        at = group_after(group_at, step, groups) * members + member_at
        first_row = lax.axis_index("narrow") * half_rows + at * rows
        ring = ((first_row + row) * LANES + lane) >> 8
        dir_z, sin_polar = turned((ring.astype(jnp.float32) + 0.5) / (2 * (sample_count // 256)))
        for axis, direction in enumerate((sin_polar * cos_azimuth, sin_polar * sin_azimuth, dir_z)):
            cosines[step, axis], sines[step, axis] = turned(2.0 * direction)
            if step == 0:
                center_dirs[axis] = direction


def prep_kernel(
    groups, members, boxes, piece, parent_of, octant_of, center, starts, axis_cos, axis_sin, center_dirs,
    cosines, sines, center_cos, center_sin, excess, held, sems,
):
    wide_at = lax.axis_index("wide")
    group_at, member_at = wide_at // members, wide_at % members
    rows = 4 * piece // LANES
    half_rows = starts.shape[0] // lax.axis_size("narrow")
    row = lax.broadcasted_iota(jnp.int32, (rows, LANES), 0)
    lane = lax.broadcasted_iota(jnp.int32, (rows, LANES), 1)
    first_rows = [
        pl.multiple_of(
            lax.axis_index("narrow") * half_rows + (group_after(group_at, step, groups) * members + member_at) * rows, 8
        )
        for step in range(groups)
    ]
    copies = [
        pltpu.make_async_copy(starts.at[pl.ds(first_rows[step], rows)], held.at[step], sems.at[step]) for step in range(groups)
    ]
    for copy in copies:
        copy.start()
    scale = 1.0 / math.sqrt(center.shape[0])
    for step in range(groups):
        parent = parent_of[group_before(group_at, step, groups) * members * boxes]
        turns = sum(center[parent, axis] * center_dirs[axis] for axis in range(3))
        turn_cos, turn_sin = turned(turns)
        center_cos[step] = turn_cos * scale
        center_sin[step] = turn_sin * scale
    for step in range(groups):
        (cos_x, cos_y, cos_z), (sin_x, sin_y, sin_z) = ([table[step, axis] for axis in range(3)] for table in (axis_cos, axis_sin))
        both_cos, both_sin, sin_cos, cos_sin = cos_x * cos_y, sin_x * sin_y, sin_x * cos_y, cos_x * sin_y
        for swap in range(members):
            for box in range(boxes):
                slot = (group_at * members + (member_at ^ swap)) * boxes + box
                octant = octant_of[slot]
                live = jnp.where(parent_of[slot] >= 0, 1.0, 0.0)
                sign_x = ((octant & 1) * 2 - 1).astype(jnp.float32)
                sign_y = (((octant >> 1) & 1) * 2 - 1).astype(jnp.float32)
                sign_z = ((octant >> 2) * 2 - 1).astype(jnp.float32)
                real = both_cos - (sign_x * sign_y) * both_sin
                imag = sign_x * sin_cos + sign_y * cos_sin
                turn_cos, turn_sin = live * cos_z, (live * sign_z) * sin_z
                cosines[step, swap * boxes + box] = real * turn_cos - imag * turn_sin
                sines[step, swap * boxes + box] = real * turn_sin + imag * turn_cos
    for step in range(groups):
        copies[step].wait()
        child = ((first_rows[step] + row) * LANES + lane) >> 2
        excess[step] = (child - 2 - held[step]).astype(jnp.float32)


def columns_of(windows):
    return [2 * window + half for window in windows for half in range(2)]


def combine_kernel(jobs, members, boxes, sources, tiles, count, *refs):
    data = refs[:count]
    cosines, sines, excess, band_zero, band_one = refs[count : count + 5]
    *outs, spread, total = refs[count + 5 :]
    for (step, *job), out in zip(jobs, outs):
        combine(
            step, *job, members, boxes, sources, tiles, data, cosines.at[step], sines.at[step], excess.at[step],
            band_zero, band_one, out, spread, total,
        )


def combine(
    step, windows, places, rims, members, boxes, sources, tiles, data, cosines, sines, excess, band_zero, band_one, out, spread, total
):
    rows = boxes * 2 * sources
    block = data[0].shape[3]
    wide_at = lax.axis_index("wide")
    last = lax.axis_size("wide") - 1
    groups = lax.axis_size("wide") // members
    at = group_after(wide_at // members, step, groups) * members + wide_at % members
    first = at * (tiles * LANES)

    def local(ref, lane):
        return ref[:, :, :, pl.ds(pl.multiple_of(lane, LANES), LANES)].reshape(rows, LANES)

    def tile(index):
        if index < 0 or index >= tiles:
            return rim_tile
        found = [local(data[member], first + index * LANES) for member in range(2)]
        for which, base in places:
            ref = data[which]
            if len(ref.shape) == 4:
                found.append(ref[:, :, :, index * LANES : (index + 1) * LANES].reshape(rows, LANES))
            else:
                found.append(ref[base + index * rows : base + (index + 1) * rows, :])
        return jnp.concatenate(found, axis=0)

    if rims is not None:
        slot, lane = rim_masks()
        from_other = slot >= 2 * HALO
        side = jnp.where(from_other, slot - 2 * HALO, slot)
        outer = ((side < HALO) & (at == 0)) | ((side >= HALO) & (at == last))
        keep = (outer == from_other) & (slot < 4 * HALO)
        place = as_mask(
            ((side < HALO) & (lane == LANES - HALO + side)) | ((side >= HALO) & (side < 2 * HALO) & (lane == side - HALO))
        )
        found = []
        for inner, (other, other_row) in rims:
            outside = data[other][other_row : other_row + RIM, :].astype(jnp.float32)
            if inner is None:
                inside = jnp.zeros((RIM, LANES), jnp.float32)
            else:
                inside = data[inner[0]][inner[1] : inner[1] + RIM, :].astype(jnp.float32)
            found.append(jnp.where(keep, jnp.where(from_other, outside, inside), 0.0).astype(jnp.bfloat16))
        rim = jnp.concatenate(found, axis=1)
        rim_tile = lax.dot_general(rim, place, (((0,), (0,)), ((), ())), preferred_element_type=jnp.float32)
        lane = lax.broadcasted_iota(jnp.int32, (rows, LANES), 1)
        from_before = (lane >= LANES - HALO) & (at != 0)
        from_after = (lane < HALO) & (at != last)
        near = []
        for member in range(2):
            before = local(data[member], jnp.maximum(first - LANES, 0)).astype(jnp.float32)
            after = local(data[member], jnp.minimum(first + tiles * LANES, block - LANES)).astype(jnp.float32)
            near.append(jnp.where(from_before, before, jnp.where(from_after, after, 0.0)))
        near = jnp.concatenate(near, axis=0)
        rim_tile = jnp.concatenate([rim_tile[: 2 * rows] + near, rim_tile[2 * rows :]], axis=0).astype(jnp.bfloat16)

    def window_of(window):
        cut = 32 if window % 2 else 96
        left, right = tile((window - 1 + window % 2) // 2), tile((window + 1) // 2)
        cells = jnp.concatenate([left[:, cut:], right[:, :cut]], axis=1)
        return jnp.concatenate([cells, cells], axis=1)

    columns = columns_of(windows)
    width = len(columns)
    whole = width == 4 * tiles

    def spread_window(turn):
        bands = []
        for half, column in enumerate(columns[2 * turn : 2 * turn + 2]):
            which = jnp.broadcast_to(excess[column : column + 1, :], (16, LANES)).astype(jnp.bfloat16)
            which = jnp.concatenate([which] * (band_zero.shape[0] // 16), axis=0)
            lanes = slice(half * LANES, (half + 1) * LANES)
            bands.append(band_zero[:, lanes] * (1 - which) + band_one[:, lanes] * which)
        spread[turn % 2] = jnp.dot(
            window_of(windows[turn]), jnp.concatenate(bands, axis=1), preferred_element_type=jnp.float32
        )

    def sum_window(turn):
        for half, column in enumerate(columns[2 * turn : 2 * turn + 2]):
            lanes = slice(half * LANES, (half + 1) * LANES)
            real_sum = jnp.zeros((sources, LANES), jnp.float32)
            imag_sum = jnp.zeros((sources, LANES), jnp.float32)
            for child in range(members * boxes):
                start = child * 2 * sources
                real = spread[turn % 2, start : start + sources, lanes].astype(jnp.bfloat16).astype(jnp.float32)
                imag = spread[turn % 2, start + sources : start + 2 * sources, lanes]
                imag = imag.astype(jnp.bfloat16).astype(jnp.float32)
                cosine = cosines[child, column : column + 1, :]
                sine = sines[child, column : column + 1, :]
                real_sum = real_sum + (cosine * real - sine * imag)
                imag_sum = imag_sum + (sine * real + cosine * imag)
            if whole:
                total[pl.ds(column, sources, stride=width), :] = real_sum
                total[pl.ds(sources * width + column, sources, stride=width), :] = imag_sum
            else:
                at_row = (2 * turn + half) * 2 * sources
                out[at_row : at_row + sources, :] = real_sum.astype(out.dtype)
                out[at_row + sources : at_row + 2 * sources, :] = imag_sum.astype(out.dtype)

    for turn in range(len(windows) + 1):
        if turn < len(windows):
            spread_window(turn)
        if turn:
            sum_window(turn - 1)
    if whole:
        out[...] = total[...].astype(out.dtype)


def place_columns(arrived, columns, sources, rows, cosines, sines, pattern, far):
    for index, column in enumerate(columns):
        real, imag = (
            arrived[pl.ds((2 * index + half) * sources, sources), :].astype(jnp.float32) for half in range(2)
        )
        at = pl.ds(column, sources, stride=rows)
        pattern[0, at, :] = real
        pattern[1, at, :] = imag
        cosine, sine = cosines[column : column + 1, :], sines[column : column + 1, :]
        far[0, at, :] += cosine * real - sine * imag
        far[1, at, :] += sine * real + cosine * imag


def finish_ahead_kernel(steps, early_step, columns, members, boxes, sources, rows, parent_of, *refs):
    whole, (early, center_cos, center_sin, parent_out, far_out, early_out) = refs[: len(steps)], refs[len(steps) :]
    groups = lax.axis_size("wide") // members
    group_at = lax.axis_index("wide") // members
    names = [parent_of[group_before(group_at, step, groups) * members * boxes] for step in steps]
    for source in range(sources):
        at = pl.ds(source * rows, rows)
        far_real = far_imag = 0.0
        for index, step in enumerate(steps):
            real, imag = (
                whole[index][pl.ds((half * sources + source) * rows, rows), :].astype(jnp.float32) for half in range(2)
            )
            cosine, sine = center_cos[step], center_sin[step]
            parent_out[names[index], 0, at, :] = real
            parent_out[names[index], 1, at, :] = imag
            far_real = far_real + (cosine * real - sine * imag)
            far_imag = far_imag + (sine * real + cosine * imag)
        far_out[0, at, :] = far_real
        far_out[1, at, :] = far_imag
    place_columns(
        early, columns, sources, rows, center_cos.at[early_step], center_sin.at[early_step], early_out, far_out
    )


def join_kernel(steps, early_step, columns, members, boxes, sources, rows, parent_of, *refs):
    whole, refs = refs[: len(steps)], refs[len(steps) :]
    late, early, center_cos, center_sin, far_in, _, parent_out, far_out, names, patterns, name_sem, sems = refs
    name_copy = pltpu.make_async_copy(parent_of, names, name_sem)
    name_copy.start()
    last = len(steps)
    groups = lax.axis_size("wide") // members
    group_at = lax.axis_index("wide") // members
    copies = []

    def send(index, step):
        name = names[group_before(group_at, step, groups) * members * boxes]
        copies.append(pltpu.make_async_copy(patterns.at[index], parent_out.at[name], sems.at[index]))
        copies[-1].start()

    patterns[last] = early[...]
    far_out[...] = far_in[...]
    place_columns(
        late, columns, sources, rows, center_cos.at[early_step], center_sin.at[early_step], patterns.at[last], far_out
    )
    name_copy.wait()
    send(last, early_step)
    for index, step in enumerate(steps):
        cosine, sine = center_cos[step], center_sin[step]
        for source in range(sources):
            at = pl.ds(source * rows, rows)
            real, imag = (
                whole[index][pl.ds((half * sources + source) * rows, rows), :].astype(jnp.float32) for half in range(2)
            )
            patterns[index, 0, at, :] = real
            patterns[index, 1, at, :] = imag
            far_out[0, at, :] += cosine * real - sine * imag
            far_out[1, at, :] += sine * real + cosine * imag
        send(index, step)
    for copy in copies:
        copy.wait()


def finish_kernel(steps, members, boxes, sources, rows, parts, parent_of, *refs):
    whole, refs = refs[: len(steps)], refs[len(steps) :]
    center_cos, center_sin, far_in, _, parent_out, far_out, names, held, far_held, name_sem, sems = refs
    name_copy = pltpu.make_async_copy(parent_of, names, name_sem)
    name_copy.start()
    group_at = lax.axis_index("wide") // members
    copies = []

    def send(source, target):
        copies.append(pltpu.make_async_copy(source, target, sems.at[len(copies)]))
        copies[-1].start()

    last = len(steps)
    name_copy.wait()
    groups = lax.axis_size("wide") // members
    places = [names[group_before(group_at, step, groups) * members * boxes] for step in steps]
    each = sources // parts
    for part in range(parts):
        for source in range(part * each, (part + 1) * each):
            at = pl.ds(source * rows, rows)
            far_real, far_imag = far_in[0, at, :], far_in[1, at, :]
            for index, step in enumerate(steps):
                real, imag = (
                    whole[index][pl.ds((half * sources + source) * rows, rows), :].astype(jnp.float32) for half in range(2)
                )
                cosine, sine = center_cos[step], center_sin[step]
                held[index, 0, at, :] = real
                held[index, 1, at, :] = imag
                far_real = far_real + (cosine * real - sine * imag)
                far_imag = far_imag + (sine * real + cosine * imag)
            far_held[0, at, :] = far_real
            far_held[1, at, :] = far_imag
        at = pl.ds(part * each * rows, each * rows)
        for index in range(last):
            send(held.at[index, :, at], parent_out.at[places[index], :, at])
        send(far_held.at[:, at], far_out.at[:, at])
    for copy in copies:
        copy.wait()


def grouped(child_pattern, child_parent, child_octant, parent_center, stencil_start, members):
    n_wide = lax.axis_size("wide")
    boxes, _, sources, block = child_pattern.shape
    groups = n_wide // members
    piece = block // n_wide
    tiles = piece // LANES
    rows = boxes * 2 * sources
    out_rows = 4 * tiles
    parents = parent_center.shape[0]
    vmem = pl.BlockSpec(memory_space=pltpu.VMEM)
    smem = pl.BlockSpec(memory_space=pltpu.SMEM)
    hbm = pl.BlockSpec(memory_space=pltpu.HBM)
    limit = pltpu.CompilerParams(vmem_limit_bytes=16 * 1024 * 1024)

    def cost(micros):
        return pl.CostEstimate(flops=int(micros * 1e9), bytes_accessed=int(micros * 3.6e6) + 1, transcendentals=0)


    def bf16(*shape):
        return jax.ShapeDtypeStruct(shape, jnp.bfloat16)

    def f32(*shape):
        return jax.ShapeDtypeStruct(shape, jnp.float32)

    def swap_with(array, step):
        return lax.ppermute(array, "wide", [(i, i ^ step) for i in range(n_wide)])

    def move_by(array, step):
        shift = shift_of(step, groups) * members
        return lax.ppermute(array, "wide", [(i, (i + shift) % n_wide) for i in range(n_wide)])

    def tie(*arrays):
        return lax.optimization_barrier(arrays)

    far = members - 2
    wide_at = lax.axis_index("wide")
    heads = []
    for swap in range(2, members):
        first = (wide_at ^ (groups // 2 * members + swap)) * piece
        heads.append(lax.dynamic_slice_in_dim(child_pattern, first, piece, 3))
    near = swap_with(child_pattern, 1)
    heads = [swap_with(head, swap + 2) for swap, head in enumerate(heads)]

    def other_half(array, step):
        pairs = [(i * 2 + n, (i ^ step) * 2 + 1 - n) for i in range(n_wide) for n in range(2)]
        return lax.ppermute(array, ("wide", "narrow"), pairs)

    axes = pl.pallas_call(
        functools.partial(axes_kernel, groups, members, piece, stencil_start.shape[0]),
        out_shape=[f32(groups, 3, out_rows, LANES)] * 2 + [f32(3, out_rows, LANES)],
        out_specs=[vmem] * 3,
        compiler_params=limit,
        cost_estimate=cost(1),
        name="axes",
    )()
    tables = pl.pallas_call(
        functools.partial(prep_kernel, groups, members, boxes, piece),
        out_shape=[
            f32(groups, members * boxes, out_rows, LANES),
            f32(groups, members * boxes, out_rows, LANES),
            f32(parents, out_rows, LANES),
            f32(parents, out_rows, LANES),
            f32(groups, out_rows, LANES),
        ],
        in_specs=[smem, smem, smem, hbm] + [vmem] * 3,
        out_specs=[vmem] * 5,
        scratch_shapes=[pltpu.VMEM((groups, out_rows, LANES), jnp.int32), pltpu.SemaphoreType.DMA((groups,))],
        compiler_params=limit,
            cost_estimate=cost(1),
        name="prep",
    )(child_parent, child_octant, parent_center, stencil_start.reshape(-1, LANES), *axes)
    cosines, sines, center_cos, center_sin, excess = tables
    full = tiles * rows + RIM
    pairs = members // 2 - 1
    *sends, edges = pl.pallas_call(
        functools.partial(rest_pack_kernel, groups, members, piece),
        out_shape=[
            bf16(2 * (full + (RIM if part == 1 else 0)), LANES) for part in range(1, groups) for _ in range(pairs)
        ]
        + [bf16(2 * RIM, LANES)],
        in_specs=[vmem] * 2,
        out_specs=[vmem] * ((groups - 1) * pairs + 1),
        compiler_params=limit,
        cost_estimate=cost(1),
        name="pack",
    )(child_pattern, near)
    common = [other_half(edges, 2 * pair) for pair in range(pairs + 1)]
    bands = stencil_tables(LANES, 2 * LANES)

    top = groups - 1

    def sums_of(jobs, data, dtype, micros):
        shapes = [jax.ShapeDtypeStruct((2 * sources * len(columns_of(job[1])), LANES), dtype) for job in jobs]
        inputs = [*data, cosines, sines, excess, bands[0], bands[1]]
        return pl.pallas_call(
            functools.partial(combine_kernel, jobs, members, boxes, sources, tiles, len(data)),
            out_shape=shapes,
            in_specs=[vmem] * len(inputs),
            out_specs=[vmem] * len(shapes),
            scratch_shapes=[
                pltpu.VMEM((2, members * rows, 2 * LANES), jnp.float32),
                pltpu.VMEM((2 * sources * out_rows, LANES), jnp.float32),
            ],
            compiler_params=limit,
            cost_estimate=cost(micros),
            name="combine",
        )(*inputs)

    inner = list(range(1, 2 * tiles - 1))
    outer = [0, 2 * tiles - 1]
    every = list(range(2 * tiles))
    locals_ = [child_pattern, near]
    first_data = locals_ + heads
    first_places = [(2 + member, 0) for member in range(far)]
    (total,) = sums_of([(top, inner, first_places, None)], first_data, jnp.bfloat16, 5)
    early_sends = sends[pairs : 2 * pairs]
    *early_sends, total = tie(*early_sends, total)
    sends[pairs : 2 * pairs] = early_sends
    done = [move_by(total, top)]
    arrived = {}
    for part in range(1, groups):
        step = top - part
        sent = sends[(part - 1) * pairs : part * pairs]
        if part > 1:
            totals = list(sums_of(jobs, data, jnp.bfloat16, 30 if part == 2 else 2))
            if part < groups - 1:
                tied = tie(*sends[part * pairs : (part + 1) * pairs], *totals)
                sends[part * pairs : (part + 1) * pairs], totals = tied[:pairs], list(tied[pairs:])
            arrived[step + 1] = move_by(totals[0], step + 1)
            if part == 2:
                done.append(move_by(totals[1], top))
        got = [swap_with(array, 2 * pair + 2) for pair, array in enumerate(sent)]
        length = full + (RIM if part == 1 else 0)
        places = [(2 + member // 2, member % 2 * length) for member in range(far)]
        data = locals_ + got + common
        shift = 2 + pairs
        edge_at = [(shift + member // 2, member % 2 * RIM) for member in range(members)]
        rims = [None, None] + [(which, row + tiles * rows) for which, row in places]
        jobs = [(step, every, places, list(zip(rims, edge_at)))]
        if part == 1:
            rims = [None, None] + [(which, row + full) for which, row in places]
            outer_places = [(len(data) + member, 0) for member in range(far)]
            jobs.append((top, outer, outer_places, list(zip(rims, edge_at))))
            data = data + heads
    data[0], done[0] = tie(data[0], done[0])
    (arrived[0],) = sums_of(jobs, data, jnp.float32, 0)
    done = [(top, columns_of(inner), done[0]), (top, columns_of(outer), done[1])]
    held = arrived
    whole = f32(2, sources * out_rows, LANES)
    (_, early_columns, early_array), (_, late_columns, late_array) = done
    ahead = [0]
    parent_pattern, far_field, early_pattern = pl.pallas_call(
        functools.partial(finish_ahead_kernel, ahead, top, early_columns, members, boxes, sources, out_rows),
        out_shape=[f32(parents, *whole.shape), whole, whole],
        in_specs=[smem] + [vmem] * (len(ahead) + 3),
        out_specs=[vmem] * 3,
        compiler_params=limit,
        cost_estimate=cost(0),
        name="finish_ahead",
    )(child_parent, *[held[step] for step in ahead], early_array, center_cos, center_sin)
    between = list(range(2, top))
    parent_pattern, far_field = pl.pallas_call(
        functools.partial(join_kernel, between, top, late_columns, members, boxes, sources, out_rows),
        out_shape=[f32(parents, *whole.shape), whole],
        in_specs=[hbm] + [vmem] * (len(between) + 5) + [hbm],
        out_specs=[hbm, vmem],
        input_output_aliases={len(between) + 6: 0},
        scratch_shapes=[
            pltpu.SMEM(child_parent.shape, jnp.int32),
            pltpu.VMEM((len(between) + 1, *whole.shape), jnp.float32),
            pltpu.SemaphoreType.DMA,
            pltpu.SemaphoreType.DMA((len(between) + 1,)),
        ],
        compiler_params=limit,
        cost_estimate=cost(5),
        name="join",
    )(
        child_parent, *[held[step] for step in between], late_array, early_pattern, center_cos, center_sin, far_field,
        parent_pattern,
    )
    steps = [1]
    parts = 4
    parent_pattern, far_field = pl.pallas_call(
        functools.partial(finish_kernel, steps, members, boxes, sources, out_rows, parts),
        out_shape=[f32(parents, *whole.shape), whole],
        in_specs=[hbm] + [vmem] * (len(steps) + 3) + [hbm],
        out_specs=[hbm, hbm],
        input_output_aliases={len(steps) + 4: 0},
        scratch_shapes=[
            pltpu.SMEM(child_parent.shape, jnp.int32),
            pltpu.VMEM((len(steps), *whole.shape), jnp.float32),
            pltpu.VMEM(whole.shape, jnp.float32),
            pltpu.SemaphoreType.DMA,
            pltpu.SemaphoreType.DMA((parts * (len(steps) + 1),)),
        ],
        compiler_params=limit,
        cost_estimate=cost(30),
        name="finish_last",
    )(child_parent, *[held[step] for step in steps], center_cos, center_sin, far_field, parent_pattern)
    return (
        parent_pattern.reshape(parents, 2, sources, 1, 4 * piece),
        far_field.reshape(2, sources, 1, 4 * piece),
    )


def power_of_two(number):
    return number > 0 and number & (number - 1) == 0


def per_device(child_pattern, child_parent, child_octant, parent_center, stencil_start):
    n_wide, n_narrow = lax.axis_size("wide"), lax.axis_size("narrow")
    boxes, _, sources, block = child_pattern.shape
    parents = parent_center.shape[0]
    run = child_parent.shape[0] // parents
    if run % boxes == 0 and block % n_wide == 0:
        members = run // boxes
        fits = (
            n_narrow == 2
            and n_wide == members * parents
            and power_of_two(members)
            and power_of_two(parents)
            and members >= 4
            and parents >= 4
            and block // n_wide % LANES == 0
            and block // n_wide // LANES >= 3
            and boxes * 2 * sources == LANES
            and sources % 16 == 0
            and stencil_start.shape[0] == 4 * block * n_narrow
        )
        if fits:
            return grouped(child_pattern, child_parent, child_octant, parent_center, stencil_start, members)
    return exchanged(child_pattern, child_parent, child_octant, parent_center, stencil_start)


def solution(mesh):
    in_specs = (P("wide", None, None, "narrow"), P(), P(), P(), P())
    out_specs = (P(None, None, None, "narrow", "wide"), P(None, None, "narrow", "wide"))
    return jax.shard_map(
        per_device, mesh=mesh, in_specs=in_specs, out_specs=out_specs, check_vma=False
    )
```

```python
import functools
import math

import jax
import jax.numpy as jnp
import ml_dtypes
import numpy as np
from jax import lax
from jax.experimental import pallas as pl
from jax.experimental.pallas import tpu as pltpu
from jax.sharding import PartitionSpec as P

K2 = 65536


def with_halo(cells, sides, width):
    for axis, dim in sides:
        count = lax.axis_size(axis)
        head = lax.slice_in_dim(cells, 0, width, axis=dim)
        tail = lax.slice_in_dim(cells, cells.shape[dim] - width, cells.shape[dim], axis=dim)
        cells = jnp.concatenate(
            [
                lax.ppermute(tail, axis, [(i, (i + 1) % count) for i in range(count)]),
                cells,
                lax.ppermute(head, axis, [((i + 1) % count, i) for i in range(count)]),
            ],
            axis=dim,
        )
    return cells


def lagrange_taps(starts, first_out):
    sample_count = starts.shape[0]
    sample = first_out + jnp.arange(sample_count, dtype=jnp.int32)
    excess = sample // 4 - 2 - starts
    offset_u = (sample % 4).astype(jnp.float32) * 0.25 + 2.125 + excess.astype(jnp.float32)
    basis = []
    for node in range(6):
        value = jnp.ones_like(offset_u)
        for other in range(6):
            if other != node:
                value = value * (offset_u - other) / (node - other)
        basis.append(value)
    zeros = jnp.zeros_like(offset_u)
    stacked = []
    for offset in range(7):
        lower = basis[offset - 1] if offset >= 1 else zeros
        upper = basis[offset] if offset <= 5 else zeros
        stacked.append(jnp.where(excess == 0, lower, upper))
    return jnp.stack(stacked).reshape(7, sample_count // 4, 4)


def interpolate(window, tap_weights):
    block_len = tap_weights.shape[1]
    leading = window.shape[:-1]
    flat_rows = window.reshape((-1, window.shape[-1]))
    row_count = flat_rows.shape[0]
    if block_len % 64 == 0 and block_len > 64:
        group = 64
    else:
        group = block_len
    blocks = block_len // group
    taps = tap_weights.reshape(7, blocks, 4 * group)
    if blocks == 1:
        band_rows = flat_rows.shape[1]
        paired = flat_rows[:, None, :]
    else:
        band_rows = 2 * group
        extended = jnp.pad(flat_rows, ((0, 0), (0, (blocks + 1) * group - flat_rows.shape[1])))
        split_rows = extended.reshape(row_count, blocks + 1, group)
        paired = jnp.concatenate([split_rows[:, :-1], split_rows[:, 1:]], axis=2)
    column = jnp.arange(band_rows, dtype=jnp.int32)[None, :, None]
    target = (jnp.arange(4 * group, dtype=jnp.int32) // 4)[None, None, :]
    offsets = jnp.arange(7, dtype=jnp.int32)[:, None, None]
    onehot = (column == target + offsets).astype(jnp.float32)
    band = jnp.einsum("kcj,kbj->bcj", onehot, taps, precision=lax.Precision.HIGHEST)
    total = jnp.einsum(
        "rbc,bcj->rbj", paired.astype(jnp.float32), band, precision=lax.Precision.HIGHEST
    )
    return total.reshape(leading + (4 * block_len,)).astype(jnp.bfloat16)


def directions(first_out, sample_count):
    sample = first_out + jnp.arange(sample_count, dtype=jnp.int32)
    cycles = K2 // 256
    azimuth = 2.0 * math.pi * ((sample % 256).astype(jnp.float32) + 0.5) / 256.0
    polar = math.pi * ((sample // 256).astype(jnp.float32) + 0.5) / cycles
    return (jnp.sin(polar) * jnp.cos(azimuth), jnp.sin(polar) * jnp.sin(azimuth), jnp.cos(polar))


def child_phase(octant, dir_x, dir_y, dir_z):
    sign_x = (octant % 2 * 2 - 1).astype(jnp.float32)
    sign_y = (octant // 2 % 2 * 2 - 1).astype(jnp.float32)
    sign_z = (octant // 4 * 2 - 1).astype(jnp.float32)
    return (
        2.0
        * math.pi
        * 2.0
        * (sign_x[:, None] * dir_x + sign_y[:, None] * dir_y + sign_z[:, None] * dir_z)
    )


def shift_children(pattern, octant, dir_x, dir_y, dir_z):
    angle = child_phase(octant, dir_x, dir_y, dir_z)
    cosine = jnp.cos(angle)[:, None, :]
    sine_part = jnp.sin(angle)[:, None, :]
    real_part = pattern[:, 0].astype(jnp.float32)
    imag_part = pattern[:, 1].astype(jnp.float32)
    return jnp.stack(
        [cosine * real_part - sine_part * imag_part, sine_part * real_part + cosine * imag_part],
        axis=1,
    )


def exchanged(child_pattern, child_parent, child_octant, parent_center, stencil_start):
    n_wide = lax.axis_size("wide")
    box_count, _, sources, block_one = child_pattern.shape
    block_two = 4 * block_one
    piece_len = block_one // n_wide
    narrow_at = lax.axis_index("narrow")
    wide_at = lax.axis_index("wide")
    out_first = narrow_at * block_two + wide_at * (4 * piece_len)
    parent_count = parent_center.shape[0]
    parent_ids = jnp.arange(parent_count, dtype=jnp.int32)
    dir_x, dir_y, dir_z = directions(out_first, 4 * piece_len)
    padded = with_halo(child_pattern, (("narrow", 3),), 3)
    shape_pieces = (box_count, 2, sources, n_wide, piece_len)
    left_rim = padded[..., 0:block_one].reshape(shape_pieces)[..., :3]
    middle = padded[..., 3 : 3 + block_one].reshape(shape_pieces)
    right_rim = padded[..., 6 : 6 + block_one].reshape(shape_pieces)[..., piece_len - 3 :]
    windows = jnp.concatenate([left_rim, middle, right_rim], axis=-1)
    starts = lax.dynamic_slice_in_dim(stencil_start, out_first, 4 * piece_len)
    tap_weights = lagrange_taps(starts, out_first)
    gathered = interpolate(
        lax.all_to_all(windows, "wide", split_axis=3, concat_axis=0, tiled=True)[:, :, :, 0, :],
        tap_weights,
    )
    shifted = shift_children(gathered, child_octant, dir_x, dir_y, dir_z)
    selector = (child_parent[:, None] == parent_ids[None, :]).astype(jnp.float32)
    parents_total = jnp.einsum("bp,bcrj->pcrj", selector, shifted, precision=lax.Precision.HIGHEST)
    center_angle = (
        2.0
        * math.pi
        * (
            parent_center[:, 0:1] * dir_x
            + parent_center[:, 1:2] * dir_y
            + parent_center[:, 2:3] * dir_z
        )
    )
    center_cos = jnp.cos(center_angle)
    center_sin = jnp.sin(center_angle)
    real_sum = jnp.einsum(
        "pj,prj->rj", center_cos, parents_total[:, 0], precision=lax.Precision.HIGHEST
    ) - jnp.einsum("pj,prj->rj", center_sin, parents_total[:, 1], precision=lax.Precision.HIGHEST)
    imag_sum = jnp.einsum(
        "pj,prj->rj", center_sin, parents_total[:, 0], precision=lax.Precision.HIGHEST
    ) + jnp.einsum("pj,prj->rj", center_cos, parents_total[:, 1], precision=lax.Precision.HIGHEST)
    far_field = jnp.stack([real_sum, imag_sum]) / math.sqrt(parent_count)
    parent_pattern = parents_total[:, :, :, None, :]
    return (parent_pattern, far_field[:, :, None, :])


LANES = 128
HALO = 3
RIM = 16


def stencil_tables(window, columns):
    tables = np.zeros((2, window, columns), np.float32)
    for excess in range(2):
        for column in range(columns):
            offset_u = np.float32((column % 4) * 0.25 + 2.125 + excess)
            first = window // 4 + column // 4 - 2 - excess
            for node in range(6):
                value = np.float32(1.0)
                for other in range(6):
                    if other != node:
                        value = np.float32(
                            value * np.float32(np.float32(offset_u - np.float32(other)) / np.float32(node - other))
                        )
                tables[excess, first + node, column] = value
    high = tables.astype(ml_dtypes.bfloat16)
    low = (tables - high.astype(np.float32)).astype(ml_dtypes.bfloat16)
    return np.concatenate([high, low], axis=1)


def shift_of(step, groups):
    half = groups // 2
    return ([0] + [half, *(shift for shift in range(1, groups) if shift != half)][::-1])[step]


def group_after(group, step, groups):
    return (group + shift_of(step, groups)) & (groups - 1)


def group_before(group, step, groups):
    return (group + groups - shift_of(step, groups)) & (groups - 1)


def rim_masks():
    slot = lax.broadcasted_iota(jnp.int32, (RIM, LANES), 0)
    lane = lax.broadcasted_iota(jnp.int32, (RIM, LANES), 1)
    return slot, lane


def as_mask(condition):
    return jnp.where(condition, 1.0, 0.0).astype(jnp.bfloat16)


def rim_of(before, after, first_slot):
    slot, lane = rim_masks()
    slot = slot - first_slot
    pick_before = as_mask((slot >= 0) & (slot < HALO) & (lane == LANES - HALO + slot))
    pick_after = as_mask((slot >= HALO) & (slot < 2 * HALO) & (lane == slot - HALO))
    across = (((1,), (1,)), ((), ()))
    rim = lax.dot_general(pick_before, before, across, preferred_element_type=jnp.float32)
    return rim + lax.dot_general(pick_after, after, across, preferred_element_type=jnp.float32)


def rest_pack_kernel(groups, members, piece, cells, near, *outs):
    boxes, parts, sources, block = cells.shape
    rows = boxes * parts * sources
    tiles = piece // LANES
    wide_at = lax.axis_index("wide")
    group_at, member_at = wide_at // members, wide_at % members

    def tile(ref, at):
        return ref[:, :, :, pl.ds(pl.multiple_of(at, LANES), LANES)].reshape(rows, LANES)

    def rim_at(ref, first):
        return rim_of(tile(ref, jnp.maximum(first - LANES, 0)), tile(ref, jnp.minimum(first + piece, block - LANES)), 0)

    edges = outs[-1]
    for half, ref in enumerate((cells, near)):
        rim = rim_of(tile(ref, block - LANES), tile(ref, 0), 2 * HALO)
        edges[half * RIM : (half + 1) * RIM, :] = rim.astype(jnp.bfloat16)
    for part in range(1, groups):
        for swap in range(2, members, 2):
            out, base = outs[(part - 1) * (members // 2 - 1) + swap // 2 - 1], 0
            target = member_at ^ swap
            first = (group_after(group_at, groups - 1 - part, groups) * members + target) * piece
            for ref in (cells, near):
                for index in range(tiles):
                    out[base : base + rows, :] = tile(ref, first + index * LANES)
                    base += rows
                out[base : base + RIM, :] = rim_at(ref, first).astype(jnp.bfloat16)
                base += RIM
                if part == 1:
                    rim = rim_at(ref, (group_after(group_at, groups - 1, groups) * members + target) * piece)
                    out[base : base + RIM, :] = rim.astype(jnp.bfloat16)
                    base += RIM


def turned(cycles):
    half = math.pi * (cycles - jnp.floor(cycles + 0.5))
    square = half * half
    sine, cosine = jnp.zeros_like(half), jnp.zeros_like(half)
    for order in range(13, 0, -2):
        sine = sine * square + (-1) ** (order // 2) / math.factorial(order)
        cosine = cosine * square + (-1) ** (order // 2) / math.factorial(order - 1)
    sine = sine * half
    return 1.0 - 2.0 * sine * sine, 2.0 * sine * cosine


def axes_kernel(groups, members, piece, sample_count, cosines, sines, center_dirs):
    wide_at = lax.axis_index("wide")
    group_at, member_at = wide_at // members, wide_at % members
    rows = 4 * piece // LANES
    half_rows = sample_count // LANES // lax.axis_size("narrow")
    row = lax.broadcasted_iota(jnp.int32, (rows, LANES), 0)
    lane = lax.broadcasted_iota(jnp.int32, (rows, LANES), 1)
    cos_azimuth, sin_azimuth = turned((((row * LANES + lane) & 255).astype(jnp.float32) + 0.5) / 256.0)
    for step in range(groups):
        at = group_after(group_at, step, groups) * members + member_at
        first_row = lax.axis_index("narrow") * half_rows + at * rows
        ring = ((first_row + row) * LANES + lane) >> 8
        dir_z, sin_polar = turned((ring.astype(jnp.float32) + 0.5) / (2 * (sample_count // 256)))
        for axis, direction in enumerate((sin_polar * cos_azimuth, sin_polar * sin_azimuth, dir_z)):
            cosines[step, axis], sines[step, axis] = turned(2.0 * direction)
            if step == 0:
                center_dirs[axis] = direction


def prep_kernel(
    groups, members, boxes, piece, parent_of, octant_of, center, starts, axis_cos, axis_sin, center_dirs,
    cosines, sines, center_cos, center_sin, excess, held, sems,
):
    wide_at = lax.axis_index("wide")
    group_at, member_at = wide_at // members, wide_at % members
    rows = 4 * piece // LANES
    half_rows = starts.shape[0] // lax.axis_size("narrow")
    row = lax.broadcasted_iota(jnp.int32, (rows, LANES), 0)
    lane = lax.broadcasted_iota(jnp.int32, (rows, LANES), 1)
    first_rows = [
        pl.multiple_of(
            lax.axis_index("narrow") * half_rows + (group_after(group_at, step, groups) * members + member_at) * rows, 8
        )
        for step in range(groups)
    ]
    copies = [
        pltpu.make_async_copy(starts.at[pl.ds(first_rows[step], rows)], held.at[step], sems.at[step]) for step in range(groups)
    ]
    for copy in copies:
        copy.start()
    scale = 1.0 / math.sqrt(center.shape[0])
    for step in range(groups):
        parent = parent_of[group_before(group_at, step, groups) * members * boxes]
        turns = sum(center[parent, axis] * center_dirs[axis] for axis in range(3))
        turn_cos, turn_sin = turned(turns)
        center_cos[step] = turn_cos * scale
        center_sin[step] = turn_sin * scale
    for step in range(groups):
        (cos_x, cos_y, cos_z), (sin_x, sin_y, sin_z) = ([table[step, axis] for axis in range(3)] for table in (axis_cos, axis_sin))
        both_cos, both_sin, sin_cos, cos_sin = cos_x * cos_y, sin_x * sin_y, sin_x * cos_y, cos_x * sin_y
        for swap in range(members):
            for box in range(boxes):
                slot = (group_at * members + (member_at ^ swap)) * boxes + box
                octant = octant_of[slot]
                live = jnp.where(parent_of[slot] >= 0, 1.0, 0.0)
                sign_x = ((octant & 1) * 2 - 1).astype(jnp.float32)
                sign_y = (((octant >> 1) & 1) * 2 - 1).astype(jnp.float32)
                sign_z = ((octant >> 2) * 2 - 1).astype(jnp.float32)
                real = both_cos - (sign_x * sign_y) * both_sin
                imag = sign_x * sin_cos + sign_y * cos_sin
                turn_cos, turn_sin = live * cos_z, (live * sign_z) * sin_z
                cosines[step, swap * boxes + box] = real * turn_cos - imag * turn_sin
                sines[step, swap * boxes + box] = real * turn_sin + imag * turn_cos
    for step in range(groups):
        copies[step].wait()
        child = ((first_rows[step] + row) * LANES + lane) >> 2
        excess[step] = (child - 2 - held[step]).astype(jnp.float32)


def columns_of(windows):
    return [2 * window + half for window in windows for half in range(2)]


def combine_kernel(jobs, members, boxes, sources, tiles, count, *refs):
    data = refs[:count]
    cosines, sines, excess, band_zero, band_one = refs[count : count + 5]
    *outs, spread, total = refs[count + 5 :]
    for (step, *job), out in zip(jobs, outs):
        combine(
            step, *job, members, boxes, sources, tiles, data, cosines.at[step], sines.at[step], excess.at[step],
            band_zero, band_one, out, spread, total,
        )


def combine(
    step, windows, places, rims, members, boxes, sources, tiles, data, cosines, sines, excess, band_zero, band_one, out, spread, total
):
    rows = boxes * 2 * sources
    block = data[0].shape[3]
    wide_at = lax.axis_index("wide")
    last = lax.axis_size("wide") - 1
    groups = lax.axis_size("wide") // members
    at = group_after(wide_at // members, step, groups) * members + wide_at % members
    first = at * (tiles * LANES)

    def local(ref, lane):
        return ref[:, :, :, pl.ds(pl.multiple_of(lane, LANES), LANES)].reshape(rows, LANES)

    def tile(index):
        if index < 0 or index >= tiles:
            return rim_tile
        found = [local(data[member], first + index * LANES) for member in range(2)]
        for which, base in places:
            ref = data[which]
            if len(ref.shape) == 4:
                found.append(ref[:, :, :, index * LANES : (index + 1) * LANES].reshape(rows, LANES))
            else:
                found.append(ref[base + index * rows : base + (index + 1) * rows, :])
        return jnp.concatenate(found, axis=0)

    if rims is not None:
        slot, lane = rim_masks()
        from_other = slot >= 2 * HALO
        side = jnp.where(from_other, slot - 2 * HALO, slot)
        outer = ((side < HALO) & (at == 0)) | ((side >= HALO) & (at == last))
        keep = (outer == from_other) & (slot < 4 * HALO)
        place = as_mask(
            ((side < HALO) & (lane == LANES - HALO + side)) | ((side >= HALO) & (side < 2 * HALO) & (lane == side - HALO))
        )
        found = []
        for inner, (other, other_row) in rims:
            outside = data[other][other_row : other_row + RIM, :].astype(jnp.float32)
            if inner is None:
                inside = jnp.zeros((RIM, LANES), jnp.float32)
            else:
                inside = data[inner[0]][inner[1] : inner[1] + RIM, :].astype(jnp.float32)
            found.append(jnp.where(keep, jnp.where(from_other, outside, inside), 0.0).astype(jnp.bfloat16))
        rim = jnp.concatenate(found, axis=1)
        rim_tile = lax.dot_general(rim, place, (((0,), (0,)), ((), ())), preferred_element_type=jnp.float32)
        lane = lax.broadcasted_iota(jnp.int32, (rows, LANES), 1)
        from_before = (lane >= LANES - HALO) & (at != 0)
        from_after = (lane < HALO) & (at != last)
        near = []
        for member in range(2):
            before = local(data[member], jnp.maximum(first - LANES, 0)).astype(jnp.float32)
            after = local(data[member], jnp.minimum(first + tiles * LANES, block - LANES)).astype(jnp.float32)
            near.append(jnp.where(from_before, before, jnp.where(from_after, after, 0.0)))
        near = jnp.concatenate(near, axis=0)
        rim_tile = jnp.concatenate([rim_tile[: 2 * rows] + near, rim_tile[2 * rows :]], axis=0).astype(jnp.bfloat16)

    def window_of(window):
        cut = 32 if window % 2 else 96
        left, right = tile((window - 1 + window % 2) // 2), tile((window + 1) // 2)
        cells = jnp.concatenate([left[:, cut:], right[:, :cut]], axis=1)
        return jnp.concatenate([cells, cells], axis=1)

    columns = columns_of(windows)
    width = len(columns)
    whole = width == 4 * tiles

    def spread_window(turn):
        bands = []
        for half, column in enumerate(columns[2 * turn : 2 * turn + 2]):
            which = jnp.broadcast_to(excess[column : column + 1, :], (16, LANES)).astype(jnp.bfloat16)
            which = jnp.concatenate([which] * (band_zero.shape[0] // 16), axis=0)
            lanes = slice(half * LANES, (half + 1) * LANES)
            bands.append(band_zero[:, lanes] * (1 - which) + band_one[:, lanes] * which)
        spread[turn % 2] = jnp.dot(
            window_of(windows[turn]), jnp.concatenate(bands, axis=1), preferred_element_type=jnp.float32
        )

    def sum_window(turn):
        for half, column in enumerate(columns[2 * turn : 2 * turn + 2]):
            lanes = slice(half * LANES, (half + 1) * LANES)
            real_sum = jnp.zeros((sources, LANES), jnp.float32)
            imag_sum = jnp.zeros((sources, LANES), jnp.float32)
            for child in range(members * boxes):
                start = child * 2 * sources
                real = spread[turn % 2, start : start + sources, lanes].astype(jnp.bfloat16).astype(jnp.float32)
                imag = spread[turn % 2, start + sources : start + 2 * sources, lanes]
                imag = imag.astype(jnp.bfloat16).astype(jnp.float32)
                cosine = cosines[child, column : column + 1, :]
                sine = sines[child, column : column + 1, :]
                real_sum = real_sum + (cosine * real - sine * imag)
                imag_sum = imag_sum + (sine * real + cosine * imag)
            if whole:
                total[pl.ds(column, sources, stride=width), :] = real_sum
                total[pl.ds(sources * width + column, sources, stride=width), :] = imag_sum
            else:
                at_row = (2 * turn + half) * 2 * sources
                out[at_row : at_row + sources, :] = real_sum.astype(out.dtype)
                out[at_row + sources : at_row + 2 * sources, :] = imag_sum.astype(out.dtype)

    for turn in range(len(windows) + 1):
        if turn < len(windows):
            spread_window(turn)
        if turn:
            sum_window(turn - 1)
    if whole:
        out[...] = total[...].astype(out.dtype)


def place_columns(arrived, columns, sources, rows, cosines, sines, pattern, far):
    for index, column in enumerate(columns):
        real, imag = (
            arrived[pl.ds((2 * index + half) * sources, sources), :].astype(jnp.float32) for half in range(2)
        )
        at = pl.ds(column, sources, stride=rows)
        pattern[0, at, :] = real
        pattern[1, at, :] = imag
        cosine, sine = cosines[column : column + 1, :], sines[column : column + 1, :]
        far[0, at, :] += cosine * real - sine * imag
        far[1, at, :] += sine * real + cosine * imag


def finish_ahead_kernel(steps, early_step, columns, members, boxes, sources, rows, parent_of, *refs):
    whole, (early, center_cos, center_sin, parent_out, far_out, early_out) = refs[: len(steps)], refs[len(steps) :]
    groups = lax.axis_size("wide") // members
    group_at = lax.axis_index("wide") // members
    names = [parent_of[group_before(group_at, step, groups) * members * boxes] for step in steps]
    for source in range(sources):
        at = pl.ds(source * rows, rows)
        far_real = far_imag = 0.0
        for index, step in enumerate(steps):
            real, imag = (
                whole[index][pl.ds((half * sources + source) * rows, rows), :].astype(jnp.float32) for half in range(2)
            )
            cosine, sine = center_cos[step], center_sin[step]
            parent_out[names[index], 0, at, :] = real
            parent_out[names[index], 1, at, :] = imag
            far_real = far_real + (cosine * real - sine * imag)
            far_imag = far_imag + (sine * real + cosine * imag)
        far_out[0, at, :] = far_real
        far_out[1, at, :] = far_imag
    place_columns(
        early, columns, sources, rows, center_cos.at[early_step], center_sin.at[early_step], early_out, far_out
    )


def join_kernel(steps, early_step, columns, members, boxes, sources, rows, parent_of, *refs):
    whole, refs = refs[: len(steps)], refs[len(steps) :]
    late, early, center_cos, center_sin, far_in, _, parent_out, far_out, names, patterns, name_sem, sems = refs
    name_copy = pltpu.make_async_copy(parent_of, names, name_sem)
    name_copy.start()
    last = len(steps)
    groups = lax.axis_size("wide") // members
    group_at = lax.axis_index("wide") // members
    copies = []

    def send(index, step):
        name = names[group_before(group_at, step, groups) * members * boxes]
        copies.append(pltpu.make_async_copy(patterns.at[index], parent_out.at[name], sems.at[index]))
        copies[-1].start()

    patterns[last] = early[...]
    far_out[...] = far_in[...]
    place_columns(
        late, columns, sources, rows, center_cos.at[early_step], center_sin.at[early_step], patterns.at[last], far_out
    )
    name_copy.wait()
    send(last, early_step)
    for index, step in enumerate(steps):
        cosine, sine = center_cos[step], center_sin[step]
        for source in range(sources):
            at = pl.ds(source * rows, rows)
            real, imag = (
                whole[index][pl.ds((half * sources + source) * rows, rows), :].astype(jnp.float32) for half in range(2)
            )
            patterns[index, 0, at, :] = real
            patterns[index, 1, at, :] = imag
            far_out[0, at, :] += cosine * real - sine * imag
            far_out[1, at, :] += sine * real + cosine * imag
        send(index, step)
    for copy in copies:
        copy.wait()


def finish_kernel(steps, members, boxes, sources, rows, parts, parent_of, *refs):
    whole, refs = refs[: len(steps)], refs[len(steps) :]
    center_cos, center_sin, far_in, _, parent_out, far_out, names, held, far_held, name_sem, sems = refs
    name_copy = pltpu.make_async_copy(parent_of, names, name_sem)
    name_copy.start()
    group_at = lax.axis_index("wide") // members
    copies = []

    def send(source, target):
        copies.append(pltpu.make_async_copy(source, target, sems.at[len(copies)]))
        copies[-1].start()

    last = len(steps)
    name_copy.wait()
    groups = lax.axis_size("wide") // members
    places = [names[group_before(group_at, step, groups) * members * boxes] for step in steps]
    each = sources // parts
    for part in range(parts):
        for source in range(part * each, (part + 1) * each):
            at = pl.ds(source * rows, rows)
            far_real, far_imag = far_in[0, at, :], far_in[1, at, :]
            for index, step in enumerate(steps):
                real, imag = (
                    whole[index][pl.ds((half * sources + source) * rows, rows), :].astype(jnp.float32) for half in range(2)
                )
                cosine, sine = center_cos[step], center_sin[step]
                held[index, 0, at, :] = real
                held[index, 1, at, :] = imag
                far_real = far_real + (cosine * real - sine * imag)
                far_imag = far_imag + (sine * real + cosine * imag)
            far_held[0, at, :] = far_real
            far_held[1, at, :] = far_imag
        at = pl.ds(part * each * rows, each * rows)
        for index in range(last):
            send(held.at[index, :, at], parent_out.at[places[index], :, at])
        send(far_held.at[:, at], far_out.at[:, at])
    for copy in copies:
        copy.wait()


def grouped(child_pattern, child_parent, child_octant, parent_center, stencil_start, members):
    n_wide = lax.axis_size("wide")
    boxes, _, sources, block = child_pattern.shape
    groups = n_wide // members
    piece = block // n_wide
    tiles = piece // LANES
    rows = boxes * 2 * sources
    out_rows = 4 * tiles
    parents = parent_center.shape[0]
    vmem = pl.BlockSpec(memory_space=pltpu.VMEM)
    smem = pl.BlockSpec(memory_space=pltpu.SMEM)
    hbm = pl.BlockSpec(memory_space=pltpu.HBM)
    limit = pltpu.CompilerParams(vmem_limit_bytes=16 * 1024 * 1024)

    def cost(micros):
        return pl.CostEstimate(flops=int(micros * 1e9), bytes_accessed=int(micros * 3.6e6) + 1, transcendentals=0)


    def bf16(*shape):
        return jax.ShapeDtypeStruct(shape, jnp.bfloat16)

    def f32(*shape):
        return jax.ShapeDtypeStruct(shape, jnp.float32)

    def swap_with(array, step):
        return lax.ppermute(array, "wide", [(i, i ^ step) for i in range(n_wide)])

    def move_by(array, step):
        shift = shift_of(step, groups) * members
        return lax.ppermute(array, "wide", [(i, (i + shift) % n_wide) for i in range(n_wide)])

    def tie(*arrays):
        return lax.optimization_barrier(arrays)

    far = members - 2
    wide_at = lax.axis_index("wide")
    heads = []
    for swap in range(2, members):
        first = (wide_at ^ (groups // 2 * members + swap)) * piece
        heads.append(lax.dynamic_slice_in_dim(child_pattern, first, piece, 3))
    near = swap_with(child_pattern, 1)
    heads = [swap_with(head, swap + 2) for swap, head in enumerate(heads)]

    def other_half(array, step):
        pairs = [(i * 2 + n, (i ^ step) * 2 + 1 - n) for i in range(n_wide) for n in range(2)]
        return lax.ppermute(array, ("wide", "narrow"), pairs)

    axes = pl.pallas_call(
        functools.partial(axes_kernel, groups, members, piece, stencil_start.shape[0]),
        out_shape=[f32(groups, 3, out_rows, LANES)] * 2 + [f32(3, out_rows, LANES)],
        out_specs=[vmem] * 3,
        compiler_params=limit,
        cost_estimate=cost(1),
        name="axes",
    )()
    tables = pl.pallas_call(
        functools.partial(prep_kernel, groups, members, boxes, piece),
        out_shape=[
            f32(groups, members * boxes, out_rows, LANES),
            f32(groups, members * boxes, out_rows, LANES),
            f32(parents, out_rows, LANES),
            f32(parents, out_rows, LANES),
            f32(groups, out_rows, LANES),
        ],
        in_specs=[smem, smem, smem, hbm] + [vmem] * 3,
        out_specs=[vmem] * 5,
        scratch_shapes=[pltpu.VMEM((groups, out_rows, LANES), jnp.int32), pltpu.SemaphoreType.DMA((groups,))],
        compiler_params=limit,
            cost_estimate=cost(1),
        name="prep",
    )(child_parent, child_octant, parent_center, stencil_start.reshape(-1, LANES), *axes)
    cosines, sines, center_cos, center_sin, excess = tables
    full = tiles * rows + RIM
    pairs = members // 2 - 1
    *sends, edges = pl.pallas_call(
        functools.partial(rest_pack_kernel, groups, members, piece),
        out_shape=[
            bf16(2 * (full + (RIM if part == 1 else 0)), LANES) for part in range(1, groups) for _ in range(pairs)
        ]
        + [bf16(2 * RIM, LANES)],
        in_specs=[vmem] * 2,
        out_specs=[vmem] * ((groups - 1) * pairs + 1),
        compiler_params=limit,
        cost_estimate=cost(1),
        name="pack",
    )(child_pattern, near)
    common = [other_half(edges, 2 * pair) for pair in range(pairs + 1)]
    bands = stencil_tables(LANES, 2 * LANES)

    top = groups - 1

    def sums_of(jobs, data, dtype, micros):
        shapes = [jax.ShapeDtypeStruct((2 * sources * len(columns_of(job[1])), LANES), dtype) for job in jobs]
        inputs = [*data, cosines, sines, excess, bands[0], bands[1]]
        return pl.pallas_call(
            functools.partial(combine_kernel, jobs, members, boxes, sources, tiles, len(data)),
            out_shape=shapes,
            in_specs=[vmem] * len(inputs),
            out_specs=[vmem] * len(shapes),
            scratch_shapes=[
                pltpu.VMEM((2, members * rows, 2 * LANES), jnp.float32),
                pltpu.VMEM((2 * sources * out_rows, LANES), jnp.float32),
            ],
            compiler_params=limit,
            cost_estimate=cost(micros),
            name="combine",
        )(*inputs)

    inner = list(range(1, 2 * tiles - 1))
    outer = [0, 2 * tiles - 1]
    every = list(range(2 * tiles))
    locals_ = [child_pattern, near]
    first_data = locals_ + heads
    first_places = [(2 + member, 0) for member in range(far)]
    (total,) = sums_of([(top, inner, first_places, None)], first_data, jnp.bfloat16, 5)
    early_sends = sends[pairs : 2 * pairs]
    *early_sends, total = tie(*early_sends, total)
    sends[pairs : 2 * pairs] = early_sends
    done = [move_by(total, top)]
    arrived = {}
    for part in range(1, groups):
        step = top - part
        sent = sends[(part - 1) * pairs : part * pairs]
        if part > 1:
            totals = list(sums_of(jobs, data, jnp.bfloat16, 30 if part == 2 else 2))
            if part < groups - 1:
                tied = tie(*sends[part * pairs : (part + 1) * pairs], *totals)
                sends[part * pairs : (part + 1) * pairs], totals = tied[:pairs], list(tied[pairs:])
            arrived[step + 1] = move_by(totals[0], step + 1)
            if part == 2:
                done.append(move_by(totals[1], top))
        got = [swap_with(array, 2 * pair + 2) for pair, array in enumerate(sent)]
        length = full + (RIM if part == 1 else 0)
        places = [(2 + member // 2, member % 2 * length) for member in range(far)]
        data = locals_ + got + common
        shift = 2 + pairs
        edge_at = [(shift + member // 2, member % 2 * RIM) for member in range(members)]
        rims = [None, None] + [(which, row + tiles * rows) for which, row in places]
        jobs = [(step, every, places, list(zip(rims, edge_at)))]
        if part == 1:
            rims = [None, None] + [(which, row + full) for which, row in places]
            outer_places = [(len(data) + member, 0) for member in range(far)]
            jobs.append((top, outer, outer_places, list(zip(rims, edge_at))))
            data = data + heads
    data[0], done[0] = tie(data[0], done[0])
    (arrived[0],) = sums_of(jobs, data, jnp.float32, 0)
    done = [(top, columns_of(inner), done[0]), (top, columns_of(outer), done[1])]
    held = arrived
    whole = f32(2, sources * out_rows, LANES)
    (_, early_columns, early_array), (_, late_columns, late_array) = done
    ahead = [0]
    parent_pattern, far_field, early_pattern = pl.pallas_call(
        functools.partial(finish_ahead_kernel, ahead, top, early_columns, members, boxes, sources, out_rows),
        out_shape=[f32(parents, *whole.shape), whole, whole],
        in_specs=[smem] + [vmem] * (len(ahead) + 3),
        out_specs=[vmem] * 3,
        compiler_params=limit,
        cost_estimate=cost(0),
        name="finish_ahead",
    )(child_parent, *[held[step] for step in ahead], early_array, center_cos, center_sin)
    between = list(range(2, top))
    parent_pattern, far_field = pl.pallas_call(
        functools.partial(join_kernel, between, top, late_columns, members, boxes, sources, out_rows),
        out_shape=[f32(parents, *whole.shape), whole],
        in_specs=[hbm] + [vmem] * (len(between) + 5) + [hbm],
        out_specs=[hbm, vmem],
        input_output_aliases={len(between) + 6: 0},
        scratch_shapes=[
            pltpu.SMEM(child_parent.shape, jnp.int32),
            pltpu.VMEM((len(between) + 1, *whole.shape), jnp.float32),
            pltpu.SemaphoreType.DMA,
            pltpu.SemaphoreType.DMA((len(between) + 1,)),
        ],
        compiler_params=limit,
        cost_estimate=cost(5),
        name="join",
    )(
        child_parent, *[held[step] for step in between], late_array, early_pattern, center_cos, center_sin, far_field,
        parent_pattern,
    )
    steps = [1]
    parts = 2
    parent_pattern, far_field = pl.pallas_call(
        functools.partial(finish_kernel, steps, members, boxes, sources, out_rows, parts),
        out_shape=[f32(parents, *whole.shape), whole],
        in_specs=[hbm] + [vmem] * (len(steps) + 3) + [hbm],
        out_specs=[hbm, hbm],
        input_output_aliases={len(steps) + 4: 0},
        scratch_shapes=[
            pltpu.SMEM(child_parent.shape, jnp.int32),
            pltpu.VMEM((len(steps), *whole.shape), jnp.float32),
            pltpu.VMEM(whole.shape, jnp.float32),
            pltpu.SemaphoreType.DMA,
            pltpu.SemaphoreType.DMA((parts * (len(steps) + 1),)),
        ],
        compiler_params=limit,
        cost_estimate=cost(30),
        name="finish_last",
    )(child_parent, *[held[step] for step in steps], center_cos, center_sin, far_field, parent_pattern)
    return (
        parent_pattern.reshape(parents, 2, sources, 1, 4 * piece),
        far_field.reshape(2, sources, 1, 4 * piece),
    )


def power_of_two(number):
    return number > 0 and number & (number - 1) == 0


def per_device(child_pattern, child_parent, child_octant, parent_center, stencil_start):
    n_wide, n_narrow = lax.axis_size("wide"), lax.axis_size("narrow")
    boxes, _, sources, block = child_pattern.shape
    parents = parent_center.shape[0]
    run = child_parent.shape[0] // parents
    if run % boxes == 0 and block % n_wide == 0:
        members = run // boxes
        fits = (
            n_narrow == 2
            and n_wide == members * parents
            and power_of_two(members)
            and power_of_two(parents)
            and members >= 4
            and parents >= 4
            and block // n_wide % LANES == 0
            and block // n_wide // LANES >= 3
            and boxes * 2 * sources == LANES
            and sources % 16 == 0
            and stencil_start.shape[0] == 4 * block * n_narrow
        )
        if fits:
            return grouped(child_pattern, child_parent, child_octant, parent_center, stencil_start, members)
    return exchanged(child_pattern, child_parent, child_octant, parent_center, stencil_start)


def solution(mesh):
    in_specs = (P("wide", None, None, "narrow"), P(), P(), P(), P())
    out_specs = (P(None, None, None, "narrow", "wide"), P(None, None, "narrow", "wide"))
    return jax.shard_map(
        per_device, mesh=mesh, in_specs=in_specs, out_specs=out_specs, check_vma=False
    )
```
